32 devices in a mesh: dp: 4 (over y, core), fsdp: 8 (over z, x).
Axes of the slice: x: 2, y: 2, z: 4, core: 2. Of those that a mesh axis runs over, the one named last changes fastest.
Arguments:
- tokens: bfloat16 [2, 8, 512, 1024], P(None, 'fsdp', 'dp'), may hold values from -6 to 6
- cotangent: bfloat16 [2, 8, 512, 1024], P(None, 'fsdp', 'dp'), may hold values from -6 to 6
- in_weight: float32 [1024, 4096], P(('dp', 'fsdp')), may hold values from -0.1875 to 0.1875
- out_weight: float32 [2048, 1024], P(('dp', 'fsdp')), may hold values from -0.25 to 0.25
- xproj_weight: float32 [2048, 96], P(('dp', 'fsdp')), may hold values from -0.125 to 0.125
- dtproj_weight: float32 [64, 2048], P(None, ('dp', 'fsdp')), may hold values from -3 to 3
- chan_params: float32 [7, 2048], P(None, ('dp', 'fsdp')), may hold values from -7.5 to 2
- a_log: float32 [16, 2048], P(None, ('dp', 'fsdp')), may hold values from -4.5 to 1
- norm_gain: float32 [1024], P(('dp', 'fsdp')), may hold values from 0.5 to 1.5
- in_moments: float32 [2, 1024, 4096], P(None, ('dp', 'fsdp')), as said below
- out_moments: float32 [2, 2048, 1024], P(None, ('dp', 'fsdp')), as said below
- xproj_moments: float32 [2, 2048, 96], P(None, ('dp', 'fsdp')), as said below
- dtproj_moments: float32 [2, 64, 2048], P(None, None, ('dp', 'fsdp')), as said below
- chan_moments: float32 [2, 7, 2048], P(None, None, ('dp', 'fsdp')), as said below
- alog_moments: float32 [2, 16, 2048], P(None, None, ('dp', 'fsdp')), as said below
- gain_moments: float32 [2, 1024], P(None, ('dp', 'fsdp')), as said below
Outputs:
- block_output: bfloat16 [2, 8, 512, 1024], P(None, 'fsdp', 'dp')
- input_grad: float32 [2, 8, 512, 1024], P(None, 'fsdp', 'dp')
- grad_norm: float32 [], replicated
- next_in_moments: float32 [2, 1024, 4096], P(None, ('dp', 'fsdp'))
- next_in_weight: float32 [1024, 4096], P(('dp', 'fsdp'))
- next_out_moments: float32 [2, 2048, 1024], P(None, ('dp', 'fsdp'))
- next_out_weight: float32 [2048, 1024], P(('dp', 'fsdp'))
- next_xproj_moments: float32 [2, 2048, 96], P(None, ('dp', 'fsdp'))
- next_xproj_weight: float32 [2048, 96], P(('dp', 'fsdp'))
- next_dtproj_moments: float32 [2, 64, 2048], P(None, None, ('dp', 'fsdp'))
- next_dtproj_weight: float32 [64, 2048], P(None, ('dp', 'fsdp'))
- next_chan_moments: float32 [2, 7, 2048], P(None, None, ('dp', 'fsdp'))
- next_chan_params: float32 [7, 2048], P(None, ('dp', 'fsdp'))
- next_alog_moments: float32 [2, 16, 2048], P(None, None, ('dp', 'fsdp'))
- next_a_log: float32 [16, 2048], P(None, ('dp', 'fsdp'))
- next_gain_moments: float32 [2, 1024], P(None, ('dp', 'fsdp'))
- next_norm_gain: float32 [1024], P(('dp', 'fsdp'))
The draws below stay inside these ranges and needn't reach their ends.
Inputs may be any that keep to these rules, and one draw needn't show every extreme that they name: `in_moments`: the roots of the second moments are positive. `out_moments`: the roots of the second moments are positive. `xproj_moments`: the roots of the second moments are positive. `dtproj_moments`: the roots of the second moments are positive. `chan_moments`: the roots of the second moments are positive. `alog_moments`: the roots of the second moments are positive. `gain_moments`: the roots of the second moments are positive.
All inputs are finite; a program needn't handle non-finite values.
Results may differ from the reference program's by a relative error of at most 0.009.
The reference program's roundings to bfloat16 on the way count: a program that leaves them out, or rounds other values in their place, can miss the bound.
Values may be sent and summed in bfloat16 or wider, within the bound.
No kernel may reach another device: no remote copies, remote signals or barrier semaphores. Data moves between devices by JAX's collectives and lax.ppermute only.
A program may use at most 192 MiB of HBM per device.

```python
import math
import jax
import jax.numpy as jnp
from jax import lax

D = 1024
E = 2048
N = 16
R = 64
KW = 4
Q = 32
MB = 2
STEP = 7
L = 512
SEQS = 8
PARAMS = 6667264


def draw_chan_params(key, part):
    key_taps, key_bias, key_step, key_skip = jax.random.split(key, 4)
    taps = 0.5 * jnp.clip(jax.random.normal(key_taps, (KW, E), jnp.float32), -4.0, 4.0)
    step_bias = jax.random.uniform(key_step, (1, E), jnp.float32, -6.5, -3.0)
    conv_bias = 0.3 * jnp.clip(jax.random.normal(key_bias, (1, E), jnp.float32), -4.0, 4.0)
    skip_gain = jax.random.uniform(key_skip, (1, E), jnp.float32, 0.5, 1.5)
    return jnp.concatenate([taps, conv_bias, step_bias, skip_gain], axis=0)


def moment_pair(key, shape_of, multiple):
    grad_scale = multiple * PARAMS ** (-0.5)
    key_first, key_second = jax.random.split(jax.random.fold_in(key, 11))
    first_moment = grad_scale / 9.0 * jnp.clip(jax.random.normal(key_first, shape_of, jnp.float32), -4.0, 4.0)
    spread = jnp.exp(jax.random.uniform(key_second, shape_of, jnp.float32, 0.0, math.log(4.0)))
    root_moment = grad_scale * jnp.sqrt(0.05 / 0.95 * spread)
    return jnp.stack([first_moment, root_moment])


def draw_in_moments(key, part):
    return moment_pair(key, (D, 2 * E), 0.5)


def draw_out_moments(key, part):
    return moment_pair(key, (E, D), 0.5)


def draw_xproj_moments(key, part):
    return moment_pair(key, (E, R + 2 * N), 3.0)


def draw_dtproj_moments(key, part):
    return moment_pair(key, (R, E), 1.0)


def draw_chan_moments(key, part):
    return moment_pair(key, (KW + 3, E), 3.0)


def draw_alog_moments(key, part):
    return moment_pair(key, (N, E), 2.0)


def draw_gain_moments(key, part):
    return moment_pair(key, (D,), 2.0)


def levels(stream_key, extent, cuts, least, largest):
    gain = 1.0
    for dim, shards_of in cuts:
        steps = jax.random.uniform(jax.random.fold_in(jax.random.fold_in(stream_key, 6), dim), (shards_of,), jnp.float32, least / len(cuts), largest / len(cuts))
        gain = gain * jnp.repeat(jnp.exp(steps), extent[dim] // shards_of).reshape((-1,) + (1,) * (len(extent) - 1 - dim))
    return gain


def scatter_about(rng, shape, deviation, bound, cuts=(), dtype=jnp.bfloat16):
    drawn = deviation * jax.random.normal(rng, shape, jnp.float32)
    if cuts:
        drawn = drawn * levels(rng, shape, cuts, -0.22, 0.18)
    return jnp.clip(drawn, -bound, bound).astype(dtype)


def setup_inputs(seed: int = 0) -> dict:
    seeds = jax.random.split(jax.random.key(seed), 17)
    return {
        "tokens": scatter_about(seeds[0], (MB, SEQS, L, D), 1.0, 6.0, ((1, 8), (2, 4))),
        "cotangent": scatter_about(seeds[1], (MB, SEQS, L, D), 1.0, 6.0, ((1, 8), (2, 4))),
        "in_weight": scatter_about(seeds[2], (D, 2 * E), D ** -0.5, 0.1875, ((0, 32),), jnp.float32),
        "out_weight": scatter_about(seeds[3], (E, D), (E // 4) ** -0.5, 0.25, ((0, 32),), jnp.float32),
        "xproj_weight": scatter_about(seeds[4], (E, R + 2 * N), E ** -0.5, 0.125, ((0, 32),), jnp.float32),
        "dtproj_weight": scatter_about(seeds[5], (R, E), (R // 16) ** -0.5, 3.0, ((1, 32),), jnp.float32),
        "chan_params": draw_chan_params(jax.random.fold_in(seeds[16], 71), 0),
        "a_log": jnp.clip(-4.5 + 5.5 * jax.random.uniform(seeds[7], (N, E), jnp.float32) ** levels(seeds[7], (N, E), ((1, 32),), -0.2, 0.2), -4.5, 1.0),
        "norm_gain": jnp.clip(1.0 + 0.1 * jax.random.normal(seeds[8], (D,), jnp.float32), 0.5, 1.5),
        "in_moments": draw_in_moments(jax.random.fold_in(seeds[16], 71), 0),
        "out_moments": draw_out_moments(jax.random.fold_in(seeds[16], 71), 0),
        "xproj_moments": draw_xproj_moments(jax.random.fold_in(seeds[16], 71), 0),
        "dtproj_moments": draw_dtproj_moments(jax.random.fold_in(seeds[16], 71), 0),
        "chan_moments": draw_chan_moments(jax.random.fold_in(seeds[16], 71), 0),
        "alog_moments": draw_alog_moments(jax.random.fold_in(seeds[16], 71), 0),
        "gain_moments": draw_gain_moments(jax.random.fold_in(seeds[16], 71), 0),
    }


@jax.custom_vjp
def low(v):
    return lax.optimization_barrier(v.astype(jnp.bfloat16)).astype(jnp.float32)

@jax.custom_vjp
def low_back(v):
    return v

def low_keep(v):
    return (low(v), None)

def low_pass(kept, grad):
    return (grad,)

def back_keep(v):
    return (v, None)

def back_low(kept, grad):
    return (low(grad),)
low.defvjp(low_keep, low_pass)
low_back.defvjp(back_keep, back_low)
clip_limit = 1.0
learn_rates = (0.03, 0.03, 0.03, 0.15, 0.3, 1.0, 0.3)

def matmul(left, right):
    return jnp.dot(left, right, precision=lax.Precision.HIGHEST, preferred_element_type=jnp.float32)

def block_scan(state_now, pieces, a_matrix):

    def advance(carried, row_data):
        step_row, act_row, drive_row, read_row = row_data
        carried = jnp.exp(step_row[None, :] * a_matrix) * carried + drive_row[:, None] * (step_row * act_row)[None, :]
        return (carried, lax.optimization_barrier(jnp.sum(read_row[:, None] * carried, axis=0)))
    return lax.scan(advance, state_now, pieces)

def selective_scan(step_sizes, act_in, drive_in, read_in, a_matrix):
    length = step_sizes.shape[0]
    block_count = length // Q
    pieces = (step_sizes.reshape(block_count, Q, E), act_in.reshape(block_count, Q, E), drive_in.reshape(block_count, Q, N), read_in.reshape(block_count, Q, N))
    stepper = jax.checkpoint(lambda state_now, stretch_data: block_scan(state_now, stretch_data, a_matrix))
    _, outputs = lax.scan(stepper, jnp.zeros((N, E), jnp.float32), pieces)
    return outputs.reshape(length, E)

def block_forward(params, inputs):
    weight_in, weight_out, weight_x, weight_dt, chan_rows, alog_low, gain_low = [low(item) for item in params]
    length = inputs.shape[0]
    inv_rms = lax.rsqrt(lax.optimization_barrier(jnp.mean(inputs * inputs, axis=-1, keepdims=True)) + 1e-05)
    normed = low(inputs * inv_rms * gain_low)
    projected = low_back(low(matmul(normed, weight_in)))
    conv_input = projected[:, :E]
    gate_part = projected[:, E:]
    padded = jnp.concatenate([jnp.zeros((KW - 1, E), jnp.float32), conv_input], axis=0)
    conv_pre = chan_rows[KW] + jnp.zeros((length, E), jnp.float32)
    for offset in range(KW):
        conv_pre = conv_pre + chan_rows[offset] * padded[offset:offset + length]
    act_low = low(jax.nn.silu(conv_pre))
    xproj_out = low_back(low(matmul(act_low, weight_x)))
    rank_part = xproj_out[:, :R]
    drive_part = xproj_out[:, R:R + N]
    read_part = xproj_out[:, R + N:]
    step_pre = low_back(matmul(rank_part, weight_dt) + chan_rows[KW + 1])
    step_sizes = jax.nn.softplus(step_pre)
    a_matrix = -jnp.exp(alog_low)
    scan_out = selective_scan(step_sizes, act_low, drive_part, read_part, a_matrix)
    gate_in = scan_out + chan_rows[KW + 2] * act_low
    gated_low = low(gate_in * jax.nn.silu(gate_part))
    return inputs + matmul(gated_low, weight_out)

def adam_update(weight, moments, gradient, learn_rate):
    first_moment = 0.9 * moments[0] + 0.1 * gradient
    root_moment = jnp.sqrt(0.95 * moments[1] * moments[1] + 0.05 * gradient * gradient)
    update = first_moment / (1.0 - 0.9 ** STEP) / (root_moment / jnp.sqrt(1.0 - 0.95 ** STEP) + 1e-08)
    return (jnp.stack([first_moment, root_moment]), weight - learn_rate * (update + 0.01 * weight))

def reference(tokens, cotangent, in_weight, out_weight, xproj_weight, dtproj_weight, chan_params, a_log, norm_gain, in_moments, out_moments, xproj_moments, dtproj_moments, chan_moments, alog_moments, gain_moments):
    params = tuple((item.astype(jnp.float32) for item in (in_weight, out_weight, xproj_weight, dtproj_weight, chan_params, a_log, norm_gain)))
    flat_in = tokens.reshape(MB * SEQS, L, D)
    flat_cot = cotangent.reshape(MB * SEQS, L, D)
    zero_grads = tuple((jnp.zeros_like(item) for item in params))

    def one_sequence(totals, pieces):
        seq_in, seq_cot = pieces
        result, pullback = jax.vjp(block_forward, params, seq_in.astype(jnp.float32))
        grads_params, grad_input = pullback(seq_cot.astype(jnp.float32))
        totals = tuple((left + right for left, right in zip(totals, grads_params)))
        return (totals, (result.astype(jnp.bfloat16), grad_input))
    totals, (results, in_grads) = lax.scan(one_sequence, zero_grads, (flat_in, flat_cot))
    squares = jnp.zeros((), jnp.float32)
    for gradient in totals:
        squares = squares + jnp.sum(gradient * gradient)
    grad_norm = jnp.sqrt(squares)
    factor = jnp.minimum(1.0, clip_limit / (grad_norm + 1e-06))
    moment_list = (in_moments, out_moments, xproj_moments, dtproj_moments, chan_moments, alog_moments, gain_moments)
    updated = [adam_update(params[place], moment_list[place].astype(jnp.float32), totals[place] * factor, learn_rates[place]) for place in range(7)]
    return (results.reshape(MB, SEQS, L, D), in_grads.reshape(MB, SEQS, L, D), grad_norm, updated[0][0], updated[0][1], updated[1][0], updated[1][1], updated[2][0], updated[2][1], updated[3][0], updated[3][1], updated[4][0], updated[4][1], updated[5][0], updated[5][1], updated[6][0], updated[6][1])
```

```python
import functools

import jax
import jax.numpy as jnp
from jax import lax
from jax.experimental import pallas as pl
from jax.experimental.pallas import tpu as pltpu
from jax.sharding import PartitionSpec as P

N = 16
R = 64
KW = 4
STEP = 7
ROWS = 128
T = 16

bf16 = jnp.bfloat16
f32 = jnp.float32
LOG2E = 1.4426950408889634
clip_limit = 1.0
learn_rates = (0.03, 0.03, 0.03, 0.15, 0.3, 1.0, 0.3)


def swap(x, axis, mask):
    peers = lax.axis_size(axis)
    return lax.ppermute(x, axis, [(i, i ^ mask) for i in range(peers)])


def bit_of(axis, mask):
    return (lax.axis_index(axis) & mask) != 0


def join(low_first, mine, other):
    return jnp.where(low_first, jnp.stack([mine, other]), jnp.stack([other, mine]))


def masks(axis):
    peers = lax.axis_size(axis)
    return [1 << k for k in range(peers.bit_length() - 1)]


def gather_by(x, axis, order):
    out = x[None]
    done = []
    for mask in order:
        other = swap(out, axis, mask)
        out = join(~bit_of(axis, mask), out, other)
        out = out.reshape((-1,) + x.shape)
        done.append(mask)
    sizes = (2,) * len(done)
    out = out.reshape(sizes + x.shape)
    slow_first = sorted(range(len(done)), key=lambda k: -done[k])
    perm = [len(done) - 1 - k for k in slow_first]
    out = out.transpose(perm + list(range(len(done), out.ndim)))
    return out.reshape((-1,) + x.shape)


def gather_dp(x):
    return gather_by(x, "dp", masks("dp")[::-1])


def gather_fsdp(x):
    return gather_by(x, "fsdp", masks("fsdp")[::-1])


def reduce_dp(x):
    for mask in masks("dp"):
        peers = x.shape[0]
        split = x.reshape((peers // 2, 2) + x.shape[1:])
        high = bit_of("dp", mask)
        mine = jnp.where(high, split[:, 1], split[:, 0])
        other = jnp.where(high, split[:, 0], split[:, 1])
        x = mine + swap(other.astype(bf16), "dp", mask).astype(f32)
    return x[0]


def sum_dp(x):
    high = bit_of("dp", 1)
    split = x.reshape((2, x.shape[0] // 2) + x.shape[1:])
    mine = jnp.where(high, split[1], split[0])
    other = jnp.where(high, split[0], split[1])
    mine = mine + swap(other, "dp", 1)
    for mask in masks("dp")[1:]:
        mine = mine + swap(mine, "dp", mask)
    mine = mine.astype(bf16)
    return join(~high, mine, swap(mine, "dp", 1)).reshape(x.shape)


def sum_all(x):
    for axis in ("dp", "fsdp"):
        for mask in masks(axis):
            x = x + swap(x, axis, mask)
    return x


def row_mask():
    rows = lax.broadcasted_iota(jnp.int32, (T, T * N), 0)
    cols = lax.broadcasted_iota(jnp.int32, (T, T * N), 1)
    return (cols // N == rows).astype(f32)


def spread(block):
    rows = lax.broadcasted_iota(jnp.int32, (N, T * N), 0)
    cols = lax.broadcasted_iota(jnp.int32, (N, T * N), 1)
    tile = (cols % N == rows).astype(f32)
    tiled = jnp.dot(block.astype(bf16), tile.astype(bf16), preferred_element_type=f32)
    return (tiled * row_mask()).astype(bf16)


def softplus(v):
    return jnp.maximum(v, 0.0) + jnp.log1p(jnp.exp(-jnp.abs(v)))


def forward_kernel(
    xt_ref, act_ref, dtw_ref, bias_ref, a_ref, scan_ref, h_ref, dt_ref, sp_ref, state, push
):
    width = act_ref.shape[-1]

    @pl.when(pl.program_id(1) == 0)
    def _():
        state[...] = jnp.zeros_like(state)

    columns = xt_ref[...].astype(f32)
    rows_in = columns.T
    rank = rows_in[:, :R].astype(bf16)
    pre = (
        lax.dot_general(rank, dtw_ref[...], (((1,), (1,)), ((), ())), preferred_element_type=f32)
        + bias_ref[...]
    )
    sp_ref[0] = pre
    steps = softplus(pre)
    dt_ref[0] = steps
    push[...] = steps * act_ref[0].astype(f32)
    scaled = a_ref[...] * LOG2E
    drive = columns[R : R + N]
    h = state[...]
    for k in range(ROWS // T):
        read = spread(rows_in[k * T : (k + 1) * T, R + N :])
        for j in range(T):
            t = k * T + j
            decay = jnp.exp2(dt_ref[0, t : t + 1, :] * scaled)
            h = decay * h + drive[:, t : t + 1] * push[t : t + 1, :]
            h_ref[0, t * N : (t + 1) * N, :] = h.astype(bf16)
        scan_ref[0, k * T : (k + 1) * T, :] = jnp.dot(
            read, h_ref[0, k * T * N : (k + 1) * T * N, :], preferred_element_type=f32
        )
    state[...] = h


def scan_forward(xt, act, dtw, bias, a_matrix):
    seqs, length, width = act.shape
    blocks = length // ROWS
    return pl.pallas_call(
        forward_kernel,
        grid=(seqs, blocks),
        in_specs=[
            pl.BlockSpec((R + 2 * N, ROWS), lambda s, b: (0, s * blocks + b)),
            pl.BlockSpec((1, ROWS, width), lambda s, b: (s, b, 0)),
            pl.BlockSpec((width, R), lambda s, b: (0, 0)),
            pl.BlockSpec((1, width), lambda s, b: (0, 0)),
            pl.BlockSpec((N, width), lambda s, b: (0, 0)),
        ],
        out_specs=[
            pl.BlockSpec((1, ROWS, width), lambda s, b: (s, b, 0)),
            pl.BlockSpec((1, ROWS * N, width), lambda s, b: (s, b, 0)),
            pl.BlockSpec((1, ROWS, width), lambda s, b: (s, b, 0)),
            pl.BlockSpec((1, ROWS, width), lambda s, b: (s, b, 0)),
        ],
        out_shape=[
            jax.ShapeDtypeStruct((seqs, length, width), f32),
            jax.ShapeDtypeStruct((seqs, length * N, width), bf16),
            jax.ShapeDtypeStruct((seqs, length, width), f32),
            jax.ShapeDtypeStruct((seqs, length, width), f32),
        ],
        scratch_shapes=[pltpu.VMEM((N, width), f32), pltpu.VMEM((ROWS, width), f32)],
        compiler_params=pltpu.CompilerParams(vmem_limit_bytes=40 * 1024 * 1024),
        name="scan_forward",
    )(xt, act, dtw, bias, a_matrix)


def backward_kernel(
    xt_ref,
    act_ref,
    dt_ref,
    sp_ref,
    ggi_ref,
    skip_ref,
    a_ref,
    h_ref,
    before_ref,
    gsp_ref,
    gact_ref,
    gdrive_ref,
    gread_ref,
    galog_ref,
    carried,
    total,
    g_buf,
    q_buf,
):
    first = pl.program_id(1) == pl.num_programs(1) - 1

    @pl.when(pl.program_id(1) == 0)
    def _():
        carried[...] = jnp.zeros_like(carried)

    @pl.when((pl.program_id(0) == 0) & (pl.program_id(1) == 0))
    def _():
        total[...] = jnp.zeros_like(total)

    columns = xt_ref[...].astype(f32)
    rows_in = columns.T
    a_now = a_ref[...]
    scaled = a_now * LOG2E
    read = columns[R + N :]
    ones = row_mask().astype(bf16)
    ggi_low = ggi_ref[0].astype(bf16)
    push_low = (dt_ref[0] * act_ref[0].astype(f32)).astype(bf16)
    lanes = lax.broadcasted_iota(jnp.int32, (N, ROWS), 1)
    gdrive = jnp.zeros((N, ROWS), f32)
    gread = jnp.zeros((N, ROWS), f32)
    p = carried[...]
    acc = total[...]
    for k in reversed(range(ROWS // T)):
        drive = spread(rows_in[k * T : (k + 1) * T, R : R + N])
        for j in reversed(range(T)):
            t = k * T + j
            step_row = dt_ref[0, t : t + 1, :]
            g = read[:, t : t + 1] * ggi_ref[0, t : t + 1, :] + p
            p = jnp.exp2(step_row * scaled) * g
            if t > 0:
                h_before = h_ref[0, (t - 1) * N : t * N, :].astype(f32)
            else:
                h_before = jnp.where(first, 0.0, before_ref[0].astype(f32))
            q = p * h_before
            acc = acc + q * step_row
            g_buf[j * N : (j + 1) * N, :] = g.astype(bf16)
            q_buf[j * N : (j + 1) * N, :] = (a_now * q).astype(bf16)
        here = slice(k * T, (k + 1) * T)
        pulled = jnp.dot(drive, g_buf[...], preferred_element_type=f32)
        along = jnp.dot(ones, q_buf[...], preferred_element_type=f32)
        act_now = act_ref[0, here, :].astype(f32)
        grad_steps = along + act_now * pulled
        gsp_ref[0, here, :] = (grad_steps * jax.nn.sigmoid(sp_ref[0, here, :])).astype(bf16)
        gact_ref[0, here, :] = pulled * dt_ref[0, here, :] + skip_ref[...] * ggi_ref[0, here, :]
        both_d = lax.dot_general(
            g_buf[...], push_low, (((1,), (1,)), ((), ())), preferred_element_type=f32
        )
        both_r = lax.dot_general(
            h_ref[0, k * T * N : (k + 1) * T * N, :],
            ggi_low,
            (((1,), (1,)), ((), ())),
            preferred_element_type=f32,
        )
        for j in range(T):
            at = lanes == k * T + j
            gdrive = jnp.where(at, both_d[j * N : (j + 1) * N], gdrive)
            gread = jnp.where(at, both_r[j * N : (j + 1) * N], gread)
    carried[...] = p
    total[...] = acc
    gdrive_ref[...] = gdrive
    gread_ref[...] = gread
    galog_ref[...] = acc * a_now


def scan_backward(xt, act, dt, sp, ggi, skip, a_matrix, states):
    seqs, length, width = act.shape
    blocks = length // ROWS

    def back(s, b):
        return (s, blocks - 1 - b, 0)

    def before(s, b):
        return (s, jnp.maximum((blocks - 1 - b) * ROWS - 1, 0), 0)

    def flat(s, b):
        return (0, s * blocks + blocks - 1 - b)

    return pl.pallas_call(
        backward_kernel,
        grid=(seqs, blocks),
        in_specs=[
            pl.BlockSpec((R + 2 * N, ROWS), flat),
            pl.BlockSpec((1, ROWS, width), back),
            pl.BlockSpec((1, ROWS, width), back),
            pl.BlockSpec((1, ROWS, width), back),
            pl.BlockSpec((1, ROWS, width), back),
            pl.BlockSpec((1, width), lambda s, b: (0, 0)),
            pl.BlockSpec((N, width), lambda s, b: (0, 0)),
            pl.BlockSpec((1, ROWS * N, width), back),
            pl.BlockSpec((1, N, width), before),
        ],
        out_specs=[
            pl.BlockSpec((1, ROWS, width), back),
            pl.BlockSpec((1, ROWS, width), back),
            pl.BlockSpec((N, ROWS), flat),
            pl.BlockSpec((N, ROWS), flat),
            pl.BlockSpec((N, width), lambda s, b: (0, 0)),
        ],
        out_shape=[
            jax.ShapeDtypeStruct((seqs, length, width), bf16),
            jax.ShapeDtypeStruct((seqs, length, width), f32),
            jax.ShapeDtypeStruct((N, seqs * length), f32),
            jax.ShapeDtypeStruct((N, seqs * length), f32),
            jax.ShapeDtypeStruct((N, width), f32),
        ],
        scratch_shapes=[
            pltpu.VMEM((N, width), f32),
            pltpu.VMEM((N, width), f32),
            pltpu.VMEM((T * N, width), bf16),
            pltpu.VMEM((T * N, width), bf16),
        ],
        compiler_params=pltpu.CompilerParams(vmem_limit_bytes=40 * 1024 * 1024),
        name="scan_backward",
    )(xt, act, dt, sp, ggi, skip, a_matrix, states, states)


def silu_slope(values):
    sigmoid = jax.nn.sigmoid(values)
    return sigmoid * (1.0 + values * (1.0 - sigmoid))


def contract(left, right, on_left, on_right):
    return lax.dot_general(
        left, right, (((on_left,), (on_right,)), ((), ())), preferred_element_type=f32
    )


def adam_update(weight, moments, gradient, learn_rate):
    first_moment = 0.9 * moments[0] + 0.1 * gradient
    root_moment = jnp.sqrt(0.95 * moments[1] * moments[1] + 0.05 * gradient * gradient)
    update = first_moment / (1.0 - 0.9**STEP) / (root_moment / jnp.sqrt(1.0 - 0.95**STEP) + 1e-08)
    return (jnp.stack([first_moment, root_moment]), weight - learn_rate * (update + 0.01 * weight))


def later(x, by):
    if by == 0:
        return x
    if by > 0:
        return jnp.pad(x, ((0, 0), (by, 0), (0, 0)))[:, : x.shape[1]]
    return jnp.pad(x, ((0, 0), (0, -by), (0, 0)))[:, -by:]


def shards(
    tokens,
    cotangent,
    in_weight,
    out_weight,
    xproj_weight,
    dtproj_weight,
    chan_params,
    a_log,
    norm_gain,
    in_moments,
    out_moments,
    xproj_moments,
    dtproj_moments,
    chan_moments,
    alog_moments,
    gain_moments,
):
    dps = lax.axis_size("dp")
    fsdps = lax.axis_size("fsdp")
    batches, groups, piece, model = tokens.shape
    seqs = batches * groups
    length = piece * dps
    own_in = in_weight.shape[0]
    own = out_weight.shape[0]
    width = own * fsdps
    rows = seqs * length

    in_low = in_weight.astype(bf16).reshape(own_in, 2, dps, width).transpose(1, 2, 0, 3)
    in_parts = lax.all_to_all(in_low, "dp", 1, 1, tiled=True)
    gain_low = gather_dp(norm_gain.astype(bf16))
    small = jnp.concatenate(
        [
            xproj_weight.astype(bf16),
            dtproj_weight.astype(bf16).T,
            a_log.astype(bf16).T,
            chan_params.astype(bf16).T,
            jnp.zeros((own, 9), bf16),
        ],
        axis=1,
    )
    all_in = gather_fsdp(in_parts)
    all_small = gather_fsdp(small)
    all_gain = gather_fsdp(gain_low)
    out_low = gather_fsdp(out_weight.astype(bf16)).reshape(width, model)
    w_in = all_in.transpose(1, 2, 0, 3, 4).reshape(2, model, width)
    small_low = all_small.reshape(width, -1)
    gain = all_gain.transpose(1, 0, 2).reshape(model).astype(f32)
    w_x = small_low[:, : R + 2 * N]
    w_dt = small_low[:, R + 2 * N : 2 * R + 2 * N]
    rest = small_low[:, 2 * R + 2 * N :].astype(f32).T
    a_matrix = -jnp.exp(rest[:N])
    chan = rest[N : N + KW + 3]

    def whole_rows(x):
        x = gather_dp(x.reshape(seqs, piece, model))
        return x.transpose(1, 0, 2, 3).reshape(rows, model)

    inputs_low = whole_rows(tokens)
    cot_low = whole_rows(cotangent)
    inputs_wide = inputs_low.astype(f32)
    inv_rms = lax.rsqrt(jnp.mean(inputs_wide * inputs_wide, axis=-1, keepdims=True) + 1e-05)
    normed = (inputs_wide * inv_rms * gain).astype(bf16)
    conv_low = contract(normed, w_in[0], 1, 0).astype(bf16)
    gate_part = contract(normed, w_in[1], 1, 0).astype(bf16).astype(f32)
    conv_input = conv_low.reshape(seqs, length, width).astype(f32)
    conv_pre = chan[KW] + jnp.zeros_like(conv_input)
    for offset in range(KW):
        conv_pre = conv_pre + chan[offset] * later(conv_input, KW - 1 - offset)
    act_low = jax.nn.silu(conv_pre).astype(bf16)
    act_rows = act_low.reshape(rows, width)
    xt = sum_dp(contract(w_x, act_rows, 0, 1))
    scan_out, states, dt, step_pre = scan_forward(xt, act_low, w_dt, chan[KW + 1 : KW + 2], a_matrix)

    act_wide = act_rows.astype(f32)
    gate_in = scan_out.reshape(rows, width) + chan[KW + 2] * act_wide
    gate_act = jax.nn.silu(gate_part)
    gated_low = (gate_in * gate_act).astype(bf16)

    def own_rows(x):
        x = x.reshape(seqs, dps, piece, model).transpose(1, 0, 2, 3)
        return reduce_dp(x).reshape(batches, groups, piece, model)

    block_output = (tokens.astype(f32) + own_rows(contract(gated_low, out_low, 1, 0))).astype(bf16)

    grad_gated = contract(cot_low, out_low, 1, 1)
    grad_gate_in = grad_gated * gate_act
    grad_gate_low = (grad_gated * gate_in * silu_slope(gate_part)).astype(bf16)
    grad_skip = jnp.sum(grad_gate_in * act_wide, axis=0)

    def own_sum(x):
        parts = lax.all_to_all(x.astype(bf16), "fsdp", 0, 0, tiled=True)
        return jnp.sum(parts.astype(f32), axis=0)

    grad_out = own_sum(contract(gated_low, cot_low, 0, 0).reshape(fsdps, own, model))

    def own_in_sum(x):
        parts = x.astype(bf16).reshape(dps * fsdps, own_in, width)
        parts = lax.all_to_all(parts, ("dp", "fsdp"), 0, 0, tiled=True)
        parts = parts.reshape(dps, fsdps, own_in, width)
        return jnp.sum(parts.astype(f32), axis=1).transpose(1, 0, 2)

    grad_in_gate = own_in_sum(contract(normed, grad_gate_low, 0, 0))
    gsp, gact, gdrive, gread, grad_alog = scan_backward(
        xt,
        act_low,
        dt,
        step_pre,
        grad_gate_in.reshape(seqs, length, width),
        chan[KW + 2 : KW + 3],
        a_matrix,
        states,
    )
    gsp = gsp.reshape(rows, width)
    grad_step_bias = jnp.sum(gsp.astype(f32), axis=0)
    grad_dt = contract(gsp, xt[:R], 0, 1)
    grad_rank = contract(w_dt, gsp, 0, 1)
    gxt = sum_dp(jnp.concatenate([grad_rank, gdrive, gread], axis=0))
    grad_x = contract(act_rows, gxt, 0, 1)
    grad_act = gact.reshape(rows, width) + contract(gxt, w_x, 0, 1)
    grad_conv = grad_act.reshape(seqs, length, width) * silu_slope(conv_pre)
    chan_rows = []
    grad_conv_input = jnp.zeros_like(grad_conv)
    for offset in range(KW):
        by = KW - 1 - offset
        chan_rows.append(jnp.sum(grad_conv * later(conv_input, by), axis=(0, 1)))
        grad_conv_input = grad_conv_input + chan[offset] * later(grad_conv, -by)
    chan_rows += [jnp.sum(grad_conv, axis=(0, 1)), grad_step_bias, grad_skip]
    grad_conv_low = grad_conv_input.reshape(rows, width).astype(bf16)
    grad_in_conv = own_in_sum(contract(normed, grad_conv_low, 0, 0))
    small_grad = jnp.concatenate(
        [
            grad_x,
            grad_dt,
            jnp.concatenate([grad_alog, jnp.stack(chan_rows), jnp.zeros((9, width), f32)], axis=0).T,
        ],
        axis=1,
    )
    own_small = own_sum(small_grad.reshape(fsdps, own, -1))
    grad_normed = own_rows(contract(grad_conv_low, w_in[0], 1, 1) + contract(grad_gate_low, w_in[1], 1, 1))

    own_tokens = tokens.astype(f32)
    own_inv = lax.rsqrt(jnp.mean(own_tokens * own_tokens, axis=-1, keepdims=True) + 1e-05)
    grad_scaled = grad_normed * gain
    input_grad = (
        own_inv * grad_scaled
        - own_tokens
        * own_inv
        * own_inv
        * own_inv
        * jnp.mean(grad_scaled * own_tokens, axis=-1, keepdims=True)
        + cotangent.astype(f32)
    )

    grad_in = jnp.stack([grad_in_conv, grad_in_gate], axis=1).reshape(own_in, 2 * dps * width)
    low_gain = norm_gain.astype(bf16).astype(f32)
    grad_gain = jnp.sum(grad_in * in_weight.astype(bf16).astype(f32), axis=1) / low_gain
    rest = own_small[:, 2 * R + 2 * N :].T
    reduced = (
        grad_in,
        grad_out,
        own_small[:, : R + 2 * N],
        own_small[:, R + 2 * N : 2 * R + 2 * N].T,
        rest[N : N + KW + 3],
        rest[:N],
        grad_gain,
    )
    squares = jnp.zeros((), f32)
    for gradient in reduced:
        squares = squares + jnp.sum(gradient * gradient)
    grad_norm = jnp.sqrt(sum_all(squares))
    factor = jnp.minimum(1.0, clip_limit / (grad_norm + 1e-06))
    weight_list = (in_weight, out_weight, xproj_weight, dtproj_weight, chan_params, a_log, norm_gain)
    moment_list = (
        in_moments,
        out_moments,
        xproj_moments,
        dtproj_moments,
        chan_moments,
        alog_moments,
        gain_moments,
    )
    outputs = [block_output, input_grad, grad_norm]
    for place in range(7):
        outputs += adam_update(
            weight_list[place], moment_list[place], reduced[place] * factor, learn_rates[place]
        )
    return tuple(outputs)


def solution(mesh):
    both = ("dp", "fsdp")
    row_specs = (P(None, "fsdp", "dp", None),) * 2
    weight_specs = (
        P(both, None),
        P(both, None),
        P(both, None),
        P(None, both),
        P(None, both),
        P(None, both),
        P(both),
    )
    moment_specs = (
        P(None, both, None),
        P(None, both, None),
        P(None, both, None),
        P(None, None, both),
        P(None, None, both),
        P(None, None, both),
        P(None, both),
    )
    updated = tuple(spec for pair in zip(moment_specs, weight_specs) for spec in pair)
    return jax.shard_map(
        shards,
        mesh=mesh,
        in_specs=row_specs + weight_specs + moment_specs,
        out_specs=row_specs + (P(),) + updated,
        check_vma=False,
    )
```

```python
import jax
import jax.numpy as jnp
from jax import lax
from jax.experimental import pallas as pl
from jax.experimental.pallas import tpu as pltpu
from jax.sharding import PartitionSpec as P

N = 16
R = 64
KW = 4
STEP = 7
ROWS = 128
T = 16
WIDE = R + 2 * N
REST = 32
GRADS = WIDE + R + REST
AT_DT = 128
AT_REST = 192
SMALL = 256
BIG = 512

bf16 = jnp.bfloat16
f32 = jnp.float32
LOG2E = 1.4426950408889634
clip_limit = 1.0
learn_rates = (0.03, 0.03, 0.03, 0.15, 0.3, 1.0, 0.3)


def dot(left, right, on_left, on_right):
    return lax.dot_general(
        left, right, (((on_left,), (on_right,)), ((), ())), preferred_element_type=f32
    )


def params(mib):
    return pltpu.CompilerParams(vmem_limit_bytes=mib * 1024 * 1024)


def cost(us):
    return pl.CostEstimate(flops=int(us * 8e7), bytes_accessed=int(us * 3e5), transcendentals=0)


def swap(x, axis, mask):
    peers = lax.axis_size(axis)
    return lax.ppermute(x, axis, [(i, i ^ mask) for i in range(peers)])


def after(x, *others):
    return lax.optimization_barrier((x,) + others)[0]


def masks(axis):
    peers = lax.axis_size(axis)
    return [1 << k for k in range(peers.bit_length() - 1)]


def in_order(parts, axis):
    peers = lax.axis_size(axis)
    for mask in masks(axis):
        pairs = parts.reshape((peers // (2 * mask), 2, mask) + parts.shape[1:])
        high = (lax.axis_index(axis) & mask) != 0
        parts = jnp.where(high, pairs[:, ::-1], pairs).reshape(parts.shape)
    return parts


def parts_dp_far(x):
    held = [x]
    for mask in masks("dp")[:0:-1]:
        held = [part for p in held for part in (p, swap(p, "dp", mask))]
    return held


def parts_dp_near(held):
    return [part for p in held for part in (p, swap(p, "dp", 1))]


def gather_far(x):
    peers = lax.axis_size("fsdp")
    depth = min(4, peers)
    return [x] + [swap(x, "fsdp", m * (peers // depth)) for m in range(1, depth)]


def gather_near(far):
    far = jnp.stack(far)
    near = lax.axis_size("fsdp") // far.shape[0]
    return [far] + [swap(far, "fsdp", m) for m in range(1, near)]


def merge_near(nears):
    parts = jnp.stack(nears, axis=1)
    return in_order(parts.reshape((-1,) + parts.shape[2:]), "fsdp")


def reduce_dp_near(parts):
    return [parts[p] + swap(parts[p + 1], "dp", 1).astype(f32) for p in range(0, len(parts), 2)]


def send_dp_far(parts):
    for mask in masks("dp")[1:-1]:
        parts = [
            parts[p] + swap(parts[p + 1].astype(bf16), "dp", mask).astype(f32)
            for p in range(0, len(parts), 2)
        ]
    return [parts[0]] + [
        swap(part.astype(bf16), "dp", masks("dp")[-1]) for part in parts[1:]
    ]


def send_dp(parts):
    return [parts[0]] + [swap(parts[m], "dp", m) for m in range(1, len(parts))]


def sum_dp_near(x):
    high = (lax.axis_index("dp") & 1) != 0
    split = x.reshape((2, x.shape[0] // 2) + x.shape[1:])
    mine = jnp.where(high, split[1], split[0])
    other = jnp.where(high, split[0], split[1])
    return mine + swap(other, "dp", 1)


def sum_dp_far(mine):
    high = (lax.axis_index("dp") & 1) != 0
    for mask in masks("dp")[1:]:
        mine = mine + swap(mine, "dp", mask)
    mine = mine.astype(bf16)
    other = swap(mine, "dp", 1)
    both = jnp.where(high, jnp.stack([other, mine]), jnp.stack([mine, other]))
    return both.reshape((-1,) + mine.shape[1:])


def reduce_near(parts):
    mine = parts[0].astype(f32)
    for m in range(1, len(parts)):
        mine = mine + swap(parts[m].astype(bf16), "fsdp", m).astype(f32)
    return mine


def split_near(x):
    peers = lax.axis_size("fsdp")
    depth = min(4, peers)
    x = in_order(x, "fsdp").reshape((depth, peers // depth) + x.shape[1:])
    return [x[:, m] for m in range(x.shape[1])]


def send_far(mine):
    depth = mine.shape[0]
    near = lax.axis_size("fsdp") // depth
    return [mine[0]] + [
        swap(mine[m].astype(bf16), "fsdp", m * near) for m in range(1, depth)
    ]


def assemble_first_kernel(me_ref, *refs):
    raws = refs[:-6]
    w_ref, small_ref, gain_ref, a_ref, chan_ref, gains = refs[-6:]
    near = len(raws)
    depth = raws[0].shape[0]
    model, width = w_ref.shape
    peers = near * depth
    own = width // peers
    fold = width // SMALL
    here = model // peers
    own_in = model // gains.shape[0]
    dps = here // own_in
    stretch = own // fold
    at_small = here + dps + -dps % 16
    for m in range(near):
        for d in range(depth):
            j = me_ref[1] ^ (d * near + m)
            for k in range(dps):
                to = pl.multiple_of((k * peers + j) * own_in, own_in)
                w_ref[pl.ds(to, own_in), :] = raws[m][d, k * own_in : (k + 1) * own_in, :]
                row = raws[m][d, here : here + 16, 0:128].astype(f32)[k : k + 1]
                gains[pl.ds(k * peers + j, 1), :] = row
            for f in range(fold):
                to = pl.multiple_of(j * own + f * stretch, stretch)
                small_ref[pl.ds(to, stretch), :] = raws[m][
                    d, at_small : at_small + stretch, f * SMALL : (f + 1) * SMALL
                ]
    row = lax.broadcasted_iota(jnp.int32, (own_in, model), 0)
    column = lax.broadcasted_iota(jnp.int32, (own_in, model), 1)
    tile = (column % own_in == row).astype(f32).astype(bf16)
    tiled = dot(gains[:, 0:own_in].astype(bf16), tile, 1, 0)
    row = lax.broadcasted_iota(jnp.int32, tiled.shape, 0)
    column = lax.broadcasted_iota(jnp.int32, tiled.shape, 1)
    gain_ref[...] = jnp.sum(jnp.where(column // own_in == row, tiled, 0.0), axis=0, keepdims=True)
    turned = small_ref[...].astype(f32).T
    a_ref[...] = -jnp.exp(turned[AT_REST : AT_REST + N])
    chan_ref[...] = turned[AT_REST + N : AT_REST + N + 8]


def assemble_second_kernel(me_ref, *refs):
    raws = refs[:-2]
    wg_ref, wo_ref = refs[-2:]
    near = len(raws)
    depth = raws[0].shape[0]
    model, width = wg_ref.shape
    peers = near * depth
    own = width // peers
    here = model // peers
    dps = lax.axis_size("dp")
    own_in = here // dps
    for m in range(near):
        for d in range(depth):
            j = me_ref[1] ^ (d * near + m)
            for k in range(dps):
                to = pl.multiple_of((k * peers + j) * own_in, own_in)
                wg_ref[pl.ds(to, own_in), :] = raws[m][d, k * own_in : (k + 1) * own_in, :]
            for c in range(model // width):
                to = pl.multiple_of(j * own, own)
                wo_ref[pl.ds(to, own), c * width : (c + 1) * width] = raws[m][
                    d, here + c * own : here + (c + 1) * own, :
                ]


def assemble(kernel, name, me, raws, shapes, scratch):
    whole = pl.BlockSpec(memory_space=pltpu.VMEM)
    return pl.pallas_call(
        kernel,
        in_specs=[pl.BlockSpec(memory_space=pltpu.SMEM)] + [whole] * len(raws),
        out_specs=[whole] * len(shapes),
        out_shape=[jax.ShapeDtypeStruct(shape, dtype) for shape, dtype in shapes],
        scratch_shapes=scratch,
        compiler_params=params(60),
        cost_estimate=cost(2),
        name=name,
    )(me, *raws)


def lay_pieces(whole, refs, me):
    piece = refs[0].shape[1]
    for p, ref in enumerate(refs):
        whole[pl.ds(pl.multiple_of((me ^ p) * piece, piece), piece), :] = ref[0]


def deal_pieces(refs, part, me, block):
    piece = refs[0].shape[1]
    per = part.shape[0] // piece
    for p, ref in enumerate(refs):
        at = (me ^ p) - block * per

        @pl.when((at >= 0) & (at < per))
        def _(ref=ref, at=at):
            ref[0] = part[pl.ds(pl.multiple_of(at * piece, piece), piece), :].astype(ref.dtype)


def piece_shapes(dps, seqs, piece, model, wide):
    return [
        jax.ShapeDtypeStruct((seqs, piece, model), bf16 if p % wide else f32) for p in range(dps)
    ]


def piece_specs(dps, piece, model):
    return [pl.BlockSpec((1, piece, model), lambda s, b, me: (s, 0, 0))] * dps


def enter_kernel(me_ref, gain_ref, w_ref, chan_ref, wx_ref, *refs):
    tok_refs = refs[:-7]
    normed_ref, conv_ref, pre_ref, act_ref, xt_ref, padded, whole = refs[-7:]
    block = pl.program_id(1)
    rows = conv_ref.shape[1]

    @pl.when(block == 0)
    def _():
        padded[0:8, :] = jnp.zeros((8, padded.shape[1]), f32)
        lay_pieces(whole, tok_refs, me_ref[0])

    @pl.when(block > 0)
    def _():
        padded[0:8, :] = padded[rows : rows + 8, :]

    x = whole[pl.ds(pl.multiple_of(block * rows, rows), rows), :].astype(f32)
    inv = lax.rsqrt(jnp.mean(x * x, axis=-1, keepdims=True) + 1e-05)
    normed = (x * inv * gain_ref[...]).astype(bf16)
    normed_ref[0] = normed
    conv = dot(normed, w_ref[...], 1, 0).astype(bf16)
    conv_ref[0] = conv
    padded[8 : rows + 8, :] = conv.astype(f32)
    pre = chan_ref[KW : KW + 1, :]
    for k in range(KW):
        pre = pre + chan_ref[k : k + 1, :] * padded[5 + k : 5 + k + rows, :]
    pre_ref[0] = pre
    act = (pre * jax.nn.sigmoid(pre)).astype(bf16)
    act_ref[0] = act
    xt_ref[...] = dot(wx_ref[:, 0:WIDE], act, 0, 1)


def enter(me, gain, w, chan, wx, tok):
    dps = len(tok)
    seqs, piece, model = tok[0].shape
    length = dps * piece
    width = w.shape[1]
    rows = min(BIG, length)
    blocks = length // rows

    def at(s, b, me):
        return (s, b, 0)

    def fixed(s, b, me):
        return (0, 0)

    return pl.pallas_call(
        enter_kernel,
        grid_spec=pltpu.PrefetchScalarGridSpec(
            num_scalar_prefetch=1,
            grid=(seqs, blocks),
            in_specs=[
                pl.BlockSpec((1, model), fixed),
                pl.BlockSpec((model, width), fixed),
                pl.BlockSpec((8, width), fixed),
                pl.BlockSpec((width, SMALL), fixed),
            ]
            + piece_specs(dps, piece, model),
            out_specs=[
                pl.BlockSpec((1, rows, model), at),
                pl.BlockSpec((1, rows, width), at),
                pl.BlockSpec((1, rows, width), at),
                pl.BlockSpec((1, rows, width), at),
                pl.BlockSpec((WIDE, rows), lambda s, b, me: (0, s * blocks + b)),
            ],
            scratch_shapes=[pltpu.VMEM((rows + 8, width), f32), pltpu.VMEM((length, model), bf16)],
        ),
        out_shape=[
            jax.ShapeDtypeStruct((seqs, length, model), bf16),
            jax.ShapeDtypeStruct((seqs, length, width), bf16),
            jax.ShapeDtypeStruct((seqs, length, width), f32),
            jax.ShapeDtypeStruct((seqs, length, width), bf16),
            jax.ShapeDtypeStruct((WIDE, seqs * length), f32),
        ],
        compiler_params=params(60),
        cost_estimate=cost(7),
        name="enter",
    )(me, gain, w, chan, wx, *tok)


def own_columns_of(rows):
    row = lax.broadcasted_iota(jnp.int32, (rows, T * N), 0)
    column = lax.broadcasted_iota(jnp.int32, (rows, T * N), 1)
    return column // N == row % T


def spread(block):
    row = lax.broadcasted_iota(jnp.int32, (N, T * N), 0)
    column = lax.broadcasted_iota(jnp.int32, (N, T * N), 1)
    tile = (column % N == row).astype(f32).astype(bf16)
    tiled = jnp.dot(block.astype(bf16), tile, preferred_element_type=f32)
    return jnp.where(own_columns_of(block.shape[0]), tiled, 0.0).astype(bf16)


def softplus(v):
    return jnp.maximum(v, 0.0) + jnp.log1p(jnp.exp(-jnp.abs(v)))


def forward_kernel(
    xt_ref, act_ref, dtw_ref, chan_ref, a_ref, gate_in_ref, h_ref, dt_ref, sp_ref, state, push
):
    @pl.when(pl.program_id(1) == 0)
    def _():
        state[...] = jnp.zeros_like(state)

    columns = xt_ref[...].astype(f32)
    rows_in = columns.T
    rank = rows_in[:, :R].astype(bf16)
    pre = dot(rank, dtw_ref[:, AT_DT : AT_DT + R], 1, 1) + chan_ref[KW + 1 : KW + 2, :]
    sp_ref[0] = pre
    steps = softplus(pre)
    dt_ref[0] = steps
    push[...] = steps * act_ref[0].astype(f32)
    scaled = a_ref[...] * LOG2E
    drive = columns[R : R + N]
    reads = spread(rows_in[:, R + N :])
    h = state[...]
    for k in range(ROWS // T):
        for j in range(T):
            t = k * T + j
            decay = jnp.exp2(dt_ref[0, t : t + 1, :] * scaled)
            h = decay * h + drive[:, t : t + 1] * push[t : t + 1, :]
            h_ref[0, t * N : (t + 1) * N, :] = h.astype(bf16)
        here = slice(k * T, (k + 1) * T)
        scanned = dot(reads[here], h_ref[0, k * T * N : (k + 1) * T * N, :], 1, 0)
        gate_in_ref[0, here, :] = scanned + chan_ref[KW + 2 : KW + 3, :] * act_ref[
            0, here, :
        ].astype(f32)
    state[...] = h


def scan_forward(xt, act, dtw, chan, a_matrix):
    seqs, length, width = act.shape
    blocks = length // ROWS

    def at(s, b):
        return (s, b, 0)

    def fixed(s, b):
        return (0, 0)

    return pl.pallas_call(
        forward_kernel,
        grid=(seqs, blocks),
        in_specs=[
            pl.BlockSpec((WIDE, ROWS), lambda s, b: (0, s * blocks + b)),
            pl.BlockSpec((1, ROWS, width), at),
            pl.BlockSpec((width, SMALL), fixed),
            pl.BlockSpec((8, width), fixed),
            pl.BlockSpec((N, width), fixed),
        ],
        out_specs=[
            pl.BlockSpec((1, ROWS, width), at),
            pl.BlockSpec((1, ROWS * N, width), at),
            pl.BlockSpec((1, ROWS, width), at),
            pl.BlockSpec((1, ROWS, width), at),
        ],
        out_shape=[
            jax.ShapeDtypeStruct((seqs, length, width), f32),
            jax.ShapeDtypeStruct((seqs, length * N, width), bf16),
            jax.ShapeDtypeStruct((seqs, length, width), f32),
            jax.ShapeDtypeStruct((seqs, length, width), f32),
        ],
        scratch_shapes=[pltpu.VMEM((N, width), f32), pltpu.VMEM((ROWS, width), f32)],
        compiler_params=params(60),
        cost_estimate=cost(18),
        name="scan_forward",
    )(xt, act, dtw, chan, a_matrix)


def middle_kernel(
    me_ref,
    gate_in_ref,
    act_ref,
    normed_ref,
    wg_ref,
    wo_ref,
    *refs,
):
    dps = lax.axis_size("dp")
    near = len(refs) - 2 * dps - 8
    cot_refs, part_refs = refs[:dps], refs[dps : 2 * dps]
    gout_refs = refs[2 * dps : 2 * dps + near]
    ggi_ref, ggp_ref, gin_ref, gskip_ref = refs[2 * dps + near : 2 * dps + near + 4]
    out_total, in_total, whole, part = refs[2 * dps + near + 4 :]
    block = pl.program_id(1)
    rows = act_ref.shape[1]
    start = (pl.program_id(0) == 0) & (block == 0)
    end = (pl.program_id(0) == pl.num_programs(0) - 1) & (block == pl.num_programs(1) - 1)

    @pl.when(start)
    def _():
        out_total[...] = jnp.zeros_like(out_total)
        in_total[...] = jnp.zeros_like(in_total)
        gskip_ref[...] = jnp.zeros_like(gskip_ref)

    @pl.when(block == 0)
    def _():
        lay_pieces(whole, cot_refs, me_ref[0])

    cot = whole[pl.ds(pl.multiple_of(block * rows, rows), rows), :]
    grad_gated = dot(cot, wo_ref[...], 1, 1)
    normed = normed_ref[0]
    gate = dot(normed, wg_ref[...], 1, 0).astype(bf16).astype(f32)
    sig = jax.nn.sigmoid(gate)
    gate_act = gate * sig
    gate_in = gate_in_ref[0]
    gated = (gate_in * gate_act).astype(bf16)
    ggi = grad_gated * gate_act
    ggi_ref[0] = ggi
    ggp = (grad_gated * gate_in * (sig * (1.0 + gate * (1.0 - sig)))).astype(bf16)
    ggp_ref[0] = ggp
    gskip_ref[...] += jnp.sum(ggi * act_ref[0].astype(f32), axis=0, keepdims=True)
    part[...] = dot(gated, wo_ref[...], 1, 0)
    deal_pieces(part_refs, part, me_ref[0], block)
    out_total[...] += dot(gated, cot, 0, 0)
    in_total[...] += dot(normed, ggp, 0, 0)

    @pl.when(end)
    def _():
        gin_ref[...] = in_total[...].astype(bf16)
        depth, own, _ = gout_refs[0].shape
        for j in range(near * depth):
            place = me_ref[1] ^ j
            for m, ref in enumerate(gout_refs):

                @pl.when(place % near == m)
                def _(ref=ref, place=place, j=j):
                    ref[place // near] = out_total[j * own : (j + 1) * own, :].astype(bf16)


def middle(me, gate_in, act, normed, wg, wo, cot, near, depth):
    dps = len(cot)
    seqs, piece, model = cot[0].shape
    length = dps * piece
    width = wo.shape[0]
    rows = min(BIG, length)
    blocks = length // rows
    own = width // (near * depth)

    def at(s, b, me):
        return (s, b, 0)

    def fixed(s, b, me):
        return (0, 0)

    return pl.pallas_call(
        middle_kernel,
        grid_spec=pltpu.PrefetchScalarGridSpec(
            num_scalar_prefetch=1,
            grid=(seqs, blocks),
            in_specs=[
                pl.BlockSpec((1, rows, width), at),
                pl.BlockSpec((1, rows, width), at),
                pl.BlockSpec((1, rows, model), at),
                pl.BlockSpec((model, width), fixed),
                pl.BlockSpec((width, model), fixed),
            ]
            + piece_specs(dps, piece, model),
            out_specs=piece_specs(dps, piece, model)
            + [pl.BlockSpec((depth, own, model), lambda s, b, me: (0, 0, 0))] * near
            + [
                pl.BlockSpec((1, rows, width), at),
                pl.BlockSpec((1, rows, width), at),
                pl.BlockSpec((model, width), fixed),
                pl.BlockSpec((1, width), fixed),
            ],
            scratch_shapes=[
                pltpu.VMEM((width, model), f32),
                pltpu.VMEM((model, width), f32),
                pltpu.VMEM((length, model), bf16),
                pltpu.VMEM((rows, model), f32),
            ],
        ),
        out_shape=piece_shapes(dps, seqs, piece, model, dps)
        + [jax.ShapeDtypeStruct((depth, own, model), bf16)] * near
        + [
            jax.ShapeDtypeStruct((seqs, length, width), f32),
            jax.ShapeDtypeStruct((seqs, length, width), bf16),
            jax.ShapeDtypeStruct((model, width), bf16),
            jax.ShapeDtypeStruct((1, width), f32),
        ],
        compiler_params=params(60),
        cost_estimate=cost(9),
        name="middle",
    )(me, gate_in, act, normed, wg, wo, *cot)


def backward_kernel(
    xt_ref,
    act_ref,
    dt_ref,
    sp_ref,
    ggi_ref,
    chan_ref,
    a_ref,
    h_ref,
    before_ref,
    dtw_ref,
    *refs,
):
    gsp_ref, gact_ref, gxt_ref, galog_ref, carried, total, g_buf, q_buf = refs[-8:]
    first = pl.program_id(0) == pl.num_programs(0) - 1

    @pl.when(pl.program_id(0) == 0)
    def _():
        carried[...] = jnp.zeros_like(carried)
        total[...] = jnp.zeros_like(total)

    columns = xt_ref[...].astype(f32)
    rows_in = columns.T
    a_now = a_ref[...]
    scaled = a_now * LOG2E
    read = columns[R + N :]
    ones = own_columns_of(T).astype(f32).astype(bf16)
    drives = spread(rows_in[:, R : R + N])
    ggi_low = ggi_ref[0].astype(bf16)
    push_low = (dt_ref[0] * act_ref[0].astype(f32)).astype(bf16)
    lanes = lax.broadcasted_iota(jnp.int32, (N, T), 1)
    p = carried[...]
    acc = total[...]
    for k in reversed(range(ROWS // T)):
        for j in reversed(range(T)):
            t = k * T + j
            step_row = dt_ref[0, t : t + 1, :]
            g = read[:, t : t + 1] * ggi_ref[0, t : t + 1, :] + p
            p = jnp.exp2(step_row * scaled) * g
            if t > 0:
                h_before = h_ref[0, (t - 1) * N : t * N, :].astype(f32)
            else:
                h_before = jnp.where(first, 0.0, before_ref[0].astype(f32))
            q = p * h_before
            acc = acc + q * step_row
            g_buf[t * N : (t + 1) * N, :] = g.astype(bf16)
            q_buf[t * N : (t + 1) * N, :] = (a_now * q).astype(bf16)
        here = slice(k * T, (k + 1) * T)
        states = slice(k * T * N, (k + 1) * T * N)
        pulled = dot(drives[here], g_buf[states, :], 1, 0)
        along = dot(ones, q_buf[states, :], 1, 0)
        act_now = act_ref[0, here, :].astype(f32)
        grad_steps = along + act_now * pulled
        gsp_ref[0, here, :] = (grad_steps * jax.nn.sigmoid(sp_ref[0, here, :])).astype(bf16)
        gact_ref[0, here, :] = (
            pulled * dt_ref[0, here, :] + chan_ref[KW + 2 : KW + 3, :] * ggi_ref[0, here, :]
        )
        both_d = dot(g_buf[states, :], push_low[here], 1, 1)
        both_r = dot(h_ref[0, states, :], ggi_low[here], 1, 1)
        gdrive = jnp.zeros((N, T), f32)
        gread = jnp.zeros((N, T), f32)
        for j in range(T):
            gdrive = jnp.where(lanes == j, both_d[j * N : (j + 1) * N], gdrive)
            gread = jnp.where(lanes == j, both_r[j * N : (j + 1) * N], gread)
        gxt_ref[R : R + N, here] = gdrive
        gxt_ref[R + N :, here] = gread
    carried[...] = p
    total[...] = acc
    gxt_ref[0:R, :] = dot(dtw_ref[:, AT_DT : AT_DT + R], gsp_ref[0], 0, 1)
    galog_ref[...] = acc * a_now


def scan_backward(s, earlier, xt, act, dt, sp, ggi, chan, a_matrix, states, dtw):
    seqs, length, width = act.shape
    blocks = length // ROWS

    def back(b):
        return (s, blocks - 1 - b, 0)

    def before(b):
        return (s, jnp.maximum((blocks - 1 - b) * ROWS - 1, 0), 0)

    def flat(b):
        return (0, s * blocks + blocks - 1 - b)

    def fixed(b):
        return (0, 0)

    return pl.pallas_call(
        backward_kernel,
        grid=(blocks,),
        in_specs=[
            pl.BlockSpec((WIDE, ROWS), flat),
            pl.BlockSpec((1, ROWS, width), back),
            pl.BlockSpec((1, ROWS, width), back),
            pl.BlockSpec((1, ROWS, width), back),
            pl.BlockSpec((1, ROWS, width), back),
            pl.BlockSpec((8, width), fixed),
            pl.BlockSpec((N, width), fixed),
            pl.BlockSpec((1, ROWS * N, width), back),
            pl.BlockSpec((1, N, width), before),
            pl.BlockSpec((width, SMALL), fixed),
        ]
        + [pl.BlockSpec(memory_space=pl.ANY)] * len(earlier),
        out_specs=[
            pl.BlockSpec((1, ROWS, width), back),
            pl.BlockSpec((1, ROWS, width), back),
            pl.BlockSpec((WIDE, ROWS), flat),
            pl.BlockSpec((N, width), fixed),
        ],
        out_shape=[
            jax.ShapeDtypeStruct((seqs, length, width), bf16),
            jax.ShapeDtypeStruct((seqs, length, width), f32),
            jax.ShapeDtypeStruct((WIDE, seqs * length), f32),
            jax.ShapeDtypeStruct((N, width), f32),
        ],
        scratch_shapes=[
            pltpu.VMEM((N, width), f32),
            pltpu.VMEM((N, width), f32),
            pltpu.VMEM((ROWS * N, width), bf16),
            pltpu.VMEM((ROWS * N, width), bf16),
        ],
        input_output_aliases={10 + k: k for k in range(len(earlier))},
        compiler_params=params(60),
        cost_estimate=cost(16),
        name=f"scan_backward_{s}",
    )(xt, act, dt, sp, ggi, chan, a_matrix, states, states, dtw, *earlier)


def leave_kernel(
    gact_ref,
    gxt_ref,
    xt_ref,
    gsp_ref,
    wx_ref,
    pre_ref,
    conv_ref,
    act_ref,
    normed_ref,
    chan_ref,
    gskip_ref,
    *refs,
):
    galog_refs = refs[:-6]
    gci_ref, gin_ref, small_ref, padded, in_total, sums = refs[-6:]
    block = pl.program_id(1)
    rows = gact_ref.shape[1]
    start = (pl.program_id(0) == 0) & (block == 0)
    end = (pl.program_id(0) == pl.num_programs(0) - 1) & (block == pl.num_programs(1) - 1)

    @pl.when(start)
    def _():
        in_total[...] = jnp.zeros_like(in_total)
        small_ref[...] = jnp.zeros_like(small_ref)
        sums[...] = jnp.zeros_like(sums)

    @pl.when(block == 0)
    def _():
        padded[rows : rows + 8, :] = jnp.zeros((8, padded.shape[1]), f32)

    @pl.when(block > 0)
    def _():
        padded[rows : rows + 8, :] = padded[0:8, :]

    gxt = gxt_ref[...]
    act = act_ref[0]
    grad_act = gact_ref[0] + dot(gxt, wx_ref[:, 0:WIDE], 0, 1)
    pre = pre_ref[0]
    sig = jax.nn.sigmoid(pre)
    grad_conv = grad_act * (sig * (1.0 + pre * (1.0 - sig)))
    padded[0:rows, :] = grad_conv
    conv = conv_ref[0].astype(f32)
    gci = jnp.zeros_like(grad_conv)
    for k in range(KW):
        moved = padded[KW - 1 - k : KW - 1 - k + rows, :]
        gci = gci + chan_ref[k : k + 1, :] * moved
        sums[N + k : N + k + 1, :] += jnp.sum(conv * moved, axis=0, keepdims=True)
    sums[N + KW : N + KW + 1, :] += jnp.sum(grad_conv, axis=0, keepdims=True)
    gsp = gsp_ref[0]
    sums[N + KW + 1 : N + KW + 2, :] += jnp.sum(gsp.astype(f32), axis=0, keepdims=True)
    low = gci.astype(bf16)
    gci_ref[0] = low
    in_total[...] += dot(normed_ref[0], low, 0, 0)
    small_ref[:, 0:WIDE] += dot(act, gxt, 0, 1)
    small_ref[:, WIDE : WIDE + R] += dot(gsp, xt_ref[0:R, :], 0, 1)

    @pl.when(end)
    def _():
        gin_ref[...] = in_total[...].astype(bf16)
        sums[0:N, :] = sum(ref[...] for ref in galog_refs)
        sums[N + KW + 2 : N + KW + 3, :] = gskip_ref[...]
        small_ref[:, WIDE + R :] = sums[...].T


def leave(gact, gxt, xt, gsp, wx, pre, conv, act, normed, chan, gskip, galog):
    seqs, length, width = act.shape
    model = normed.shape[2]
    rows = min(BIG, length)
    blocks = length // rows

    def back(s, b):
        return (s, blocks - 1 - b, 0)

    def flat(s, b):
        return (0, s * blocks + blocks - 1 - b)

    def fixed(s, b):
        return (0, 0)

    return pl.pallas_call(
        leave_kernel,
        grid=(seqs, blocks),
        in_specs=[
            pl.BlockSpec((1, rows, width), back),
            pl.BlockSpec((WIDE, rows), flat),
            pl.BlockSpec((WIDE, rows), flat),
            pl.BlockSpec((1, rows, width), back),
            pl.BlockSpec((width, SMALL), fixed),
            pl.BlockSpec((1, rows, width), back),
            pl.BlockSpec((1, rows, width), back),
            pl.BlockSpec((1, rows, width), back),
            pl.BlockSpec((1, rows, model), back),
            pl.BlockSpec((8, width), fixed),
            pl.BlockSpec((1, width), fixed),
        ]
        + [pl.BlockSpec((N, width), fixed)] * len(galog),
        out_specs=[
            pl.BlockSpec((1, rows, width), back),
            pl.BlockSpec((model, width), fixed),
            pl.BlockSpec((width, GRADS), fixed),
        ],
        out_shape=[
            jax.ShapeDtypeStruct((seqs, length, width), bf16),
            jax.ShapeDtypeStruct((model, width), bf16),
            jax.ShapeDtypeStruct((width, GRADS), f32),
        ],
        scratch_shapes=[
            pltpu.VMEM((rows + 8, width), f32),
            pltpu.VMEM((model, width), f32),
            pltpu.VMEM((REST, width), f32),
        ],
        compiler_params=params(60),
        cost_estimate=cost(8),
        name="leave",
    )(gact, gxt, xt, gsp, wx, pre, conv, act, normed, chan, gskip, *galog)


def rows_back_kernel(me_ref, gci_ref, ggp_ref, w0_ref, w1_ref, *refs):
    part = refs[-1]
    part[...] = dot(gci_ref[0], w0_ref[...], 1, 1) + dot(ggp_ref[0], w1_ref[...], 1, 1)
    deal_pieces(refs[:-1], part, me_ref[0], pl.program_id(1))


def rows_back(me, gci, ggp, w0, w1, dps):
    seqs, length, width = gci.shape
    model = w0.shape[0]
    piece = length // dps
    rows = min(BIG, length)
    blocks = length // rows

    def at(s, b, me):
        return (s, b, 0)

    def fixed(s, b, me):
        return (0, 0)

    return pl.pallas_call(
        rows_back_kernel,
        grid_spec=pltpu.PrefetchScalarGridSpec(
            num_scalar_prefetch=1,
            grid=(seqs, blocks),
            in_specs=[
                pl.BlockSpec((1, rows, width), at),
                pl.BlockSpec((1, rows, width), at),
                pl.BlockSpec((model, width), fixed),
                pl.BlockSpec((model, width), fixed),
            ],
            out_specs=piece_specs(dps, piece, model),
            scratch_shapes=[pltpu.VMEM((rows, model), f32)],
        ),
        out_shape=piece_shapes(dps, seqs, piece, model, 2),
        compiler_params=params(60),
        cost_estimate=cost(5),
        name="rows_back",
    )(me, gci, ggp, w0, w1)


def finish_kernel(tok_ref, cot_ref, gain_ref, *refs):
    out_ref = refs[-1]
    grad = refs[0][0]
    for ref in refs[1:-1]:
        grad = grad + ref[0].astype(f32)
    x = tok_ref[0].astype(f32)
    inv = lax.rsqrt(jnp.mean(x * x, axis=-1, keepdims=True) + 1e-05)
    grad = grad * gain_ref[...]
    back = x * inv * inv * inv * jnp.mean(grad * x, axis=-1, keepdims=True)
    out_ref[0] = inv * grad - back + cot_ref[0].astype(f32)


def finish(tok, cot, gain, parts):
    seqs, piece, model = tok.shape
    rows = pl.BlockSpec((1, piece, model), lambda s: (s, 0, 0))
    return pl.pallas_call(
        finish_kernel,
        grid=(seqs,),
        in_specs=[rows, rows, pl.BlockSpec((1, model), lambda s: (0, 0))] + [rows] * len(parts),
        out_specs=rows,
        out_shape=jax.ShapeDtypeStruct(tok.shape, f32),
        compiler_params=params(60),
        cost_estimate=cost(3),
        name="finish",
    )(tok, cot, gain, *parts)


def collect_kernel(
    conv_ref, gate_ref, out_ref, small_ref, w_ref, gain_ref, gin_ref, gx_ref, gdt_ref, gchan_ref, galog_ref, ggain_ref, squares_ref, square
):
    own_in, columns = w_ref.shape
    width = conv_ref.shape[2]
    dps = columns // (2 * width)
    peers = conv_ref.shape[0] // dps
    own = small_ref.shape[0]
    total = jnp.zeros((1, 128), f32)

    def squares(x):
        x = jnp.sum(x * x, axis=0, keepdims=True)
        return jnp.sum(x, axis=1, keepdims=True)

    ggain = jnp.zeros((own_in, 1), f32)
    for half in range(2):
        for k in range(dps):
            parts = gate_ref if half else conv_ref
            grad = parts[k * peers].astype(f32)
            for j in range(1, peers):
                grad = grad + parts[k * peers + j].astype(f32)
            here = slice((half * dps + k) * width, (half * dps + k + 1) * width)
            gin_ref[:, here] = grad
            total = total + squares(grad)
            low = w_ref[:, here].astype(bf16).astype(f32)
            ggain = ggain + jnp.sum(grad * low, axis=1, keepdims=True)
    total = total + squares(out_ref[...])
    small = small_ref[...]
    total = total + squares(small)
    gx_ref[...] = small[:, :WIDE]
    square[...] = jnp.zeros_like(square)
    square[0:own, 0:GRADS] = small
    square[0:own_in, GRADS : GRADS + 1] = ggain
    turned = square[...].T
    gdt_ref[...] = turned[WIDE : WIDE + R, :own]
    galog_ref[...] = turned[WIDE + R : WIDE + R + N, :own]
    gchan_ref[...] = turned[WIDE + R + N : WIDE + R + N + KW + 3, :own]
    grad = turned[GRADS : GRADS + 1, :own_in] / gain_ref[...].astype(bf16).astype(f32)
    ggain_ref[...] = grad
    squares_ref[...] = total + squares(grad)


def collect(conv, gate, out, small, w, gain):
    own_in, columns = w.shape
    own = small.shape[0]
    shapes = [
        (own_in, columns),
        (own, WIDE),
        (R, own),
        (KW + 3, own),
        (N, own),
        (1, own_in),
        (1, 128),
    ]
    whole = pl.BlockSpec(memory_space=pltpu.VMEM)
    return pl.pallas_call(
        collect_kernel,
        in_specs=[whole] * 6,
        out_specs=[whole] * len(shapes),
        out_shape=[jax.ShapeDtypeStruct(shape, f32) for shape in shapes],
        scratch_shapes=[pltpu.VMEM((128, 256), f32)],
        compiler_params=params(16),
        cost_estimate=cost(3),
        name="collect",
    )(conv, gate, out, small, w, gain)


def adam_kernel(squares_ref, *refs):
    count = len(learn_rates)
    weights, moments, grads = refs[:count], refs[count : 2 * count], refs[2 * count : 3 * count]
    outs = refs[3 * count :]
    norm = jnp.sqrt(jnp.sum(squares_ref[...], axis=0)[:, 0:1])
    outs[2 * count][...] = norm
    factor = jnp.minimum(1.0, clip_limit / (norm + 1e-06))
    for place in range(count):
        rate = learn_rates[place]
        gradient = grads[place][...] * factor
        weight = weights[place][...]
        rows_first = len(moments[place].shape) == 3 and moments[place].shape[1] == 2
        at = (lambda k: (slice(None), k)) if rows_first else (lambda k: k)
        first = 0.9 * moments[place][at(0)] + 0.1 * gradient
        old = moments[place][at(1)]
        root = jnp.sqrt(0.95 * old * old + 0.05 * gradient * gradient)
        update = first / (1.0 - 0.9**STEP) / (root / (1.0 - 0.95**STEP) ** 0.5 + 1e-08)
        outs[2 * place][at(0)] = first
        outs[2 * place][at(1)] = root
        outs[2 * place + 1][...] = weight - rate * (update + 0.01 * weight)


def adam(squares, weights, moments, grads):
    shapes = []
    for weight, moment in zip(weights, moments):
        shapes.append(jax.ShapeDtypeStruct(moment.shape, f32))
        shapes.append(jax.ShapeDtypeStruct(weight.shape, f32))
    shapes.append(jax.ShapeDtypeStruct((1, 1), f32))
    whole = pl.BlockSpec(memory_space=pltpu.VMEM)
    return pl.pallas_call(
        adam_kernel,
        in_specs=[whole] * (1 + 3 * len(weights)),
        out_specs=[whole] * len(shapes),
        out_shape=shapes,
        compiler_params=params(16),
        cost_estimate=cost(4),
        name="adam",
    )(squares, *weights, *moments, *grads)


def shards(
    tokens,
    cotangent,
    in_weight,
    out_weight,
    xproj_weight,
    dtproj_weight,
    chan_params,
    a_log,
    norm_gain,
    in_moments,
    out_moments,
    xproj_moments,
    dtproj_moments,
    chan_moments,
    alog_moments,
    gain_moments,
):
    both = ("dp", "fsdp")
    dps = lax.axis_size("dp")
    fsdps = lax.axis_size("fsdp")
    depth = min(4, fsdps)
    near = fsdps // depth
    me = jnp.stack([lax.axis_index("dp"), lax.axis_index("fsdp")])
    batches, groups, piece, model = tokens.shape
    seqs = batches * groups
    length = piece * dps
    own_in = in_weight.shape[0]
    own = out_weight.shape[0]
    width = own * fsdps

    in_low = in_weight.astype(bf16).reshape(own_in, 2, dps, width).transpose(2, 1, 0, 3)
    gain_row = jnp.pad(norm_gain.astype(bf16)[None], ((0, 7), (0, width - own_in)))
    in_parts = jnp.concatenate(
        [in_low[:, 0], in_low[:, 1], jnp.broadcast_to(gain_row, (dps, 8, width))], axis=1
    )
    in_parts = lax.all_to_all(in_parts, "dp", 0, 0, tiled=True)
    small = jnp.concatenate(
        [
            xproj_weight.astype(bf16),
            jnp.zeros((own, AT_DT - WIDE), bf16),
            dtproj_weight.astype(bf16).T,
            a_log.astype(bf16).T,
            chan_params.astype(bf16).T,
            jnp.zeros((own, SMALL - AT_REST - N - KW - 3), bf16),
        ],
        axis=1,
    )
    fold = max(width // SMALL, 1)
    aligned = own_in % 16 == 0 and own % (16 * fold) == 0 and width % SMALL == 0
    if aligned:
        packed = jnp.concatenate(jnp.split(small, fold), axis=1)
    else:
        packed = small.reshape(-1, width)
    here = dps * own_in
    gain_rows = jnp.pad(in_parts[:, 2 * own_in], ((0, -dps % 16), (0, 0)))
    first = jnp.concatenate([in_parts[:, :own_in].reshape(here, width), gain_rows, packed])
    tok = parts_dp_far(tokens.reshape(seqs, piece, model))
    first, tok = lax.optimization_barrier((gather_far(first), tok))
    cot = parts_dp_far(after(cotangent.reshape(seqs, piece, model), first))
    tok = parts_dp_near(tok)
    first, cot = lax.optimization_barrier((gather_near(first), cot))

    def own_columns(parts):
        parts = parts.reshape(fsdps, dps, own_in, width)
        return parts.transpose(1, 0, 2, 3).reshape(model, width)

    if aligned:
        w_conv, small, gain, a_matrix, chan = assemble(
            assemble_first_kernel,
            "assemble_first",
            me,
            first,
            [
                ((model, width), bf16),
                ((width, SMALL), bf16),
                ((1, model), f32),
                ((N, width), f32),
                ((8, width), f32),
            ],
            [pltpu.VMEM((model // own_in, 128), f32)],
        )
    else:
        merged = merge_near(first)
        w_conv = own_columns(merged[:, :here])
        gain = merged[:, here : here + dps, :own_in].transpose(1, 0, 2)
        gain = gain.reshape(1, model).astype(f32)
        small = merged[:, here + dps + -dps % 16 :].reshape(width, SMALL)
        rest = small[:, AT_REST : AT_REST + REST].astype(f32).T
        a_matrix = -jnp.exp(rest[:N])
        chan = rest[N : N + 8]

    out_low = out_weight.astype(bf16).reshape(own, model // width, width).transpose(1, 0, 2)
    second = [
        in_parts[:, own_in : 2 * own_in].reshape(here, width),
        out_low.reshape(-1, width),
    ]
    far = gather_far(jnp.concatenate(second))
    normed, conv, pre, act, xt = enter(me, gain, w_conv, chan, small, tok)
    cot = parts_dp_near(cot)
    xt, far = lax.optimization_barrier((xt, far))
    xt = sum_dp_near(xt)
    xt, far = lax.optimization_barrier((xt, far))
    second = gather_near(far)
    xt = sum_dp_far(xt)
    if aligned:
        w_gate, w_out = assemble(
            assemble_second_kernel,
            "assemble_second",
            me,
            second,
            [((model, width), bf16), ((width, model), bf16)],
            [],
        )
    else:
        merged = merge_near(second)
        w_gate = own_columns(merged[:, :here])
        w_out = merged[:, here:].reshape(fsdps, model // width, own, width)
        w_out = w_out.transpose(0, 2, 1, 3).reshape(width, model)
    gate_in, states, dt, step_pre = scan_forward(xt, act, small, chan, a_matrix)
    outs = middle(me, gate_in, act, normed, w_gate, w_out, cot, near, depth)
    part, gout = outs[:dps], outs[dps : dps + near]
    ggi, ggp, gin_gate, gskip = outs[dps + near :]
    gate_parts = lax.all_to_all(gin_gate.reshape(-1, own_in, width), both, 0, 0, tiled=True)
    gout_near = reduce_near(gout)
    out_rows = send_dp(part)

    back = ()
    galog = []
    for s in reversed(range(seqs)):
        *back, one = scan_backward(s, back, xt, act, dt, step_pre, ggi, chan, a_matrix, states, small)
        galog.append(one)
        if s == seqs - 1:
            ggi, gout_near = lax.optimization_barrier((ggi, gout_near))
    gsp, gact, gxt = back
    gout_far = send_far(gout_near)
    gxt, out_rows, gout_far = lax.optimization_barrier((gxt, out_rows, gout_far))
    gxt = sum_dp_far(sum_dp_near(gxt))
    gxt, gate_parts = lax.optimization_barrier((gxt, gate_parts))
    gci, gin_conv, small_grad = leave(
        gact, gxt, xt, gsp, small, pre, conv, act, normed, chan, gskip, galog
    )
    conv_parts = lax.all_to_all(gin_conv.reshape(-1, own_in, width), both, 0, 0, tiled=True)
    grad_out = sum(part.astype(f32) for part in gout_far)
    out_rows = sum(part.astype(f32) for part in out_rows).reshape(tokens.shape)
    block_output = (tokens.astype(f32) + out_rows).astype(bf16)
    small_near = reduce_near(split_near(small_grad.reshape(fsdps, own, GRADS)))
    part_back = rows_back(me, gci, ggp, w_conv, w_gate, dps)
    small_near, part_back = lax.optimization_barrier((small_near, part_back))
    own_small = sum(part.astype(f32) for part in send_far(small_near))
    part_back = send_dp_far(reduce_dp_near(part_back))

    def flat2(x):
        return x.reshape(x.shape[:-1] + (1, x.shape[-1]))

    grad_in, grad_x, grad_dt, grad_chan, grad_alog, grad_gain, squares = collect(
        conv_parts, gate_parts, grad_out, own_small, in_weight, flat2(norm_gain)
    )
    grad_normed = sum(part.astype(f32) for part in after(part_back, squares)).reshape(tokens.shape)

    input_grad = finish(
        tokens.reshape(seqs, piece, model),
        cotangent.reshape(seqs, piece, model),
        gain,
        after(part_back, squares),
    ).reshape(tokens.shape)
    squares = lax.all_to_all(
        jnp.broadcast_to(squares[None], (dps * fsdps, 1, 128)), both, 0, 0, tiled=True
    )
    weights = (in_weight, out_weight, xproj_weight, dtproj_weight, chan_params, a_log, flat2(norm_gain))
    moments = (
        in_moments,
        out_moments,
        xproj_moments,
        dtproj_moments,
        chan_moments.transpose(1, 0, 2),
        alog_moments,
        flat2(gain_moments),
    )
    grads = (grad_in, grad_out, grad_x, grad_dt, grad_chan, grad_alog, grad_gain)
    updated = list(adam(squares, weights, moments, grads))
    grad_norm = updated.pop().reshape(())
    updated[8] = updated[8].transpose(1, 0, 2)
    updated[-2] = updated[-2].reshape(gain_moments.shape)
    updated[-1] = updated[-1].reshape(norm_gain.shape)
    return (block_output, input_grad, grad_norm) + tuple(updated)


def solution(mesh):
    both = ("dp", "fsdp")
    row_specs = (P(None, "fsdp", "dp", None),) * 2
    weight_specs = (
        P(both, None),
        P(both, None),
        P(both, None),
        P(None, both),
        P(None, both),
        P(None, both),
        P(both),
    )
    moment_specs = (
        P(None, both, None),
        P(None, both, None),
        P(None, both, None),
        P(None, None, both),
        P(None, None, both),
        P(None, None, both),
        P(None, both),
    )
    updated = tuple(spec for pair in zip(moment_specs, weight_specs) for spec in pair)
    return jax.shard_map(
        shards,
        mesh=mesh,
        in_specs=row_specs + weight_specs + moment_specs,
        out_specs=row_specs + (P(),) + updated,
        check_vma=False,
    )
```

```python
import jax
import jax.numpy as jnp
from jax import lax
from jax.experimental import pallas as pl
from jax.experimental.pallas import tpu as pltpu
from jax.sharding import PartitionSpec as P

N = 16
R = 64
KW = 4
STEP = 7
ROWS = 128
T = 16
WIDE = R + 2 * N
REST = 32
GRADS = WIDE + R + REST
AT_DT = 128
AT_REST = 192
SMALL = 256
BIG = 512

bf16 = jnp.bfloat16
f32 = jnp.float32
LOG2E = 1.4426950408889634
clip_limit = 1.0
learn_rates = (0.03, 0.03, 0.03, 0.15, 0.3, 1.0, 0.3)


def dot(left, right, on_left, on_right):
    return lax.dot_general(
        left, right, (((on_left,), (on_right,)), ((), ())), preferred_element_type=f32
    )


def params(mib):
    return pltpu.CompilerParams(vmem_limit_bytes=mib * 1024 * 1024)


def cost(us):
    return pl.CostEstimate(flops=int(us * 8e7), bytes_accessed=int(us * 3e5), transcendentals=0)


def swap(x, axis, mask):
    peers = lax.axis_size(axis)
    return lax.ppermute(x, axis, [(i, i ^ mask) for i in range(peers)])


def after(x, *others):
    return lax.optimization_barrier((x,) + others)[0]


def masks(axis):
    peers = lax.axis_size(axis)
    return [1 << k for k in range(peers.bit_length() - 1)]


def in_order(parts, axis):
    peers = lax.axis_size(axis)
    for mask in masks(axis):
        pairs = parts.reshape((peers // (2 * mask), 2, mask) + parts.shape[1:])
        high = (lax.axis_index(axis) & mask) != 0
        parts = jnp.where(high, pairs[:, ::-1], pairs).reshape(parts.shape)
    return parts


def parts_dp_far(x):
    held = [x]
    for mask in masks("dp")[:0:-1]:
        held = [part for p in held for part in (p, swap(p, "dp", mask))]
    return held


def parts_dp_near(held):
    return [part for p in held for part in (p, swap(p, "dp", 1))]


def gather_far(x):
    peers = lax.axis_size("fsdp")
    depth = min(4, peers)
    return [x] + [swap(x, "fsdp", m * (peers // depth)) for m in range(1, depth)]


def swap_near(x):
    near = lax.axis_size("fsdp") // min(4, lax.axis_size("fsdp"))
    return [swap(x, "fsdp", m) for m in range(1, near)]


def merge_near(far, own, rest):
    nears = [far] + [[one] + list(stack) for one, stack in zip(own, rest)]
    parts = jnp.stack([part for both in zip(*nears) for part in both])
    return in_order(parts, "fsdp")


def send_dp_near(parts):
    moved = [swap(part, "dp", 1) for part in parts[1::2]]
    sums = [kept + part.astype(f32) for kept, part in zip(parts[2::2], moved[1:])]
    return [parts[0], moved[0]], [part.astype(bf16) for part in sums]


def send_dp_far(mine, parts):
    for mask in masks("dp")[1:]:
        moved = [swap(part, "dp", mask) for part in parts[0::2]]
        mine = mine + [moved[0]]
        parts = [
            (kept.astype(f32) + part.astype(f32)).astype(bf16)
            for kept, part in zip(parts[1::2], moved[1:])
        ]
    return mine


def sum_dp_near(mine, other):
    return mine + swap(other, "dp", 1)


def sum_dp_far(mine, sent):
    high = (lax.axis_index("dp") & 1) != 0
    for mask in masks("dp")[1:]:
        mine = mine + swap(mine.astype(sent), "dp", mask).astype(f32)
    mine = mine.astype(bf16)
    other = swap(mine, "dp", 1)
    both = jnp.where(high, jnp.stack([other, mine]), jnp.stack([mine, other]))
    return both.reshape((-1,) + mine.shape[1:])


def reduce_near(parts):
    mine = parts[0].astype(f32)
    for m in range(1, len(parts)):
        mine = mine + swap(parts[m].astype(bf16), "fsdp", m).astype(f32)
    return [mine[0]] + [mine[d].astype(bf16) for d in range(1, mine.shape[0])]


def split_near(x):
    peers = lax.axis_size("fsdp")
    depth = min(4, peers)
    x = in_order(x, "fsdp").reshape((depth, peers // depth) + x.shape[1:])
    return [x[:, m] for m in range(x.shape[1])]


def send_far(mine):
    near = lax.axis_size("fsdp") // len(mine)
    return mine[:1] + [swap(mine[m], "fsdp", m * near) for m in range(1, len(mine))]


def by_near(refs, depth):
    parts = []
    for ref in refs:
        parts += [ref] if len(ref.shape) == 2 else [ref.at[d] for d in range(ref.shape[0])]
    return [parts[k : k + depth] for k in range(0, len(parts), depth)]


def assemble_first_kernel(me_ref, *refs):
    w_ref, small_ref, gain_ref, a_ref, chan_ref, gains = refs[-6:]
    model, width = w_ref.shape
    peers = lax.axis_size("fsdp")
    depth = min(4, peers)
    near = peers // depth
    raws = by_near(refs[:-6], depth)
    own = width // peers
    fold = width // SMALL
    here = model // peers
    own_in = model // gains.shape[0]
    dps = here // own_in
    stretch = own // fold
    at_small = here + dps + -dps % 16
    for m in range(near):
        for d in range(depth):
            j = me_ref[1] ^ (d * near + m)
            for k in range(dps):
                to = pl.multiple_of((k * peers + j) * own_in, own_in)
                w_ref[pl.ds(to, own_in), :] = raws[m][d][k * own_in : (k + 1) * own_in, :]
                row = raws[m][d][here : here + 16, 0:128].astype(f32)[k : k + 1]
                gains[pl.ds(k * peers + j, 1), :] = row
            for f in range(fold):
                to = pl.multiple_of(j * own + f * stretch, stretch)
                small_ref[pl.ds(to, stretch), :] = raws[m][d][
                    at_small : at_small + stretch, f * SMALL : (f + 1) * SMALL
                ]
    row = lax.broadcasted_iota(jnp.int32, (own_in, model), 0)
    column = lax.broadcasted_iota(jnp.int32, (own_in, model), 1)
    tile = (column % own_in == row).astype(f32).astype(bf16)
    tiled = dot(gains[:, 0:own_in].astype(bf16), tile, 1, 0)
    row = lax.broadcasted_iota(jnp.int32, tiled.shape, 0)
    column = lax.broadcasted_iota(jnp.int32, tiled.shape, 1)
    gain_ref[...] = jnp.sum(jnp.where(column // own_in == row, tiled, 0.0), axis=0, keepdims=True)
    turned = small_ref[...].astype(f32).T
    a_ref[...] = -jnp.exp(turned[AT_REST : AT_REST + N])
    chan_ref[...] = turned[AT_REST + N : AT_REST + N + 8]


def assemble_second_kernel(me_ref, *refs):
    wg_ref, wo_ref = refs[-2:]
    model, width = wg_ref.shape
    peers = lax.axis_size("fsdp")
    depth = min(4, peers)
    near = peers // depth
    raws = by_near(refs[:-2], depth)
    own = width // peers
    here = model // peers
    dps = lax.axis_size("dp")
    own_in = here // dps
    for m in range(near):
        for d in range(depth):
            j = me_ref[1] ^ (d * near + m)
            for k in range(dps):
                to = pl.multiple_of((k * peers + j) * own_in, own_in)
                wg_ref[pl.ds(to, own_in), :] = raws[m][d][k * own_in : (k + 1) * own_in, :]
            for c in range(model // width):
                to = pl.multiple_of(j * own, own)
                wo_ref[pl.ds(to, own), c * width : (c + 1) * width] = raws[m][d][
                    here + c * own : here + (c + 1) * own, :
                ]


def assemble(kernel, name, me, far, own, rest, shapes, scratch):
    raws = far + [part for both in zip(own, rest) for part in both]
    whole = pl.BlockSpec(memory_space=pltpu.VMEM)
    return pl.pallas_call(
        kernel,
        in_specs=[pl.BlockSpec(memory_space=pltpu.SMEM)] + [whole] * len(raws),
        out_specs=[whole] * len(shapes),
        out_shape=[jax.ShapeDtypeStruct(shape, dtype) for shape, dtype in shapes],
        scratch_shapes=scratch,
        compiler_params=params(24),
        cost_estimate=cost(2),
        name=name,
    )(me, *raws)


def lay_pieces(whole, refs, me):
    piece = refs[0].shape[1]
    for p, ref in enumerate(refs):
        whole[pl.ds(pl.multiple_of((me ^ p) * piece, piece), piece), :] = ref[0]


def deal_pieces(refs, part, me, block):
    piece = refs[0].shape[1]
    per = part.shape[0] // piece
    for p, ref in enumerate(refs):
        at = (me ^ p) - block * per

        @pl.when((at >= 0) & (at < per))
        def _(ref=ref, at=at):
            ref[0] = part[pl.ds(pl.multiple_of(at * piece, piece), piece), :].astype(ref.dtype)


def piece_shapes(dps, seqs, piece, model, wide):
    return [
        jax.ShapeDtypeStruct((seqs, piece, model), bf16 if p % wide else f32) for p in range(dps)
    ]


def piece_specs(dps, piece, model):
    return [pl.BlockSpec((1, piece, model), lambda s, b, me: (s, 0, 0))] * dps


def halve(mine_ref, other_ref, rows, me):
    low, high = rows[: WIDE // 2], rows[WIDE // 2 :]
    odd = me % 2 == 1
    mine_ref[...] = jnp.where(odd, high, low)
    other_ref[...] = jnp.where(odd, low, high)


def enter_kernel(me_ref, gain_ref, w_ref, chan_ref, wx_ref, *refs):
    tok_refs = refs[:-8]
    normed_ref, conv_ref, pre_ref, act_ref, xt_ref, other_ref, padded, whole = refs[-8:]
    block = pl.program_id(1)
    rows = conv_ref.shape[1]

    @pl.when(block == 0)
    def _():
        padded[0:8, :] = jnp.zeros((8, padded.shape[1]), f32)
        lay_pieces(whole, tok_refs, me_ref[0])

    @pl.when(block > 0)
    def _():
        padded[0:8, :] = padded[rows : rows + 8, :]

    x = whole[pl.ds(pl.multiple_of(block * rows, rows), rows), :].astype(f32)
    inv = lax.rsqrt(jnp.mean(x * x, axis=-1, keepdims=True) + 1e-05)
    normed = (x * inv * gain_ref[...]).astype(bf16)
    normed_ref[0] = normed
    conv = dot(normed, w_ref[...], 1, 0).astype(bf16)
    conv_ref[0] = conv
    padded[8 : rows + 8, :] = conv.astype(f32)
    pre = chan_ref[KW : KW + 1, :]
    for k in range(KW):
        pre = pre + chan_ref[k : k + 1, :] * padded[5 + k : 5 + k + rows, :]
    pre_ref[0] = pre
    act = (pre * jax.nn.sigmoid(pre)).astype(bf16)
    act_ref[0] = act
    halve(xt_ref, other_ref, dot(wx_ref[:, 0:WIDE], act, 0, 1), me_ref[0])


def enter(me, gain, w, chan, wx, tok):
    dps = len(tok)
    seqs, piece, model = tok[0].shape
    length = dps * piece
    width = w.shape[1]
    rows = min(BIG, length)
    blocks = length // rows

    def at(s, b, me):
        return (s, b, 0)

    def fixed(s, b, me):
        return (0, 0)

    return pl.pallas_call(
        enter_kernel,
        grid_spec=pltpu.PrefetchScalarGridSpec(
            num_scalar_prefetch=1,
            grid=(seqs, blocks),
            in_specs=[
                pl.BlockSpec((1, model), fixed),
                pl.BlockSpec((model, width), fixed),
                pl.BlockSpec((8, width), fixed),
                pl.BlockSpec((width, SMALL), fixed),
            ]
            + piece_specs(dps, piece, model),
            out_specs=[
                pl.BlockSpec((1, rows, model), at),
                pl.BlockSpec((1, rows, width), at),
                pl.BlockSpec((1, rows, width), at),
                pl.BlockSpec((1, rows, width), at),
                pl.BlockSpec((WIDE // 2, rows), lambda s, b, me: (0, s * blocks + b)),
                pl.BlockSpec((WIDE // 2, rows), lambda s, b, me: (0, s * blocks + b)),
            ],
            scratch_shapes=[pltpu.VMEM((rows + 8, width), f32), pltpu.VMEM((length, model), bf16)],
        ),
        out_shape=[
            jax.ShapeDtypeStruct((seqs, length, model), bf16),
            jax.ShapeDtypeStruct((seqs, length, width), bf16),
            jax.ShapeDtypeStruct((seqs, length, width), f32),
            jax.ShapeDtypeStruct((seqs, length, width), bf16),
            jax.ShapeDtypeStruct((WIDE // 2, seqs * length), f32),
            jax.ShapeDtypeStruct((WIDE // 2, seqs * length), f32),
        ],
        compiler_params=params(60),
        cost_estimate=cost(7),
        name="enter",
    )(me, gain, w, chan, wx, *tok)


def own_columns_of(rows):
    row = lax.broadcasted_iota(jnp.int32, (rows, T * N), 0)
    column = lax.broadcasted_iota(jnp.int32, (rows, T * N), 1)
    return column // N == row % T


def spread(block):
    row = lax.broadcasted_iota(jnp.int32, (N, T * N), 0)
    column = lax.broadcasted_iota(jnp.int32, (N, T * N), 1)
    tile = (column % N == row).astype(f32).astype(bf16)
    tiled = jnp.dot(block.astype(bf16), tile, preferred_element_type=f32)
    return jnp.where(own_columns_of(block.shape[0]), tiled, 0.0).astype(bf16)


def softplus(v):
    return jnp.maximum(v, 0.0) + jnp.log1p(jnp.exp(-jnp.abs(v)))


def forward_kernel(
    xt_ref, act_ref, dtw_ref, chan_ref, a_ref, gate_in_ref, h_ref, dt_ref, sp_ref, state, push
):
    @pl.when(pl.program_id(1) == 0)
    def _():
        state[...] = jnp.zeros_like(state)

    columns = xt_ref[...].astype(f32)
    rows_in = columns.T
    rank = rows_in[:, :R].astype(bf16)
    pre = dot(rank, dtw_ref[:, AT_DT : AT_DT + R], 1, 1) + chan_ref[KW + 1 : KW + 2, :]
    sp_ref[0] = pre
    steps = softplus(pre)
    dt_ref[0] = steps
    push[...] = steps * act_ref[0].astype(f32)
    scaled = a_ref[...] * LOG2E
    drive = columns[R : R + N]
    reads = spread(rows_in[:, R + N :])
    h = state[...]
    for k in range(ROWS // T):
        for j in range(T):
            t = k * T + j
            decay = jnp.exp2(dt_ref[0, t : t + 1, :] * scaled)
            h = decay * h + drive[:, t : t + 1] * push[t : t + 1, :]
            h_ref[0, t * N : (t + 1) * N, :] = h.astype(bf16)
        here = slice(k * T, (k + 1) * T)
        scanned = dot(reads[here], h_ref[0, k * T * N : (k + 1) * T * N, :], 1, 0)
        gate_in_ref[0, here, :] = scanned + chan_ref[KW + 2 : KW + 3, :] * act_ref[
            0, here, :
        ].astype(f32)
    state[...] = h


def scan_forward(xt, act, dtw, chan, a_matrix):
    seqs, length, width = act.shape
    blocks = length // ROWS

    def at(s, b):
        return (s, b, 0)

    def fixed(s, b):
        return (0, 0)

    return pl.pallas_call(
        forward_kernel,
        grid=(seqs, blocks),
        in_specs=[
            pl.BlockSpec((WIDE, ROWS), lambda s, b: (0, s * blocks + b)),
            pl.BlockSpec((1, ROWS, width), at),
            pl.BlockSpec((width, SMALL), fixed),
            pl.BlockSpec((8, width), fixed),
            pl.BlockSpec((N, width), fixed),
        ],
        out_specs=[
            pl.BlockSpec((1, ROWS, width), at),
            pl.BlockSpec((1, ROWS * N, width), at),
            pl.BlockSpec((1, ROWS, width), at),
            pl.BlockSpec((1, ROWS, width), at),
        ],
        out_shape=[
            jax.ShapeDtypeStruct((seqs, length, width), f32),
            jax.ShapeDtypeStruct((seqs, length * N, width), bf16),
            jax.ShapeDtypeStruct((seqs, length, width), f32),
            jax.ShapeDtypeStruct((seqs, length, width), f32),
        ],
        scratch_shapes=[pltpu.VMEM((N, width), f32), pltpu.VMEM((ROWS, width), f32)],
        compiler_params=params(60),
        cost_estimate=cost(18),
        name="scan_forward",
    )(xt, act, dtw, chan, a_matrix)


def middle_kernel(
    me_ref,
    gate_in_ref,
    act_ref,
    normed_ref,
    wg_ref,
    wo_ref,
    *refs,
):
    dps = lax.axis_size("dp")
    near = len(refs) - 2 * dps - 8
    cot_refs, part_refs = refs[:dps], refs[dps : 2 * dps]
    gout_refs = refs[2 * dps : 2 * dps + near]
    ggi_ref, ggp_ref, gin_ref, gskip_ref = refs[2 * dps + near : 2 * dps + near + 4]
    out_total, in_total, whole, part = refs[2 * dps + near + 4 :]
    block = pl.program_id(1)
    rows = act_ref.shape[1]
    start = (pl.program_id(0) == 0) & (block == 0)
    end = (pl.program_id(0) == pl.num_programs(0) - 1) & (block == pl.num_programs(1) - 1)

    @pl.when(start)
    def _():
        out_total[...] = jnp.zeros_like(out_total)
        in_total[...] = jnp.zeros_like(in_total)
        gskip_ref[...] = jnp.zeros_like(gskip_ref)

    @pl.when(block == 0)
    def _():
        lay_pieces(whole, cot_refs, me_ref[0])

    cot = whole[pl.ds(pl.multiple_of(block * rows, rows), rows), :]
    grad_gated = dot(cot, wo_ref[...], 1, 1)
    normed = normed_ref[0]
    gate = dot(normed, wg_ref[...], 1, 0).astype(bf16).astype(f32)
    sig = jax.nn.sigmoid(gate)
    gate_act = gate * sig
    gate_in = gate_in_ref[0]
    gated = (gate_in * gate_act).astype(bf16)
    ggi = grad_gated * gate_act
    ggi_ref[0] = ggi
    ggp = (grad_gated * gate_in * (sig * (1.0 + gate * (1.0 - sig)))).astype(bf16)
    ggp_ref[0] = ggp
    gskip_ref[...] += jnp.sum(ggi * act_ref[0].astype(f32), axis=0, keepdims=True)
    part[...] = dot(gated, wo_ref[...], 1, 0)
    deal_pieces(part_refs, part, me_ref[0], block)
    out_total[...] += dot(gated, cot, 0, 0)
    in_total[...] += dot(normed, ggp, 0, 0)

    @pl.when(end)
    def _():
        gin_ref[...] = in_total[...].astype(bf16)
        depth, own, _ = gout_refs[0].shape
        for j in range(near * depth):
            place = me_ref[1] ^ j
            for m, ref in enumerate(gout_refs):

                @pl.when(place % near == m)
                def _(ref=ref, place=place, j=j):
                    ref[place // near] = out_total[j * own : (j + 1) * own, :].astype(bf16)


def middle(me, gate_in, act, normed, wg, wo, cot, near, depth):
    dps = len(cot)
    seqs, piece, model = cot[0].shape
    length = dps * piece
    width = wo.shape[0]
    rows = min(BIG, length)
    blocks = length // rows
    own = width // (near * depth)

    def at(s, b, me):
        return (s, b, 0)

    def fixed(s, b, me):
        return (0, 0)

    return pl.pallas_call(
        middle_kernel,
        grid_spec=pltpu.PrefetchScalarGridSpec(
            num_scalar_prefetch=1,
            grid=(seqs, blocks),
            in_specs=[
                pl.BlockSpec((1, rows, width), at),
                pl.BlockSpec((1, rows, width), at),
                pl.BlockSpec((1, rows, model), at),
                pl.BlockSpec((model, width), fixed),
                pl.BlockSpec((width, model), fixed),
            ]
            + piece_specs(dps, piece, model),
            out_specs=piece_specs(dps, piece, model)
            + [pl.BlockSpec((depth, own, model), lambda s, b, me: (0, 0, 0))] * near
            + [
                pl.BlockSpec((1, rows, width), at),
                pl.BlockSpec((1, rows, width), at),
                pl.BlockSpec((model, width), fixed),
                pl.BlockSpec((1, width), fixed),
            ],
            scratch_shapes=[
                pltpu.VMEM((width, model), f32),
                pltpu.VMEM((model, width), f32),
                pltpu.VMEM((length, model), bf16),
                pltpu.VMEM((rows, model), f32),
            ],
        ),
        out_shape=piece_shapes(dps, seqs, piece, model, 2)
        + [jax.ShapeDtypeStruct((depth, own, model), bf16)] * near
        + [
            jax.ShapeDtypeStruct((seqs, length, width), f32),
            jax.ShapeDtypeStruct((seqs, length, width), bf16),
            jax.ShapeDtypeStruct((model, width), bf16),
            jax.ShapeDtypeStruct((1, width), f32),
        ],
        compiler_params=params(60),
        cost_estimate=cost(9),
        name="middle",
    )(me, gate_in, act, normed, wg, wo, *cot)


def backward_kernel(
    me_ref,
    xt_ref,
    act_ref,
    dt_ref,
    sp_ref,
    ggi_ref,
    chan_ref,
    a_ref,
    h_ref,
    before_ref,
    dtw_ref,
    *refs,
):
    gsp_ref, gact_ref, mine_ref, other_ref, galog_ref = refs[-10:-5]
    carried, total, g_buf, q_buf, gxt_ref = refs[-5:]
    first = pl.program_id(1) == pl.num_programs(1) - 1

    @pl.when(pl.program_id(1) == 0)
    def _():
        carried[...] = jnp.zeros_like(carried)

    @pl.when((pl.program_id(0) == 0) & (pl.program_id(1) == 0))
    def _():
        total[...] = jnp.zeros_like(total)

    columns = xt_ref[...].astype(f32)
    rows_in = columns.T
    a_now = a_ref[...]
    scaled = a_now * LOG2E
    read = columns[R + N :]
    ones = own_columns_of(T).astype(f32).astype(bf16)
    drives = spread(rows_in[:, R : R + N])
    ggi_low = ggi_ref[0].astype(bf16)
    push_low = (dt_ref[0] * act_ref[0].astype(f32)).astype(bf16)
    lanes = lax.broadcasted_iota(jnp.int32, (N, T), 1)
    p = carried[...]
    acc = total[...]
    for k in reversed(range(ROWS // T)):
        for j in reversed(range(T)):
            t = k * T + j
            step_row = dt_ref[0, t : t + 1, :]
            g = read[:, t : t + 1] * ggi_ref[0, t : t + 1, :] + p
            p = jnp.exp2(step_row * scaled) * g
            if t > 0:
                h_before = h_ref[0, (t - 1) * N : t * N, :].astype(f32)
            else:
                h_before = jnp.where(first, 0.0, before_ref[0].astype(f32))
            q = p * h_before
            acc = acc + q * step_row
            g_buf[t * N : (t + 1) * N, :] = g.astype(bf16)
            q_buf[t * N : (t + 1) * N, :] = (a_now * q).astype(bf16)
        here = slice(k * T, (k + 1) * T)
        states = slice(k * T * N, (k + 1) * T * N)
        pulled = dot(drives[here], g_buf[states, :], 1, 0)
        along = dot(ones, q_buf[states, :], 1, 0)
        act_now = act_ref[0, here, :].astype(f32)
        grad_steps = along + act_now * pulled
        gsp_ref[0, here, :] = (grad_steps * jax.nn.sigmoid(sp_ref[0, here, :])).astype(bf16)
        gact_ref[0, here, :] = (
            pulled * dt_ref[0, here, :] + chan_ref[KW + 2 : KW + 3, :] * ggi_ref[0, here, :]
        )
        both_d = dot(g_buf[states, :], push_low[here], 1, 1)
        both_r = dot(h_ref[0, states, :], ggi_low[here], 1, 1)
        gdrive = jnp.zeros((N, T), f32)
        gread = jnp.zeros((N, T), f32)
        for j in range(T):
            gdrive = jnp.where(lanes == j, both_d[j * N : (j + 1) * N], gdrive)
            gread = jnp.where(lanes == j, both_r[j * N : (j + 1) * N], gread)
        gxt_ref[R : R + N, here] = gdrive
        gxt_ref[R + N :, here] = gread
    carried[...] = p
    total[...] = acc
    gxt_ref[0:R, :] = dot(dtw_ref[:, AT_DT : AT_DT + R], gsp_ref[0], 0, 1)
    halve(mine_ref, other_ref, gxt_ref[...], me_ref[0])
    galog_ref[...] = acc * a_now


def scan_backward(me, xt, act, dt, sp, ggi, chan, a_matrix, states, dtw):
    seqs, length, width = act.shape
    blocks = length // ROWS

    def back(s, b):
        return (s, blocks - 1 - b, 0)

    def before(s, b):
        return (s, jnp.maximum((blocks - 1 - b) * ROWS - 1, 0), 0)

    def flat(s, b):
        return (0, s * blocks + blocks - 1 - b)

    def fixed(s, b):
        return (0, 0)

    return pl.pallas_call(
        backward_kernel,
        grid=(seqs, blocks),
        in_specs=[
            pl.BlockSpec(memory_space=pltpu.SMEM),
            pl.BlockSpec((WIDE, ROWS), flat),
            pl.BlockSpec((1, ROWS, width), back),
            pl.BlockSpec((1, ROWS, width), back),
            pl.BlockSpec((1, ROWS, width), back),
            pl.BlockSpec((1, ROWS, width), back),
            pl.BlockSpec((8, width), fixed),
            pl.BlockSpec((N, width), fixed),
            pl.BlockSpec((1, ROWS * N, width), back),
            pl.BlockSpec((1, N, width), before),
            pl.BlockSpec((width, SMALL), fixed),
        ],
        out_specs=[
            pl.BlockSpec((1, ROWS, width), back),
            pl.BlockSpec((1, ROWS, width), back),
            pl.BlockSpec((WIDE // 2, ROWS), flat),
            pl.BlockSpec((WIDE // 2, ROWS), flat),
            pl.BlockSpec((N, width), fixed),
        ],
        out_shape=[
            jax.ShapeDtypeStruct((seqs, length, width), bf16),
            jax.ShapeDtypeStruct((seqs, length, width), f32),
            jax.ShapeDtypeStruct((WIDE // 2, seqs * length), f32),
            jax.ShapeDtypeStruct((WIDE // 2, seqs * length), f32),
            jax.ShapeDtypeStruct((N, width), f32),
        ],
        scratch_shapes=[
            pltpu.VMEM((N, width), f32),
            pltpu.VMEM((N, width), f32),
            pltpu.VMEM((ROWS * N, width), bf16),
            pltpu.VMEM((ROWS * N, width), bf16),
            pltpu.VMEM((WIDE, ROWS), f32),
        ],
        compiler_params=params(60),
        cost_estimate=cost(28),
        name="scan_backward",
    )(me, xt, act, dt, sp, ggi, chan, a_matrix, states, states, dtw)


def leave_kernel(
    gact_ref,
    gxt_ref,
    xt_ref,
    gsp_ref,
    wx_ref,
    pre_ref,
    conv_ref,
    act_ref,
    normed_ref,
    chan_ref,
    gskip_ref,
    *refs,
):
    galog_refs = refs[:-6]
    gci_ref, gin_ref, small_ref, padded, in_total, sums = refs[-6:]
    block = pl.program_id(1)
    rows = gact_ref.shape[1]
    start = (pl.program_id(0) == 0) & (block == 0)
    end = (pl.program_id(0) == pl.num_programs(0) - 1) & (block == pl.num_programs(1) - 1)

    @pl.when(start)
    def _():
        in_total[...] = jnp.zeros_like(in_total)
        small_ref[...] = jnp.zeros_like(small_ref)
        sums[...] = jnp.zeros_like(sums)

    @pl.when(block == 0)
    def _():
        padded[rows : rows + 8, :] = jnp.zeros((8, padded.shape[1]), f32)

    @pl.when(block > 0)
    def _():
        padded[rows : rows + 8, :] = padded[0:8, :]

    gxt = gxt_ref[...]
    act = act_ref[0]
    grad_act = gact_ref[0] + dot(gxt, wx_ref[:, 0:WIDE], 0, 1)
    pre = pre_ref[0]
    sig = jax.nn.sigmoid(pre)
    grad_conv = grad_act * (sig * (1.0 + pre * (1.0 - sig)))
    padded[0:rows, :] = grad_conv
    conv = conv_ref[0].astype(f32)
    gci = jnp.zeros_like(grad_conv)
    for k in range(KW):
        moved = padded[KW - 1 - k : KW - 1 - k + rows, :]
        gci = gci + chan_ref[k : k + 1, :] * moved
        sums[N + k : N + k + 1, :] += jnp.sum(conv * moved, axis=0, keepdims=True)
    sums[N + KW : N + KW + 1, :] += jnp.sum(grad_conv, axis=0, keepdims=True)
    gsp = gsp_ref[0]
    sums[N + KW + 1 : N + KW + 2, :] += jnp.sum(gsp.astype(f32), axis=0, keepdims=True)
    low = gci.astype(bf16)
    gci_ref[0] = low
    in_total[...] += dot(normed_ref[0], low, 0, 0)
    small_ref[:, 0:WIDE] += dot(act, gxt, 0, 1)
    small_ref[:, WIDE : WIDE + R] += dot(gsp, xt_ref[0:R, :], 0, 1)

    @pl.when(end)
    def _():
        gin_ref[...] = in_total[...].astype(bf16)
        sums[0:N, :] = sum(ref[...] for ref in galog_refs)
        sums[N + KW + 2 : N + KW + 3, :] = gskip_ref[...]
        small_ref[:, WIDE + R :] = sums[...].T


def leave(gact, gxt, xt, gsp, wx, pre, conv, act, normed, chan, gskip, galog):
    seqs, length, width = act.shape
    model = normed.shape[2]
    rows = min(BIG, length)
    blocks = length // rows

    def back(s, b):
        return (s, blocks - 1 - b, 0)

    def flat(s, b):
        return (0, s * blocks + blocks - 1 - b)

    def fixed(s, b):
        return (0, 0)

    return pl.pallas_call(
        leave_kernel,
        grid=(seqs, blocks),
        in_specs=[
            pl.BlockSpec((1, rows, width), back),
            pl.BlockSpec((WIDE, rows), flat),
            pl.BlockSpec((WIDE, rows), flat),
            pl.BlockSpec((1, rows, width), back),
            pl.BlockSpec((width, SMALL), fixed),
            pl.BlockSpec((1, rows, width), back),
            pl.BlockSpec((1, rows, width), back),
            pl.BlockSpec((1, rows, width), back),
            pl.BlockSpec((1, rows, model), back),
            pl.BlockSpec((8, width), fixed),
            pl.BlockSpec((1, width), fixed),
        ]
        + [pl.BlockSpec((N, width), fixed)] * len(galog),
        out_specs=[
            pl.BlockSpec((1, rows, width), back),
            pl.BlockSpec((model, width), fixed),
            pl.BlockSpec((width, GRADS), fixed),
        ],
        out_shape=[
            jax.ShapeDtypeStruct((seqs, length, width), bf16),
            jax.ShapeDtypeStruct((model, width), bf16),
            jax.ShapeDtypeStruct((width, GRADS), f32),
        ],
        scratch_shapes=[
            pltpu.VMEM((rows + 8, width), f32),
            pltpu.VMEM((model, width), f32),
            pltpu.VMEM((REST, width), f32),
        ],
        compiler_params=params(60),
        cost_estimate=cost(8),
        name="leave",
    )(gact, gxt, xt, gsp, wx, pre, conv, act, normed, chan, gskip, *galog)


def rows_back_kernel(me_ref, gci_ref, ggp_ref, w0_ref, w1_ref, *refs):
    part = refs[-1]
    part[...] = dot(gci_ref[0], w0_ref[...], 1, 1) + dot(ggp_ref[0], w1_ref[...], 1, 1)
    deal_pieces(refs[:-1], part, me_ref[0], pl.program_id(1))


def rows_back(me, gci, ggp, w0, w1, dps):
    seqs, length, width = gci.shape
    model = w0.shape[0]
    piece = length // dps
    rows = min(BIG, length)
    blocks = length // rows

    def at(s, b, me):
        return (s, b, 0)

    def fixed(s, b, me):
        return (0, 0)

    return pl.pallas_call(
        rows_back_kernel,
        grid_spec=pltpu.PrefetchScalarGridSpec(
            num_scalar_prefetch=1,
            grid=(seqs, blocks),
            in_specs=[
                pl.BlockSpec((1, rows, width), at),
                pl.BlockSpec((1, rows, width), at),
                pl.BlockSpec((model, width), fixed),
                pl.BlockSpec((model, width), fixed),
            ],
            out_specs=piece_specs(dps, piece, model),
            scratch_shapes=[pltpu.VMEM((rows, model), f32)],
        ),
        out_shape=piece_shapes(dps, seqs, piece, model, 2),
        compiler_params=params(60),
        cost_estimate=cost(5),
        name="rows_back",
    )(me, gci, ggp, w0, w1)


def finish_kernel(tok_ref, cot_ref, gain_ref, *refs):
    out_ref = refs[-1]
    grad = refs[0][0]
    for ref in refs[1:-1]:
        grad = grad + ref[0].astype(f32)
    x = tok_ref[0].astype(f32)
    inv = lax.rsqrt(jnp.mean(x * x, axis=-1, keepdims=True) + 1e-05)
    grad = grad * gain_ref[...]
    back = x * inv * inv * inv * jnp.mean(grad * x, axis=-1, keepdims=True)
    out_ref[0] = inv * grad - back + cot_ref[0].astype(f32)


def finish(tok, cot, gain, parts):
    seqs, piece, model = tok.shape
    rows = pl.BlockSpec((1, piece, model), lambda s: (s, 0, 0))
    return pl.pallas_call(
        finish_kernel,
        grid=(seqs,),
        in_specs=[rows, rows, pl.BlockSpec((1, model), lambda s: (0, 0))] + [rows] * len(parts),
        out_specs=rows,
        out_shape=jax.ShapeDtypeStruct(tok.shape, f32),
        compiler_params=params(60),
        cost_estimate=cost(3),
        name="finish",
    )(tok, cot, gain, *parts)


def collect_kernel(
    conv_ref, gate_ref, out_ref, small_ref, w_ref, gain_ref, gin_ref, gx_ref, gdt_ref, gchan_ref, galog_ref, ggain_ref, squares_ref, square
):
    own_in, columns = w_ref.shape
    width = conv_ref.shape[2]
    dps = columns // (2 * width)
    peers = conv_ref.shape[0] // dps
    own = small_ref.shape[0]
    total = jnp.zeros((1, 128), f32)

    def squares(x):
        x = jnp.sum(x * x, axis=0, keepdims=True)
        return jnp.sum(x, axis=1, keepdims=True)

    ggain = jnp.zeros((own_in, 1), f32)
    for half in range(2):
        for k in range(dps):
            parts = gate_ref if half else conv_ref
            grad = parts[k * peers].astype(f32)
            for j in range(1, peers):
                grad = grad + parts[k * peers + j].astype(f32)
            here = slice((half * dps + k) * width, (half * dps + k + 1) * width)
            gin_ref[:, here] = grad
            total = total + squares(grad)
            low = w_ref[:, here].astype(bf16).astype(f32)
            ggain = ggain + jnp.sum(grad * low, axis=1, keepdims=True)
    total = total + squares(out_ref[...])
    small = small_ref[...]
    total = total + squares(small)
    gx_ref[...] = small[:, :WIDE]
    square[...] = jnp.zeros_like(square)
    square[0:own, 0:GRADS] = small
    square[0:own_in, GRADS : GRADS + 1] = ggain
    turned = square[...].T
    gdt_ref[...] = turned[WIDE : WIDE + R, :own]
    galog_ref[...] = turned[WIDE + R : WIDE + R + N, :own]
    gchan_ref[...] = turned[WIDE + R + N : WIDE + R + N + KW + 3, :own]
    grad = turned[GRADS : GRADS + 1, :own_in] / gain_ref[...].astype(bf16).astype(f32)
    ggain_ref[...] = grad
    squares_ref[...] = jnp.broadcast_to((total + squares(grad))[None], squares_ref.shape)


def collect(conv, gate, out, small, w, gain):
    own_in, columns = w.shape
    own = small.shape[0]
    shapes = [
        (own_in, columns),
        (own, WIDE),
        (R, own),
        (KW + 3, own),
        (N, own),
        (1, own_in),
        (conv.shape[0], 1, 128),
    ]
    whole = pl.BlockSpec(memory_space=pltpu.VMEM)
    return pl.pallas_call(
        collect_kernel,
        in_specs=[whole] * 6,
        out_specs=[whole] * len(shapes),
        out_shape=[jax.ShapeDtypeStruct(shape, f32) for shape in shapes],
        scratch_shapes=[pltpu.VMEM((128, 256), f32)],
        compiler_params=params(16),
        cost_estimate=cost(3),
        name="collect",
    )(conv, gate, out, small, w, gain)


def adam_kernel(squares_ref, *refs):
    count = len(learn_rates)
    weights, moments, grads = refs[:count], refs[count : 2 * count], refs[2 * count : 3 * count]
    outs = refs[3 * count :]
    norm = jnp.sqrt(jnp.sum(squares_ref[...], axis=0)[:, 0:1])
    outs[2 * count][...] = norm
    factor = jnp.minimum(1.0, clip_limit / (norm + 1e-06))
    for place in range(count):
        rate = learn_rates[place]
        gradient = grads[place][...] * factor
        weight = weights[place][...]
        rows_first = len(moments[place].shape) == 3 and moments[place].shape[1] == 2
        at = (lambda k: (slice(None), k)) if rows_first else (lambda k: k)
        first = 0.9 * moments[place][at(0)] + 0.1 * gradient
        old = moments[place][at(1)]
        root = jnp.sqrt(0.95 * old * old + 0.05 * gradient * gradient)
        update = first / (1.0 - 0.9**STEP) / (root / (1.0 - 0.95**STEP) ** 0.5 + 1e-08)
        outs[2 * place][at(0)] = first
        outs[2 * place][at(1)] = root
        outs[2 * place + 1][...] = weight - rate * (update + 0.01 * weight)


def adam(squares, weights, moments, grads):
    shapes = []
    for weight, moment in zip(weights, moments):
        shapes.append(jax.ShapeDtypeStruct(moment.shape, f32))
        shapes.append(jax.ShapeDtypeStruct(weight.shape, f32))
    shapes.append(jax.ShapeDtypeStruct((1, 1), f32))
    whole = pl.BlockSpec(memory_space=pltpu.VMEM)
    return pl.pallas_call(
        adam_kernel,
        in_specs=[whole] * (1 + 3 * len(weights)),
        out_specs=[whole] * len(shapes),
        out_shape=shapes,
        compiler_params=params(16),
        cost_estimate=cost(4),
        name="adam",
    )(squares, *weights, *moments, *grads)


def shards(
    tokens,
    cotangent,
    in_weight,
    out_weight,
    xproj_weight,
    dtproj_weight,
    chan_params,
    a_log,
    norm_gain,
    in_moments,
    out_moments,
    xproj_moments,
    dtproj_moments,
    chan_moments,
    alog_moments,
    gain_moments,
):
    both = ("dp", "fsdp")
    dps = lax.axis_size("dp")
    fsdps = lax.axis_size("fsdp")
    depth = min(4, fsdps)
    near = fsdps // depth
    me = jnp.stack([lax.axis_index("dp"), lax.axis_index("fsdp")])
    batches, groups, piece, model = tokens.shape
    seqs = batches * groups
    length = piece * dps
    own_in = in_weight.shape[0]
    own = out_weight.shape[0]
    width = own * fsdps

    in_low = in_weight.astype(bf16).reshape(own_in, 2, dps, width).transpose(2, 1, 0, 3)
    gain_row = jnp.pad(norm_gain.astype(bf16)[None], ((0, 7), (0, width - own_in)))
    in_parts = jnp.concatenate(
        [in_low[:, 0], in_low[:, 1], jnp.broadcast_to(gain_row, (dps, 8, width))], axis=1
    )
    in_parts = lax.all_to_all(in_parts, "dp", 0, 0, tiled=True)
    small = jnp.concatenate(
        [
            xproj_weight.astype(bf16),
            jnp.zeros((own, AT_DT - WIDE), bf16),
            dtproj_weight.astype(bf16).T,
            a_log.astype(bf16).T,
            chan_params.astype(bf16).T,
            jnp.zeros((own, SMALL - AT_REST - N - KW - 3), bf16),
        ],
        axis=1,
    )
    fold = max(width // SMALL, 1)
    aligned = own_in % 16 == 0 and own % (16 * fold) == 0 and width % SMALL == 0
    if aligned:
        packed = jnp.concatenate(jnp.split(small, fold), axis=1)
    else:
        packed = small.reshape(-1, width)
    here = dps * own_in
    gain_rows = jnp.pad(in_parts[:, 2 * own_in], ((0, -dps % 16), (0, 0)))
    first = jnp.concatenate([in_parts[:, :own_in].reshape(here, width), gain_rows, packed])
    out_low = out_weight.astype(bf16).reshape(own, model // width, width).transpose(1, 0, 2)
    second = [
        in_parts[:, own_in : 2 * own_in].reshape(here, width),
        out_low.reshape(-1, width),
    ]
    second = jnp.concatenate(second)
    tok = parts_dp_far(tokens.reshape(seqs, piece, model))
    first_own = swap_near(first)
    second_own = swap_near(second)
    first, tok, first_own, second_own = lax.optimization_barrier(
        (gather_far(first), tok, first_own, second_own)
    )
    cot = parts_dp_far(after(cotangent.reshape(seqs, piece, model), first))
    tok = parts_dp_near(tok)
    first_rest = swap_near(jnp.stack(first[1:]))
    first, first_rest, cot = lax.optimization_barrier((first, first_rest, cot))

    def own_columns(parts):
        parts = parts.reshape(fsdps, dps, own_in, width)
        return parts.transpose(1, 0, 2, 3).reshape(model, width)

    if aligned:
        w_conv, small, gain, a_matrix, chan = assemble(
            assemble_first_kernel,
            "assemble_first",
            me,
            first,
            first_own,
            first_rest,
            [
                ((model, width), bf16),
                ((width, SMALL), bf16),
                ((1, model), f32),
                ((N, width), f32),
                ((8, width), f32),
            ],
            [pltpu.VMEM((model // own_in, 128), f32)],
        )
    else:
        merged = merge_near(first, first_own, first_rest)
        w_conv = own_columns(merged[:, :here])
        gain = merged[:, here : here + dps, :own_in].transpose(1, 0, 2)
        gain = gain.reshape(1, model).astype(f32)
        small = merged[:, here + dps + -dps % 16 :].reshape(width, SMALL)
        rest = small[:, AT_REST : AT_REST + REST].astype(f32).T
        a_matrix = -jnp.exp(rest[:N])
        chan = rest[N : N + 8]

    far = gather_far(second)
    normed, conv, pre, act, *xt = enter(me, gain, w_conv, chan, small, tok)
    cot = parts_dp_near(cot)
    xt, far = lax.optimization_barrier((xt, far))
    xt = sum_dp_near(*xt)
    second_rest = swap_near(jnp.stack(after(far[1:], xt)))
    xt = sum_dp_far(xt, f32)
    if aligned:
        w_gate, w_out = assemble(
            assemble_second_kernel,
            "assemble_second",
            me,
            far,
            second_own,
            second_rest,
            [((model, width), bf16), ((width, model), bf16)],
            [],
        )
    else:
        merged = merge_near(far, second_own, second_rest)
        w_gate = own_columns(merged[:, :here])
        w_out = merged[:, here:].reshape(fsdps, model // width, own, width)
        w_out = w_out.transpose(0, 2, 1, 3).reshape(width, model)
    gate_in, states, dt, step_pre = scan_forward(xt, act, small, chan, a_matrix)
    outs = middle(me, gate_in, act, normed, w_gate, w_out, cot, near, depth)
    part, gout = outs[:dps], outs[dps : dps + near]
    ggi, ggp, gin_gate, gskip = outs[dps + near :]
    gate_parts = lax.all_to_all(gin_gate.reshape(-1, own_in, width), both, 0, 0, tiled=True)
    gout_near = reduce_near(gout)
    out_mine, out_parts = send_dp_near(part)

    gsp, gact, *gxt, galog = scan_backward(
        me, xt, act, dt, step_pre, ggi, chan, a_matrix, states, small
    )
    gxt, out_mine, gout_near = lax.optimization_barrier((gxt, out_mine, gout_near))
    gxt = sum_dp_near(*gxt)
    gout_far = send_far(list(after(gout_near, gxt)))
    out_rows = send_dp_far(list(out_mine), list(after(out_parts, gxt)))
    gxt = sum_dp_far(gxt, bf16)
    gxt, gate_parts = lax.optimization_barrier((gxt, gate_parts))
    gci, gin_conv, small_grad = leave(
        gact, gxt, xt, gsp, small, pre, conv, act, normed, chan, gskip, [galog]
    )
    gin_conv, gout_far, out_rows = lax.optimization_barrier((gin_conv, gout_far, out_rows))
    conv_parts = lax.all_to_all(gin_conv.reshape(-1, own_in, width), both, 0, 0, tiled=True)
    grad_out = sum(part.astype(f32) for part in gout_far)
    small_near = reduce_near(split_near(small_grad.reshape(fsdps, own, GRADS)))
    part_back = rows_back(me, gci, ggp, w_conv, w_gate, dps)
    back_mine, back_parts = send_dp_near(part_back)
    small_near, back_parts = lax.optimization_barrier((small_near, back_parts))
    own_small = sum(part.astype(f32) for part in send_far(list(small_near)))
    part_back = send_dp_far(back_mine, list(back_parts))
    out_rows = sum(part.astype(f32) for part in out_rows).reshape(tokens.shape)
    block_output = (tokens.astype(f32) + out_rows).astype(bf16)

    def flat2(x):
        return x.reshape(x.shape[:-1] + (1, x.shape[-1]))

    grad_in, grad_x, grad_dt, grad_chan, grad_alog, grad_gain, squares = collect(
        conv_parts, gate_parts, grad_out, own_small, in_weight, flat2(norm_gain)
    )
    grad_normed = sum(part.astype(f32) for part in after(part_back, squares)).reshape(tokens.shape)

    input_grad = finish(
        tokens.reshape(seqs, piece, model),
        cotangent.reshape(seqs, piece, model),
        gain,
        after(part_back, squares),
    ).reshape(tokens.shape)
    squares = lax.all_to_all(squares, both, 0, 0, tiled=True)
    weights = (in_weight, out_weight, xproj_weight, dtproj_weight, chan_params, a_log, flat2(norm_gain))
    moments = (
        in_moments,
        out_moments,
        xproj_moments,
        dtproj_moments,
        chan_moments.transpose(1, 0, 2),
        alog_moments,
        flat2(gain_moments),
    )
    grads = (grad_in, grad_out, grad_x, grad_dt, grad_chan, grad_alog, grad_gain)
    updated = list(adam(squares, weights, moments, grads))
    grad_norm = updated.pop().reshape(())
    updated[8] = updated[8].transpose(1, 0, 2)
    updated[-2] = updated[-2].reshape(gain_moments.shape)
    updated[-1] = updated[-1].reshape(norm_gain.shape)
    return (block_output, input_grad, grad_norm) + tuple(updated)


def solution(mesh):
    both = ("dp", "fsdp")
    row_specs = (P(None, "fsdp", "dp", None),) * 2
    weight_specs = (
        P(both, None),
        P(both, None),
        P(both, None),
        P(None, both),
        P(None, both),
        P(None, both),
        P(both),
    )
    moment_specs = (
        P(None, both, None),
        P(None, both, None),
        P(None, both, None),
        P(None, None, both),
        P(None, None, both),
        P(None, None, both),
        P(None, both),
    )
    updated = tuple(spec for pair in zip(moment_specs, weight_specs) for spec in pair)
    return jax.shard_map(
        shards,
        mesh=mesh,
        in_specs=row_specs + weight_specs + moment_specs,
        out_specs=row_specs + (P(),) + updated,
        check_vma=False,
    )
```

```python
import jax
import jax.numpy as jnp
from jax import lax
from jax.experimental import pallas as pl
from jax.experimental.pallas import tpu as pltpu
from jax.sharding import PartitionSpec as P

N = 16
R = 64
KW = 4
STEP = 7
ROWS = 128
T = 16
WIDE = R + 2 * N
REST = 32
GRADS = WIDE + R + REST
AT_DT = 128
AT_REST = 192
SMALL = 256
BIG = 512

bf16 = jnp.bfloat16
f32 = jnp.float32
LOG2E = 1.4426950408889634
clip_limit = 1.0
learn_rates = (0.03, 0.03, 0.03, 0.15, 0.3, 1.0, 0.3)


def dot(left, right, on_left, on_right):
    return lax.dot_general(
        left, right, (((on_left,), (on_right,)), ((), ())), preferred_element_type=f32
    )


def params(mib):
    return pltpu.CompilerParams(vmem_limit_bytes=mib * 1024 * 1024)


def cost(us):
    return pl.CostEstimate(flops=int(us * 8e7), bytes_accessed=int(us * 3e5), transcendentals=0)


def swap(x, axis, mask):
    peers = lax.axis_size(axis)
    return lax.ppermute(x, axis, [(i, i ^ mask) for i in range(peers)])


def after(x, *others):
    return lax.optimization_barrier((x,) + others)[0]


def masks(axis):
    peers = lax.axis_size(axis)
    return [1 << k for k in range(peers.bit_length() - 1)]


def in_order(parts, axis):
    peers = lax.axis_size(axis)
    for mask in masks(axis):
        pairs = parts.reshape((peers // (2 * mask), 2, mask) + parts.shape[1:])
        high = (lax.axis_index(axis) & mask) != 0
        parts = jnp.where(high, pairs[:, ::-1], pairs).reshape(parts.shape)
    return parts


def parts_dp_far(x):
    held = [x]
    for mask in masks("dp")[:0:-1]:
        held = [part for p in held for part in (p, swap(p, "dp", mask))]
    return held


def parts_dp_near(held):
    return [part for p in held for part in (p, swap(p, "dp", 1))]


def gather_far(x):
    peers = lax.axis_size("fsdp")
    depth = min(4, peers)
    return [x] + [swap(x, "fsdp", m * (peers // depth)) for m in range(1, depth)]


def swap_near(x):
    near = lax.axis_size("fsdp") // min(4, lax.axis_size("fsdp"))
    return [swap(x, "fsdp", m) for m in range(1, near)]


def merge_near(far, own, rest):
    nears = [far] + [[one] + list(stack) for one, stack in zip(own, rest)]
    parts = jnp.stack([part for both in zip(*nears) for part in both])
    return in_order(parts, "fsdp")


def send_dp_near(parts):
    moved = [swap(part, "dp", 1) for part in parts[1::2]]
    sums = [kept + part.astype(f32) for kept, part in zip(parts[2::2], moved[1:])]
    return [parts[0], moved[0]], [part.astype(bf16) for part in sums]


def send_dp_far(mine, parts):
    for mask in masks("dp")[1:]:
        moved = [swap(part, "dp", mask) for part in parts[0::2]]
        mine = mine + [moved[0]]
        parts = [
            (kept.astype(f32) + part.astype(f32)).astype(bf16)
            for kept, part in zip(parts[1::2], moved[1:])
        ]
    return mine


def sum_dp_near(mine, other):
    return mine + swap(other, "dp", 1)


def sum_dp_far(mine, sent):
    high = (lax.axis_index("dp") & 1) != 0
    for mask in masks("dp")[1:]:
        mine = mine + swap(mine.astype(sent), "dp", mask).astype(f32)
    mine = mine.astype(bf16)
    other = swap(mine, "dp", 1)
    both = jnp.where(high, jnp.stack([other, mine]), jnp.stack([mine, other]))
    return both.reshape((-1,) + mine.shape[1:])


def reduce_near(parts):
    mine = parts[0].astype(f32)
    for m in range(1, len(parts)):
        mine = mine + swap(parts[m].astype(bf16), "fsdp", m).astype(f32)
    return [mine[0]] + [mine[d].astype(bf16) for d in range(1, mine.shape[0])]


def split_near(x):
    peers = lax.axis_size("fsdp")
    depth = min(4, peers)
    x = in_order(x, "fsdp").reshape((depth, peers // depth) + x.shape[1:])
    return [x[:, m] for m in range(x.shape[1])]


def send_far(mine):
    near = lax.axis_size("fsdp") // len(mine)
    return mine[:1] + [swap(mine[m], "fsdp", m * near) for m in range(1, len(mine))]


def by_near(refs, depth):
    parts = []
    for ref in refs:
        parts += [ref] if len(ref.shape) == 2 else [ref.at[d] for d in range(ref.shape[0])]
    return [parts[k : k + depth] for k in range(0, len(parts), depth)]


def assemble_first_kernel(me_ref, *refs):
    w_ref, small_ref, gain_ref, a_ref, chan_ref, gains = refs[-6:]
    model, width = w_ref.shape
    peers = lax.axis_size("fsdp")
    depth = min(4, peers)
    near = peers // depth
    raws = by_near(refs[:-6], depth)
    own = width // peers
    fold = width // SMALL
    here = model // peers
    own_in = model // gains.shape[0]
    dps = here // own_in
    stretch = own // fold
    at_small = here + dps + -dps % 16
    for m in range(near):
        for d in range(depth):
            j = me_ref[1] ^ (d * near + m)
            for k in range(dps):
                to = pl.multiple_of((k * peers + j) * own_in, own_in)
                w_ref[pl.ds(to, own_in), :] = raws[m][d][k * own_in : (k + 1) * own_in, :]
                row = raws[m][d][here : here + 16, 0:128].astype(f32)[k : k + 1]
                gains[pl.ds(k * peers + j, 1), :] = row
            for f in range(fold):
                to = pl.multiple_of(j * own + f * stretch, stretch)
                small_ref[pl.ds(to, stretch), :] = raws[m][d][
                    at_small : at_small + stretch, f * SMALL : (f + 1) * SMALL
                ]
    row = lax.broadcasted_iota(jnp.int32, (own_in, model), 0)
    column = lax.broadcasted_iota(jnp.int32, (own_in, model), 1)
    tile = (column % own_in == row).astype(f32).astype(bf16)
    tiled = dot(gains[:, 0:own_in].astype(bf16), tile, 1, 0)
    row = lax.broadcasted_iota(jnp.int32, tiled.shape, 0)
    column = lax.broadcasted_iota(jnp.int32, tiled.shape, 1)
    gain_ref[...] = jnp.sum(jnp.where(column // own_in == row, tiled, 0.0), axis=0, keepdims=True)
    turned = small_ref[...].astype(f32).T
    a_ref[...] = -jnp.exp(turned[AT_REST : AT_REST + N])
    chan_ref[...] = turned[AT_REST + N : AT_REST + N + 8]


def assemble_second_kernel(me_ref, *refs):
    wg_ref, wo_ref = refs[-2:]
    model, width = wg_ref.shape
    peers = lax.axis_size("fsdp")
    depth = min(4, peers)
    near = peers // depth
    raws = by_near(refs[:-2], depth)
    own = width // peers
    here = model // peers
    dps = lax.axis_size("dp")
    own_in = here // dps
    for m in range(near):
        for d in range(depth):
            j = me_ref[1] ^ (d * near + m)
            for k in range(dps):
                to = pl.multiple_of((k * peers + j) * own_in, own_in)
                wg_ref[pl.ds(to, own_in), :] = raws[m][d][k * own_in : (k + 1) * own_in, :]
            for c in range(model // width):
                to = pl.multiple_of(j * own, own)
                wo_ref[pl.ds(to, own), c * width : (c + 1) * width] = raws[m][d][
                    here + c * own : here + (c + 1) * own, :
                ]


def assemble(kernel, name, me, far, own, rest, shapes, scratch, mib):
    raws = far + [part for both in zip(own, rest) for part in both]
    whole = pl.BlockSpec(memory_space=pltpu.VMEM)
    return pl.pallas_call(
        kernel,
        in_specs=[pl.BlockSpec(memory_space=pltpu.SMEM)] + [whole] * len(raws),
        out_specs=[whole] * len(shapes),
        out_shape=[jax.ShapeDtypeStruct(shape, dtype) for shape, dtype in shapes],
        scratch_shapes=scratch,
        compiler_params=params(mib),
        cost_estimate=cost(2),
        name=name,
    )(me, *raws)


def lay_pieces(whole, refs, me):
    piece = refs[0].shape[1]
    for p, ref in enumerate(refs):
        whole[pl.ds(pl.multiple_of((me ^ p) * piece, piece), piece), :] = ref[0]


def deal_pieces(refs, part, me, block):
    piece = refs[0].shape[1]
    per = part.shape[0] // piece
    for p, ref in enumerate(refs):
        at = (me ^ p) - block * per

        @pl.when((at >= 0) & (at < per))
        def _(ref=ref, at=at):
            ref[0] = part[pl.ds(pl.multiple_of(at * piece, piece), piece), :].astype(ref.dtype)


def piece_shapes(dps, seqs, piece, model, wide):
    return [
        jax.ShapeDtypeStruct((seqs, piece, model), bf16 if p % wide else f32) for p in range(dps)
    ]


def piece_specs(dps, piece, model):
    return [pl.BlockSpec((1, piece, model), lambda s, b, me: (s, 0, 0))] * dps


def halve(mine_ref, other_ref, rows, me):
    low, high = rows[: WIDE // 2], rows[WIDE // 2 :]
    odd = me % 2 == 1
    mine_ref[...] = jnp.where(odd, high, low)
    other_ref[...] = jnp.where(odd, low, high)


def enter_kernel(me_ref, gain_ref, w_ref, chan_ref, wx_ref, *refs):
    tok_refs = refs[:-8]
    normed_ref, conv_ref, pre_ref, act_ref, xt_ref, other_ref, padded, whole = refs[-8:]
    block = pl.program_id(1)
    rows = conv_ref.shape[1]

    @pl.when(block == 0)
    def _():
        padded[0:8, :] = jnp.zeros((8, padded.shape[1]), f32)
        lay_pieces(whole, tok_refs, me_ref[0])

    @pl.when(block > 0)
    def _():
        padded[0:8, :] = padded[rows : rows + 8, :]

    x = whole[pl.ds(pl.multiple_of(block * rows, rows), rows), :].astype(f32)
    inv = lax.rsqrt(jnp.mean(x * x, axis=-1, keepdims=True) + 1e-05)
    normed = (x * inv * gain_ref[...]).astype(bf16)
    normed_ref[0] = normed
    conv = dot(normed, w_ref[...], 1, 0).astype(bf16)
    conv_ref[0] = conv
    padded[8 : rows + 8, :] = conv.astype(f32)
    pre = chan_ref[KW : KW + 1, :]
    for k in range(KW):
        pre = pre + chan_ref[k : k + 1, :] * padded[5 + k : 5 + k + rows, :]
    pre_ref[0] = pre
    act = (pre * jax.nn.sigmoid(pre)).astype(bf16)
    act_ref[0] = act
    halve(xt_ref, other_ref, dot(wx_ref[:, 0:WIDE], act, 0, 1), me_ref[0])


def enter(me, gain, w, chan, wx, tok):
    dps = len(tok)
    seqs, piece, model = tok[0].shape
    length = dps * piece
    width = w.shape[1]
    rows = min(BIG, length)
    blocks = length // rows

    def at(s, b, me):
        return (s, b, 0)

    def fixed(s, b, me):
        return (0, 0)

    return pl.pallas_call(
        enter_kernel,
        grid_spec=pltpu.PrefetchScalarGridSpec(
            num_scalar_prefetch=1,
            grid=(seqs, blocks),
            in_specs=[
                pl.BlockSpec((1, model), fixed),
                pl.BlockSpec((model, width), fixed),
                pl.BlockSpec((8, width), fixed),
                pl.BlockSpec((width, SMALL), fixed),
            ]
            + piece_specs(dps, piece, model),
            out_specs=[
                pl.BlockSpec((1, rows, model), at),
                pl.BlockSpec((1, rows, width), at),
                pl.BlockSpec((1, rows, width), at),
                pl.BlockSpec((1, rows, width), at),
                pl.BlockSpec((WIDE // 2, rows), lambda s, b, me: (0, s * blocks + b)),
                pl.BlockSpec((WIDE // 2, rows), lambda s, b, me: (0, s * blocks + b)),
            ],
            scratch_shapes=[pltpu.VMEM((rows + 8, width), f32), pltpu.VMEM((length, model), bf16)],
        ),
        out_shape=[
            jax.ShapeDtypeStruct((seqs, length, model), bf16),
            jax.ShapeDtypeStruct((seqs, length, width), bf16),
            jax.ShapeDtypeStruct((seqs, length, width), f32),
            jax.ShapeDtypeStruct((seqs, length, width), bf16),
            jax.ShapeDtypeStruct((WIDE // 2, seqs * length), f32),
            jax.ShapeDtypeStruct((WIDE // 2, seqs * length), f32),
        ],
        compiler_params=params(60),
        cost_estimate=cost(7),
        name="enter",
    )(me, gain, w, chan, wx, *tok)


def own_columns_of(rows):
    row = lax.broadcasted_iota(jnp.int32, (rows, T * N), 0)
    column = lax.broadcasted_iota(jnp.int32, (rows, T * N), 1)
    return column // N == row % T


def spread(block):
    row = lax.broadcasted_iota(jnp.int32, (N, T * N), 0)
    column = lax.broadcasted_iota(jnp.int32, (N, T * N), 1)
    tile = (column % N == row).astype(f32).astype(bf16)
    tiled = jnp.dot(block.astype(bf16), tile, preferred_element_type=f32)
    return jnp.where(own_columns_of(block.shape[0]), tiled, 0.0).astype(bf16)


def softplus(v):
    return jnp.maximum(v, 0.0) + jnp.log1p(jnp.exp(-jnp.abs(v)))


def forward_kernel(
    xt_ref, act_ref, dtw_ref, chan_ref, a_ref, gate_in_ref, h_ref, dt_ref, state, push
):
    @pl.when(pl.program_id(1) == 0)
    def _():
        state[...] = jnp.zeros_like(state)

    columns = xt_ref[...].astype(f32)
    rows_in = columns.T
    rank = rows_in[:, :R].astype(bf16)
    pre = dot(rank, dtw_ref[:, AT_DT : AT_DT + R], 1, 1) + chan_ref[KW + 1 : KW + 2, :]
    steps = softplus(pre)
    dt_ref[0] = steps
    push[...] = steps * act_ref[0].astype(f32)
    scaled = a_ref[...] * LOG2E
    drive = columns[R : R + N]
    reads = spread(rows_in[:, R + N :])
    h = state[...]
    for k in range(ROWS // T):
        for j in range(T):
            t = k * T + j
            decay = jnp.exp2(dt_ref[0, t : t + 1, :] * scaled)
            h = decay * h + drive[:, t : t + 1] * push[t : t + 1, :]
            h_ref[0, t * N : (t + 1) * N, :] = h.astype(bf16)
        here = slice(k * T, (k + 1) * T)
        scanned = dot(reads[here], h_ref[0, k * T * N : (k + 1) * T * N, :], 1, 0)
        gate_in_ref[0, here, :] = scanned + chan_ref[KW + 2 : KW + 3, :] * act_ref[
            0, here, :
        ].astype(f32)
    state[...] = h


def scan_forward(xt, act, dtw, chan, a_matrix):
    seqs, length, width = act.shape
    blocks = length // ROWS

    def at(s, b):
        return (s, b, 0)

    def fixed(s, b):
        return (0, 0)

    return pl.pallas_call(
        forward_kernel,
        grid=(seqs, blocks),
        in_specs=[
            pl.BlockSpec((WIDE, ROWS), lambda s, b: (0, s * blocks + b)),
            pl.BlockSpec((1, ROWS, width), at),
            pl.BlockSpec((width, SMALL), fixed),
            pl.BlockSpec((8, width), fixed),
            pl.BlockSpec((N, width), fixed),
        ],
        out_specs=[
            pl.BlockSpec((1, ROWS, width), at),
            pl.BlockSpec((1, ROWS * N, width), at),
            pl.BlockSpec((1, ROWS, width), at),
        ],
        out_shape=[
            jax.ShapeDtypeStruct((seqs, length, width), f32),
            jax.ShapeDtypeStruct((seqs, length * N, width), bf16),
            jax.ShapeDtypeStruct((seqs, length, width), f32),
        ],
        scratch_shapes=[pltpu.VMEM((N, width), f32), pltpu.VMEM((ROWS, width), f32)],
        compiler_params=params(60),
        cost_estimate=cost(18),
        name="scan_forward",
    )(xt, act, dtw, chan, a_matrix)


def middle_kernel(
    me_ref,
    gate_in_ref,
    act_ref,
    normed_ref,
    wg_ref,
    wo_ref,
    *refs,
):
    dps = lax.axis_size("dp")
    near = len(refs) - 2 * dps - 8
    cot_refs, part_refs = refs[:dps], refs[dps : 2 * dps]
    gout_refs = refs[2 * dps : 2 * dps + near]
    ggi_ref, ggp_ref, gin_ref, gskip_ref = refs[2 * dps + near : 2 * dps + near + 4]
    out_total, in_total, whole, part = refs[2 * dps + near + 4 :]
    block = pl.program_id(1)
    rows = act_ref.shape[1]
    start = (pl.program_id(0) == 0) & (block == 0)
    end = (pl.program_id(0) == pl.num_programs(0) - 1) & (block == pl.num_programs(1) - 1)

    @pl.when(start)
    def _():
        out_total[...] = jnp.zeros_like(out_total)
        in_total[...] = jnp.zeros_like(in_total)
        gskip_ref[...] = jnp.zeros_like(gskip_ref)

    @pl.when(block == 0)
    def _():
        lay_pieces(whole, cot_refs, me_ref[0])

    cot = whole[pl.ds(pl.multiple_of(block * rows, rows), rows), :]
    grad_gated = dot(cot, wo_ref[...], 1, 1)
    normed = normed_ref[0]
    gate = dot(normed, wg_ref[...], 1, 0).astype(bf16).astype(f32)
    sig = jax.nn.sigmoid(gate)
    gate_act = gate * sig
    gate_in = gate_in_ref[0]
    gated = (gate_in * gate_act).astype(bf16)
    ggi = grad_gated * gate_act
    ggi_ref[0] = ggi
    ggp = (grad_gated * gate_in * (sig * (1.0 + gate * (1.0 - sig)))).astype(bf16)
    ggp_ref[0] = ggp
    gskip_ref[...] += jnp.sum(ggi * act_ref[0].astype(f32), axis=0, keepdims=True)
    part[...] = dot(gated, wo_ref[...], 1, 0)
    deal_pieces(part_refs, part, me_ref[0], block)
    out_total[...] += dot(gated, cot, 0, 0)
    in_total[...] += dot(normed, ggp, 0, 0)

    @pl.when(end)
    def _():
        gin_ref[...] = in_total[...].astype(bf16)
        depth, own, _ = gout_refs[0].shape
        for j in range(near * depth):
            place = me_ref[1] ^ j
            for m, ref in enumerate(gout_refs):

                @pl.when(place % near == m)
                def _(ref=ref, place=place, j=j):
                    ref[place // near] = out_total[j * own : (j + 1) * own, :].astype(bf16)


def middle(me, gate_in, act, normed, wg, wo, cot, near, depth):
    dps = len(cot)
    seqs, piece, model = cot[0].shape
    length = dps * piece
    width = wo.shape[0]
    rows = min(BIG, length)
    blocks = length // rows
    own = width // (near * depth)

    def at(s, b, me):
        return (s, b, 0)

    def fixed(s, b, me):
        return (0, 0)

    return pl.pallas_call(
        middle_kernel,
        grid_spec=pltpu.PrefetchScalarGridSpec(
            num_scalar_prefetch=1,
            grid=(seqs, blocks),
            in_specs=[
                pl.BlockSpec((1, rows, width), at),
                pl.BlockSpec((1, rows, width), at),
                pl.BlockSpec((1, rows, model), at),
                pl.BlockSpec((model, width), fixed),
                pl.BlockSpec((width, model), fixed),
            ]
            + piece_specs(dps, piece, model),
            out_specs=piece_specs(dps, piece, model)
            + [pl.BlockSpec((depth, own, model), lambda s, b, me: (0, 0, 0))] * near
            + [
                pl.BlockSpec((1, rows, width), at),
                pl.BlockSpec((1, rows, width), at),
                pl.BlockSpec((model, width), fixed),
                pl.BlockSpec((1, width), fixed),
            ],
            scratch_shapes=[
                pltpu.VMEM((width, model), f32),
                pltpu.VMEM((model, width), f32),
                pltpu.VMEM((length, model), bf16),
                pltpu.VMEM((rows, model), f32),
            ],
        ),
        out_shape=piece_shapes(dps, seqs, piece, model, 2)
        + [jax.ShapeDtypeStruct((depth, own, model), bf16)] * near
        + [
            jax.ShapeDtypeStruct((seqs, length, width), f32),
            jax.ShapeDtypeStruct((seqs, length, width), bf16),
            jax.ShapeDtypeStruct((model, width), bf16),
            jax.ShapeDtypeStruct((1, width), f32),
        ],
        compiler_params=params(60),
        cost_estimate=cost(9),
        name="middle",
    )(me, gate_in, act, normed, wg, wo, *cot)


def backward_kernel(
    me_ref,
    xt_ref,
    act_ref,
    dt_ref,
    ggi_ref,
    chan_ref,
    a_ref,
    h_ref,
    before_ref,
    dtw_ref,
    *refs,
):
    gsp_ref, gact_ref, mine_ref, other_ref, galog_ref = refs[-10:-5]
    carried, total, g_buf, q_buf, gxt_ref = refs[-5:]
    first = pl.program_id(1) == pl.num_programs(1) - 1

    @pl.when(pl.program_id(1) == 0)
    def _():
        carried[...] = jnp.zeros_like(carried)

    @pl.when((pl.program_id(0) == 0) & (pl.program_id(1) == 0))
    def _():
        total[...] = jnp.zeros_like(total)

    columns = xt_ref[...].astype(f32)
    rows_in = columns.T
    a_now = a_ref[...]
    scaled = a_now * LOG2E
    read = columns[R + N :]
    rank = rows_in[:, :R].astype(bf16)
    pre = dot(rank, dtw_ref[:, AT_DT : AT_DT + R], 1, 1) + chan_ref[KW + 1 : KW + 2, :]
    ones = own_columns_of(T).astype(f32).astype(bf16)
    drives = spread(rows_in[:, R : R + N])
    ggi_low = ggi_ref[0].astype(bf16)
    push_low = (dt_ref[0] * act_ref[0].astype(f32)).astype(bf16)
    lanes = lax.broadcasted_iota(jnp.int32, (N, T), 1)
    p = carried[...]
    acc = total[...]
    for k in reversed(range(ROWS // T)):
        for j in reversed(range(T)):
            t = k * T + j
            step_row = dt_ref[0, t : t + 1, :]
            g = read[:, t : t + 1] * ggi_ref[0, t : t + 1, :] + p
            p = jnp.exp2(step_row * scaled) * g
            if t > 0:
                h_before = h_ref[0, (t - 1) * N : t * N, :].astype(f32)
            else:
                h_before = jnp.where(first, 0.0, before_ref[0].astype(f32))
            q = p * h_before
            acc = acc + q * step_row
            g_buf[t * N : (t + 1) * N, :] = g.astype(bf16)
            q_buf[t * N : (t + 1) * N, :] = (a_now * q).astype(bf16)
        here = slice(k * T, (k + 1) * T)
        states = slice(k * T * N, (k + 1) * T * N)
        pulled = dot(drives[here], g_buf[states, :], 1, 0)
        along = dot(ones, q_buf[states, :], 1, 0)
        act_now = act_ref[0, here, :].astype(f32)
        grad_steps = along + act_now * pulled
        gsp_ref[0, here, :] = (grad_steps * jax.nn.sigmoid(pre[here])).astype(bf16)
        gact_ref[0, here, :] = (
            pulled * dt_ref[0, here, :] + chan_ref[KW + 2 : KW + 3, :] * ggi_ref[0, here, :]
        )
        both_d = dot(g_buf[states, :], push_low[here], 1, 1)
        both_r = dot(h_ref[0, states, :], ggi_low[here], 1, 1)
        gdrive = jnp.zeros((N, T), f32)
        gread = jnp.zeros((N, T), f32)
        for j in range(T):
            gdrive = jnp.where(lanes == j, both_d[j * N : (j + 1) * N], gdrive)
            gread = jnp.where(lanes == j, both_r[j * N : (j + 1) * N], gread)
        gxt_ref[R : R + N, here] = gdrive
        gxt_ref[R + N :, here] = gread
    carried[...] = p
    total[...] = acc
    gxt_ref[0:R, :] = dot(dtw_ref[:, AT_DT : AT_DT + R], gsp_ref[0], 0, 1)
    halve(mine_ref, other_ref, gxt_ref[...], me_ref[0])
    galog_ref[...] = acc * a_now


def scan_backward(me, xt, act, dt, ggi, chan, a_matrix, states, dtw):
    seqs, length, width = act.shape
    blocks = length // ROWS

    def back(s, b):
        return (s, blocks - 1 - b, 0)

    def before(s, b):
        return (s, jnp.maximum((blocks - 1 - b) * ROWS - 1, 0), 0)

    def flat(s, b):
        return (0, s * blocks + blocks - 1 - b)

    def fixed(s, b):
        return (0, 0)

    return pl.pallas_call(
        backward_kernel,
        grid=(seqs, blocks),
        in_specs=[
            pl.BlockSpec(memory_space=pltpu.SMEM),
            pl.BlockSpec((WIDE, ROWS), flat),
            pl.BlockSpec((1, ROWS, width), back),
            pl.BlockSpec((1, ROWS, width), back),
            pl.BlockSpec((1, ROWS, width), back),
            pl.BlockSpec((8, width), fixed),
            pl.BlockSpec((N, width), fixed),
            pl.BlockSpec((1, ROWS * N, width), back),
            pl.BlockSpec((1, N, width), before),
            pl.BlockSpec((width, SMALL), fixed),
        ],
        out_specs=[
            pl.BlockSpec((1, ROWS, width), back),
            pl.BlockSpec((1, ROWS, width), back),
            pl.BlockSpec((WIDE // 2, ROWS), flat),
            pl.BlockSpec((WIDE // 2, ROWS), flat),
            pl.BlockSpec((N, width), fixed),
        ],
        out_shape=[
            jax.ShapeDtypeStruct((seqs, length, width), bf16),
            jax.ShapeDtypeStruct((seqs, length, width), f32),
            jax.ShapeDtypeStruct((WIDE // 2, seqs * length), f32),
            jax.ShapeDtypeStruct((WIDE // 2, seqs * length), f32),
            jax.ShapeDtypeStruct((N, width), f32),
        ],
        scratch_shapes=[
            pltpu.VMEM((N, width), f32),
            pltpu.VMEM((N, width), f32),
            pltpu.VMEM((ROWS * N, width), bf16),
            pltpu.VMEM((ROWS * N, width), bf16),
            pltpu.VMEM((WIDE, ROWS), f32),
        ],
        compiler_params=params(60),
        cost_estimate=cost(28),
        name="scan_backward",
    )(me, xt, act, dt, ggi, chan, a_matrix, states, states, dtw)


def leave_kernel(
    gact_ref,
    gxt_ref,
    xt_ref,
    gsp_ref,
    wx_ref,
    pre_ref,
    conv_ref,
    act_ref,
    normed_ref,
    chan_ref,
    gskip_ref,
    *refs,
):
    galog_refs = refs[:-6]
    gci_ref, gin_ref, small_ref, padded, in_total, sums = refs[-6:]
    block = pl.program_id(1)
    rows = gact_ref.shape[1]
    start = (pl.program_id(0) == 0) & (block == 0)
    end = (pl.program_id(0) == pl.num_programs(0) - 1) & (block == pl.num_programs(1) - 1)

    @pl.when(start)
    def _():
        in_total[...] = jnp.zeros_like(in_total)
        small_ref[...] = jnp.zeros_like(small_ref)
        sums[...] = jnp.zeros_like(sums)

    @pl.when(block == 0)
    def _():
        padded[rows : rows + 8, :] = jnp.zeros((8, padded.shape[1]), f32)

    @pl.when(block > 0)
    def _():
        padded[rows : rows + 8, :] = padded[0:8, :]

    gxt = gxt_ref[...]
    act = act_ref[0]
    grad_act = gact_ref[0] + dot(gxt, wx_ref[:, 0:WIDE], 0, 1)
    pre = pre_ref[0]
    sig = jax.nn.sigmoid(pre)
    grad_conv = grad_act * (sig * (1.0 + pre * (1.0 - sig)))
    padded[0:rows, :] = grad_conv
    conv = conv_ref[0].astype(f32)
    gci = jnp.zeros_like(grad_conv)
    for k in range(KW):
        moved = padded[KW - 1 - k : KW - 1 - k + rows, :]
        gci = gci + chan_ref[k : k + 1, :] * moved
        sums[N + k : N + k + 1, :] += jnp.sum(conv * moved, axis=0, keepdims=True)
    sums[N + KW : N + KW + 1, :] += jnp.sum(grad_conv, axis=0, keepdims=True)
    gsp = gsp_ref[0]
    sums[N + KW + 1 : N + KW + 2, :] += jnp.sum(gsp.astype(f32), axis=0, keepdims=True)
    low = gci.astype(bf16)
    gci_ref[0] = low
    in_total[...] += dot(normed_ref[0], low, 0, 0)
    small_ref[:, 0:WIDE] += dot(act, gxt, 0, 1)
    small_ref[:, WIDE : WIDE + R] += dot(gsp, xt_ref[0:R, :], 0, 1)

    @pl.when(end)
    def _():
        gin_ref[...] = in_total[...].astype(bf16)
        sums[0:N, :] = sum(ref[...] for ref in galog_refs)
        sums[N + KW + 2 : N + KW + 3, :] = gskip_ref[...]
        small_ref[:, WIDE + R :] = sums[...].T


def leave(gact, gxt, xt, gsp, wx, pre, conv, act, normed, chan, gskip, galog):
    seqs, length, width = act.shape
    model = normed.shape[2]
    rows = min(BIG, length)
    blocks = length // rows

    def back(s, b):
        return (s, blocks - 1 - b, 0)

    def flat(s, b):
        return (0, s * blocks + blocks - 1 - b)

    def fixed(s, b):
        return (0, 0)

    return pl.pallas_call(
        leave_kernel,
        grid=(seqs, blocks),
        in_specs=[
            pl.BlockSpec((1, rows, width), back),
            pl.BlockSpec((WIDE, rows), flat),
            pl.BlockSpec((WIDE, rows), flat),
            pl.BlockSpec((1, rows, width), back),
            pl.BlockSpec((width, SMALL), fixed),
            pl.BlockSpec((1, rows, width), back),
            pl.BlockSpec((1, rows, width), back),
            pl.BlockSpec((1, rows, width), back),
            pl.BlockSpec((1, rows, model), back),
            pl.BlockSpec((8, width), fixed),
            pl.BlockSpec((1, width), fixed),
        ]
        + [pl.BlockSpec((N, width), fixed)] * len(galog),
        out_specs=[
            pl.BlockSpec((1, rows, width), back),
            pl.BlockSpec((model, width), fixed),
            pl.BlockSpec((width, GRADS), fixed),
        ],
        out_shape=[
            jax.ShapeDtypeStruct((seqs, length, width), bf16),
            jax.ShapeDtypeStruct((model, width), bf16),
            jax.ShapeDtypeStruct((width, GRADS), f32),
        ],
        scratch_shapes=[
            pltpu.VMEM((rows + 8, width), f32),
            pltpu.VMEM((model, width), f32),
            pltpu.VMEM((REST, width), f32),
        ],
        compiler_params=params(60),
        cost_estimate=cost(8),
        name="leave",
    )(gact, gxt, xt, gsp, wx, pre, conv, act, normed, chan, gskip, *galog)


def rows_back_kernel(me_ref, gci_ref, ggp_ref, w0_ref, w1_ref, *refs):
    part = refs[-1]
    part[...] = dot(gci_ref[0], w0_ref[...], 1, 1) + dot(ggp_ref[0], w1_ref[...], 1, 1)
    deal_pieces(refs[:-1], part, me_ref[0], pl.program_id(1))


def rows_back(me, gci, ggp, w0, w1, dps):
    seqs, length, width = gci.shape
    model = w0.shape[0]
    piece = length // dps
    rows = min(BIG, length)
    blocks = length // rows

    def at(s, b, me):
        return (s, b, 0)

    def fixed(s, b, me):
        return (0, 0)

    return pl.pallas_call(
        rows_back_kernel,
        grid_spec=pltpu.PrefetchScalarGridSpec(
            num_scalar_prefetch=1,
            grid=(seqs, blocks),
            in_specs=[
                pl.BlockSpec((1, rows, width), at),
                pl.BlockSpec((1, rows, width), at),
                pl.BlockSpec((model, width), fixed),
                pl.BlockSpec((model, width), fixed),
            ],
            out_specs=piece_specs(dps, piece, model),
            scratch_shapes=[pltpu.VMEM((rows, model), f32)],
        ),
        out_shape=piece_shapes(dps, seqs, piece, model, 2),
        compiler_params=params(60),
        cost_estimate=cost(5),
        name="rows_back",
    )(me, gci, ggp, w0, w1)


def finish_kernel(tok_ref, cot_ref, gain_ref, *refs):
    out_ref = refs[-1]
    grad = refs[0][0]
    for ref in refs[1:-1]:
        grad = grad + ref[0].astype(f32)
    x = tok_ref[0].astype(f32)
    inv = lax.rsqrt(jnp.mean(x * x, axis=-1, keepdims=True) + 1e-05)
    grad = grad * gain_ref[...]
    back = x * inv * inv * inv * jnp.mean(grad * x, axis=-1, keepdims=True)
    out_ref[0] = inv * grad - back + cot_ref[0].astype(f32)


def finish(tok, cot, gain, parts):
    seqs, piece, model = tok.shape
    rows = pl.BlockSpec((1, piece, model), lambda s: (s, 0, 0))
    return pl.pallas_call(
        finish_kernel,
        grid=(seqs,),
        in_specs=[rows, rows, pl.BlockSpec((1, model), lambda s: (0, 0))] + [rows] * len(parts),
        out_specs=rows,
        out_shape=jax.ShapeDtypeStruct(tok.shape, f32),
        compiler_params=params(60),
        cost_estimate=cost(3),
        name="finish",
    )(tok, cot, gain, *parts)


def collect_kernel(
    conv_ref, gate_ref, out_ref, small_ref, w_ref, gain_ref, gin_ref, gx_ref, gdt_ref, gchan_ref, galog_ref, ggain_ref, squares_ref, square
):
    own_in, columns = w_ref.shape
    width = conv_ref.shape[2]
    dps = columns // (2 * width)
    peers = conv_ref.shape[0] // dps
    own = small_ref.shape[0]
    total = jnp.zeros((1, 128), f32)

    def squares(x):
        x = jnp.sum(x * x, axis=0, keepdims=True)
        return jnp.sum(x, axis=1, keepdims=True)

    ggain = jnp.zeros((own_in, 1), f32)
    for half in range(2):
        for k in range(dps):
            parts = gate_ref if half else conv_ref
            grad = parts[k * peers].astype(f32)
            for j in range(1, peers):
                grad = grad + parts[k * peers + j].astype(f32)
            here = slice((half * dps + k) * width, (half * dps + k + 1) * width)
            gin_ref[:, here] = grad
            total = total + squares(grad)
            low = w_ref[:, here].astype(bf16).astype(f32)
            ggain = ggain + jnp.sum(grad * low, axis=1, keepdims=True)
    total = total + squares(out_ref[...])
    small = small_ref[...]
    total = total + squares(small)
    gx_ref[...] = small[:, :WIDE]
    square[...] = jnp.zeros_like(square)
    square[0:own, 0:GRADS] = small
    square[0:own_in, GRADS : GRADS + 1] = ggain
    turned = square[...].T
    gdt_ref[...] = turned[WIDE : WIDE + R, :own]
    galog_ref[...] = turned[WIDE + R : WIDE + R + N, :own]
    gchan_ref[...] = turned[WIDE + R + N : WIDE + R + N + KW + 3, :own]
    grad = turned[GRADS : GRADS + 1, :own_in] / gain_ref[...].astype(bf16).astype(f32)
    ggain_ref[...] = grad
    squares_ref[...] = jnp.broadcast_to((total + squares(grad))[None], squares_ref.shape)


def collect(conv, gate, out, small, w, gain):
    own_in, columns = w.shape
    own = small.shape[0]
    shapes = [
        (own_in, columns),
        (own, WIDE),
        (R, own),
        (KW + 3, own),
        (N, own),
        (1, own_in),
        (conv.shape[0], 1, 128),
    ]
    whole = pl.BlockSpec(memory_space=pltpu.VMEM)
    return pl.pallas_call(
        collect_kernel,
        in_specs=[whole] * 6,
        out_specs=[whole] * len(shapes),
        out_shape=[jax.ShapeDtypeStruct(shape, f32) for shape in shapes],
        scratch_shapes=[pltpu.VMEM((128, 256), f32)],
        compiler_params=params(16),
        cost_estimate=cost(3),
        name="collect",
    )(conv, gate, out, small, w, gain)


def adam_kernel(squares_ref, *refs):
    count = len(learn_rates)
    weights, moments, grads = refs[:count], refs[count : 2 * count], refs[2 * count : 3 * count]
    outs = refs[3 * count :]
    norm = jnp.sqrt(jnp.sum(squares_ref[...], axis=0)[:, 0:1])
    outs[2 * count][...] = norm
    factor = jnp.minimum(1.0, clip_limit / (norm + 1e-06))
    for place in range(count):
        rate = learn_rates[place]
        gradient = grads[place][...] * factor
        weight = weights[place][...]
        rows_first = len(moments[place].shape) == 3 and moments[place].shape[1] == 2
        at = (lambda k: (slice(None), k)) if rows_first else (lambda k: k)
        first = 0.9 * moments[place][at(0)] + 0.1 * gradient
        old = moments[place][at(1)]
        root = jnp.sqrt(0.95 * old * old + 0.05 * gradient * gradient)
        update = first / (1.0 - 0.9**STEP) / (root / (1.0 - 0.95**STEP) ** 0.5 + 1e-08)
        outs[2 * place][at(0)] = first
        outs[2 * place][at(1)] = root
        outs[2 * place + 1][...] = weight - rate * (update + 0.01 * weight)


def adam(squares, weights, moments, grads):
    shapes = []
    for weight, moment in zip(weights, moments):
        shapes.append(jax.ShapeDtypeStruct(moment.shape, f32))
        shapes.append(jax.ShapeDtypeStruct(weight.shape, f32))
    shapes.append(jax.ShapeDtypeStruct((1, 1), f32))
    whole = pl.BlockSpec(memory_space=pltpu.VMEM)
    return pl.pallas_call(
        adam_kernel,
        in_specs=[whole] * (1 + 3 * len(weights)),
        out_specs=[whole] * len(shapes),
        out_shape=shapes,
        compiler_params=params(16),
        cost_estimate=cost(4),
        name="adam",
    )(squares, *weights, *moments, *grads)


def shards(
    tokens,
    cotangent,
    in_weight,
    out_weight,
    xproj_weight,
    dtproj_weight,
    chan_params,
    a_log,
    norm_gain,
    in_moments,
    out_moments,
    xproj_moments,
    dtproj_moments,
    chan_moments,
    alog_moments,
    gain_moments,
):
    both = ("dp", "fsdp")
    dps = lax.axis_size("dp")
    fsdps = lax.axis_size("fsdp")
    depth = min(4, fsdps)
    near = fsdps // depth
    me = jnp.stack([lax.axis_index("dp"), lax.axis_index("fsdp")])
    batches, groups, piece, model = tokens.shape
    seqs = batches * groups
    length = piece * dps
    own_in = in_weight.shape[0]
    own = out_weight.shape[0]
    width = own * fsdps

    in_low = in_weight.astype(bf16).reshape(own_in, 2, dps, width).transpose(2, 1, 0, 3)
    gain_row = jnp.pad(norm_gain.astype(bf16)[None], ((0, 7), (0, width - own_in)))
    in_parts = jnp.concatenate(
        [in_low[:, 0], in_low[:, 1], jnp.broadcast_to(gain_row, (dps, 8, width))], axis=1
    )
    in_parts = lax.all_to_all(in_parts, "dp", 0, 0, tiled=True)
    small = jnp.concatenate(
        [
            xproj_weight.astype(bf16),
            jnp.zeros((own, AT_DT - WIDE), bf16),
            dtproj_weight.astype(bf16).T,
            a_log.astype(bf16).T,
            chan_params.astype(bf16).T,
            jnp.zeros((own, SMALL - AT_REST - N - KW - 3), bf16),
        ],
        axis=1,
    )
    fold = max(width // SMALL, 1)
    aligned = own_in % 16 == 0 and own % (16 * fold) == 0 and width % SMALL == 0
    if aligned:
        packed = jnp.concatenate(jnp.split(small, fold), axis=1)
    else:
        packed = small.reshape(-1, width)
    here = dps * own_in
    gain_rows = jnp.pad(in_parts[:, 2 * own_in], ((0, -dps % 16), (0, 0)))
    first = jnp.concatenate([in_parts[:, :own_in].reshape(here, width), gain_rows, packed])
    out_low = out_weight.astype(bf16).reshape(own, model // width, width).transpose(1, 0, 2)
    second = [
        in_parts[:, own_in : 2 * own_in].reshape(here, width),
        out_low.reshape(-1, width),
    ]
    second = jnp.concatenate(second)
    tok = parts_dp_far(tokens.reshape(seqs, piece, model))
    first_own = swap_near(first)
    first, tok, first_own = lax.optimization_barrier((gather_far(first), tok, first_own))
    cot = parts_dp_far(after(cotangent.reshape(seqs, piece, model), first))
    tok = parts_dp_near(tok)
    first_rest = swap_near(jnp.stack(first[1:]))
    first, first_rest, cot = lax.optimization_barrier((first, first_rest, cot))

    def own_columns(parts):
        parts = parts.reshape(fsdps, dps, own_in, width)
        return parts.transpose(1, 0, 2, 3).reshape(model, width)

    if aligned:
        w_conv, small, gain, a_matrix, chan = assemble(
            assemble_first_kernel,
            "assemble_first",
            me,
            first,
            first_own,
            first_rest,
            [
                ((model, width), bf16),
                ((width, SMALL), bf16),
                ((1, model), f32),
                ((N, width), f32),
                ((8, width), f32),
            ],
            [pltpu.VMEM((model // own_in, 128), f32)],
            60,
        )
    else:
        merged = merge_near(first, first_own, first_rest)
        w_conv = own_columns(merged[:, :here])
        gain = merged[:, here : here + dps, :own_in].transpose(1, 0, 2)
        gain = gain.reshape(1, model).astype(f32)
        small = merged[:, here + dps + -dps % 16 :].reshape(width, SMALL)
        rest = small[:, AT_REST : AT_REST + REST].astype(f32).T
        a_matrix = -jnp.exp(rest[:N])
        chan = rest[N : N + 8]

    far = gather_far(second)
    normed, conv, pre, act, *xt = enter(me, gain, w_conv, chan, small, tok)
    cot = parts_dp_near(cot)
    xt, far = lax.optimization_barrier((xt, far))
    xt = sum_dp_near(*xt)
    second_own = swap_near(after(far[0], xt))
    second_rest = swap_near(jnp.stack(after(far[1:], xt)))
    xt = sum_dp_far(xt, f32)
    if aligned:
        w_gate, w_out = assemble(
            assemble_second_kernel,
            "assemble_second",
            me,
            far,
            second_own,
            second_rest,
            [((model, width), bf16), ((width, model), bf16)],
            [],
            24,
        )
    else:
        merged = merge_near(far, second_own, second_rest)
        w_gate = own_columns(merged[:, :here])
        w_out = merged[:, here:].reshape(fsdps, model // width, own, width)
        w_out = w_out.transpose(0, 2, 1, 3).reshape(width, model)
    gate_in, states, dt = scan_forward(xt, act, small, chan, a_matrix)
    outs = middle(me, gate_in, act, normed, w_gate, w_out, cot, near, depth)
    part, gout = outs[:dps], outs[dps : dps + near]
    ggi, ggp, gin_gate, gskip = outs[dps + near :]
    gate_parts = lax.all_to_all(gin_gate.reshape(-1, own_in, width), both, 0, 0, tiled=True)
    gout_near = reduce_near(gout)
    out_mine, out_parts = send_dp_near(part)

    gsp, gact, *gxt, galog = scan_backward(
        me, xt, act, dt, ggi, chan, a_matrix, states, small
    )
    gxt, out_mine, gout_near = lax.optimization_barrier((gxt, out_mine, gout_near))
    gxt = sum_dp_near(*gxt)
    gout_far = send_far(list(after(gout_near, gxt)))
    out_rows = send_dp_far(list(out_mine), list(after(out_parts, gxt)))
    gxt = sum_dp_far(gxt, bf16)
    gxt, gate_parts = lax.optimization_barrier((gxt, gate_parts))
    gci, gin_conv, small_grad = leave(
        gact, gxt, xt, gsp, small, pre, conv, act, normed, chan, gskip, [galog]
    )
    gin_conv, gout_far, out_rows = lax.optimization_barrier((gin_conv, gout_far, out_rows))
    conv_parts = lax.all_to_all(gin_conv.reshape(-1, own_in, width), both, 0, 0, tiled=True)
    grad_out = sum(part.astype(f32) for part in gout_far)
    small_near = reduce_near(split_near(small_grad.reshape(fsdps, own, GRADS)))
    part_back = rows_back(me, gci, ggp, w_conv, w_gate, dps)
    back_mine, back_parts = send_dp_near(part_back)
    small_near, back_parts = lax.optimization_barrier((small_near, back_parts))
    own_small = sum(part.astype(f32) for part in send_far(list(small_near)))
    part_back = send_dp_far(back_mine, list(back_parts))
    out_rows = sum(part.astype(f32) for part in out_rows).reshape(tokens.shape)
    block_output = (tokens.astype(f32) + out_rows).astype(bf16)

    def flat2(x):
        return x.reshape(x.shape[:-1] + (1, x.shape[-1]))

    grad_in, grad_x, grad_dt, grad_chan, grad_alog, grad_gain, squares = collect(
        conv_parts, gate_parts, grad_out, own_small, in_weight, flat2(norm_gain)
    )
    grad_normed = sum(part.astype(f32) for part in after(part_back, squares)).reshape(tokens.shape)

    input_grad = finish(
        tokens.reshape(seqs, piece, model),
        cotangent.reshape(seqs, piece, model),
        gain,
        after(part_back, squares),
    ).reshape(tokens.shape)
    squares = lax.all_to_all(squares, both, 0, 0, tiled=True)
    weights = (in_weight, out_weight, xproj_weight, dtproj_weight, chan_params, a_log, flat2(norm_gain))
    moments = (
        in_moments,
        out_moments,
        xproj_moments,
        dtproj_moments,
        chan_moments.transpose(1, 0, 2),
        alog_moments,
        flat2(gain_moments),
    )
    grads = (grad_in, grad_out, grad_x, grad_dt, grad_chan, grad_alog, grad_gain)
    updated = list(adam(squares, weights, moments, grads))
    grad_norm = updated.pop().reshape(())
    updated[8] = updated[8].transpose(1, 0, 2)
    updated[-2] = updated[-2].reshape(gain_moments.shape)
    updated[-1] = updated[-1].reshape(norm_gain.shape)
    return (block_output, input_grad, grad_norm) + tuple(updated)


def solution(mesh):
    both = ("dp", "fsdp")
    row_specs = (P(None, "fsdp", "dp", None),) * 2
    weight_specs = (
        P(both, None),
        P(both, None),
        P(both, None),
        P(None, both),
        P(None, both),
        P(None, both),
        P(both),
    )
    moment_specs = (
        P(None, both, None),
        P(None, both, None),
        P(None, both, None),
        P(None, None, both),
        P(None, None, both),
        P(None, None, both),
        P(None, both),
    )
    updated = tuple(spec for pair in zip(moment_specs, weight_specs) for spec in pair)
    return jax.shard_map(
        shards,
        mesh=mesh,
        in_specs=row_specs + weight_specs + moment_specs,
        out_specs=row_specs + (P(),) + updated,
        check_vma=False,
    )
```

```python
import jax
import jax.numpy as jnp
from jax import lax
from jax.experimental import pallas as pl
from jax.experimental.pallas import tpu as pltpu
from jax.sharding import PartitionSpec as P

N = 16
R = 64
KW = 4
STEP = 7
ROWS = 128
T = 16
WIDE = R + 2 * N
REST = 32
GRADS = WIDE + R + REST
AT_DT = 128
AT_REST = 192
SMALL = 256
BIG = 512

bf16 = jnp.bfloat16
f32 = jnp.float32
LOG2E = 1.4426950408889634
clip_limit = 1.0
learn_rates = (0.03, 0.03, 0.03, 0.15, 0.3, 1.0, 0.3)


def dot(left, right, on_left, on_right):
    return lax.dot_general(
        left, right, (((on_left,), (on_right,)), ((), ())), preferred_element_type=f32
    )


def params(mib):
    return pltpu.CompilerParams(vmem_limit_bytes=mib * 1024 * 1024)


def cost(us):
    return pl.CostEstimate(flops=int(us * 8e7), bytes_accessed=int(us * 3e5), transcendentals=0)


def swap(x, axis, mask):
    peers = lax.axis_size(axis)
    return lax.ppermute(x, axis, [(i, i ^ mask) for i in range(peers)])


def after(x, *others):
    return lax.optimization_barrier((x,) + others)[0]


def masks(axis):
    peers = lax.axis_size(axis)
    return [1 << k for k in range(peers.bit_length() - 1)]


def in_order(parts, axis):
    peers = lax.axis_size(axis)
    for mask in masks(axis):
        pairs = parts.reshape((peers // (2 * mask), 2, mask) + parts.shape[1:])
        high = (lax.axis_index(axis) & mask) != 0
        parts = jnp.where(high, pairs[:, ::-1], pairs).reshape(parts.shape)
    return parts


def parts_dp_far(x):
    held = [x]
    for mask in masks("dp")[:0:-1]:
        held = [part for p in held for part in (p, swap(p, "dp", mask))]
    return held


def parts_dp_near(held):
    return [part for p in held for part in (p, swap(p, "dp", 1))]


def gather_far(x):
    peers = lax.axis_size("fsdp")
    depth = min(4, peers)
    return [x] + [swap(x, "fsdp", m * (peers // depth)) for m in range(1, depth)]


def swap_near(x):
    near = lax.axis_size("fsdp") // min(4, lax.axis_size("fsdp"))
    return [swap(x, "fsdp", m) for m in range(1, near)]


def merge_near(far, own, rest):
    nears = [far] + [[one] + list(stack) for one, stack in zip(own, rest)]
    parts = jnp.stack([part for both in zip(*nears) for part in both])
    return in_order(parts, "fsdp")


def send_dp_near(parts):
    moved = [swap(part, "dp", 1) for part in parts[1::2]]
    sums = [kept + part.astype(f32) for kept, part in zip(parts[2::2], moved[1:])]
    return [parts[0], moved[0]], [part.astype(bf16) for part in sums]


def send_dp_far(mine, parts):
    for mask in masks("dp")[1:]:
        moved = [swap(part, "dp", mask) for part in parts[0::2]]
        mine = mine + [moved[0]]
        parts = [
            (kept.astype(f32) + part.astype(f32)).astype(bf16)
            for kept, part in zip(parts[1::2], moved[1:])
        ]
    return mine


def sum_dp_near(mine, other):
    return mine + swap(other, "dp", 1)


def sum_dp_far(mine, sent):
    high = (lax.axis_index("dp") & 1) != 0
    for mask in masks("dp")[1:]:
        mine = mine + swap(mine.astype(sent), "dp", mask).astype(f32)
    mine = mine.astype(bf16)
    other = swap(mine, "dp", 1)
    both = jnp.where(high, jnp.stack([other, mine]), jnp.stack([mine, other]))
    return both.reshape((-1,) + mine.shape[1:])


def reduce_near(parts):
    mine = parts[0].astype(f32)
    for m in range(1, len(parts)):
        mine = mine + swap(parts[m].astype(bf16), "fsdp", m).astype(f32)
    return [mine[0]] + [mine[d].astype(bf16) for d in range(1, mine.shape[0])]


def split_near(x):
    peers = lax.axis_size("fsdp")
    depth = min(4, peers)
    x = in_order(x, "fsdp").reshape((depth, peers // depth) + x.shape[1:])
    return [x[:, m] for m in range(x.shape[1])]


def send_far(mine):
    near = lax.axis_size("fsdp") // len(mine)
    return mine[:1] + [swap(mine[m], "fsdp", m * near) for m in range(1, len(mine))]


def by_near(refs, depth):
    parts = []
    for ref in refs:
        parts += [ref] if len(ref.shape) == 2 else [ref.at[d] for d in range(ref.shape[0])]
    return [parts[k : k + depth] for k in range(0, len(parts), depth)]


def assemble_first_kernel(me_ref, *refs):
    w_ref, small_ref, gain_ref, a_ref, chan_ref, gains = refs[-6:]
    model, width = w_ref.shape
    peers = lax.axis_size("fsdp")
    depth = min(4, peers)
    near = peers // depth
    raws = by_near(refs[:-6], depth)
    own = width // peers
    fold = width // SMALL
    here = model // peers
    own_in = model // gains.shape[0]
    dps = here // own_in
    stretch = own // fold
    at_small = here + dps + -dps % 16
    for m in range(near):
        for d in range(depth):
            j = me_ref[1] ^ (d * near + m)
            for k in range(dps):
                to = pl.multiple_of((k * peers + j) * own_in, own_in)
                w_ref[pl.ds(to, own_in), :] = raws[m][d][k * own_in : (k + 1) * own_in, :]
                row = raws[m][d][here : here + 16, 0:128].astype(f32)[k : k + 1]
                gains[pl.ds(k * peers + j, 1), :] = row
            for f in range(fold):
                to = pl.multiple_of(j * own + f * stretch, stretch)
                small_ref[pl.ds(to, stretch), :] = raws[m][d][
                    at_small : at_small + stretch, f * SMALL : (f + 1) * SMALL
                ]
    row = lax.broadcasted_iota(jnp.int32, (own_in, model), 0)
    column = lax.broadcasted_iota(jnp.int32, (own_in, model), 1)
    tile = (column % own_in == row).astype(f32).astype(bf16)
    tiled = dot(gains[:, 0:own_in].astype(bf16), tile, 1, 0)
    row = lax.broadcasted_iota(jnp.int32, tiled.shape, 0)
    column = lax.broadcasted_iota(jnp.int32, tiled.shape, 1)
    gain_ref[...] = jnp.sum(jnp.where(column // own_in == row, tiled, 0.0), axis=0, keepdims=True)
    turned = small_ref[...].astype(f32).T
    a_ref[...] = -jnp.exp(turned[AT_REST : AT_REST + N])
    chan_ref[...] = turned[AT_REST + N : AT_REST + N + 8]


def assemble_second_kernel(me_ref, *refs):
    wg_ref, wo_ref = refs[-2:]
    model, width = wg_ref.shape
    peers = lax.axis_size("fsdp")
    depth = min(4, peers)
    near = peers // depth
    raws = by_near(refs[:-2], depth)
    own = width // peers
    here = model // peers
    dps = lax.axis_size("dp")
    own_in = here // dps
    for m in range(near):
        for d in range(depth):
            j = me_ref[1] ^ (d * near + m)
            for k in range(dps):
                to = pl.multiple_of((k * peers + j) * own_in, own_in)
                wg_ref[pl.ds(to, own_in), :] = raws[m][d][k * own_in : (k + 1) * own_in, :]
            for c in range(model // width):
                to = pl.multiple_of(j * own, own)
                wo_ref[pl.ds(to, own), c * width : (c + 1) * width] = raws[m][d][
                    here + c * own : here + (c + 1) * own, :
                ]


def assemble(kernel, name, me, far, own, rest, shapes, scratch, mib):
    raws = far + [part for both in zip(own, rest) for part in both]
    whole = pl.BlockSpec(memory_space=pltpu.VMEM)
    return pl.pallas_call(
        kernel,
        in_specs=[pl.BlockSpec(memory_space=pltpu.SMEM)] + [whole] * len(raws),
        out_specs=[whole] * len(shapes),
        out_shape=[jax.ShapeDtypeStruct(shape, dtype) for shape, dtype in shapes],
        scratch_shapes=scratch,
        compiler_params=params(mib),
        cost_estimate=cost(2),
        name=name,
    )(me, *raws)


def lay_pieces(whole, refs, me):
    piece = refs[0].shape[1]
    for p, ref in enumerate(refs):
        whole[pl.ds(pl.multiple_of((me ^ p) * piece, piece), piece), :] = ref[0]


def deal_pieces(refs, part, me, block):
    piece = refs[0].shape[1]
    per = part.shape[0] // piece
    for p, ref in enumerate(refs):
        at = (me ^ p) - block * per

        @pl.when((at >= 0) & (at < per))
        def _(ref=ref, at=at):
            ref[0] = part[pl.ds(pl.multiple_of(at * piece, piece), piece), :].astype(ref.dtype)


def piece_shapes(dps, seqs, piece, model, wide):
    return [
        jax.ShapeDtypeStruct((seqs, piece, model), bf16 if p % wide else f32) for p in range(dps)
    ]


def piece_specs(dps, piece, model):
    return [pl.BlockSpec((1, piece, model), lambda s, b, me: (s, 0, 0))] * dps


def halve(mine_ref, other_ref, rows, me):
    low, high = rows[: WIDE // 2], rows[WIDE // 2 :]
    odd = me % 2 == 1
    mine_ref[...] = jnp.where(odd, high, low)
    other_ref[...] = jnp.where(odd, low, high)


def enter_kernel(me_ref, gain_ref, w_ref, chan_ref, wx_ref, *refs):
    tok_refs = refs[:-8]
    normed_ref, conv_ref, pre_ref, act_ref, xt_ref, other_ref, padded, whole = refs[-8:]
    block = pl.program_id(1)
    rows = conv_ref.shape[1]

    @pl.when(block == 0)
    def _():
        padded[0:8, :] = jnp.zeros((8, padded.shape[1]), f32)
        lay_pieces(whole, tok_refs, me_ref[0])

    @pl.when(block > 0)
    def _():
        padded[0:8, :] = padded[rows : rows + 8, :]

    x = whole[pl.ds(pl.multiple_of(block * rows, rows), rows), :].astype(f32)
    inv = lax.rsqrt(jnp.mean(x * x, axis=-1, keepdims=True) + 1e-05)
    normed = (x * inv * gain_ref[...]).astype(bf16)
    normed_ref[0] = normed
    conv = dot(normed, w_ref[...], 1, 0).astype(bf16)
    conv_ref[0] = conv
    padded[8 : rows + 8, :] = conv.astype(f32)
    pre = chan_ref[KW : KW + 1, :]
    for k in range(KW):
        pre = pre + chan_ref[k : k + 1, :] * padded[5 + k : 5 + k + rows, :]
    pre_ref[0] = pre
    act = (pre * jax.nn.sigmoid(pre)).astype(bf16)
    act_ref[0] = act
    halve(xt_ref, other_ref, dot(wx_ref[:, 0:WIDE], act, 0, 1), me_ref[0])


def enter(me, gain, w, chan, wx, tok):
    dps = len(tok)
    seqs, piece, model = tok[0].shape
    length = dps * piece
    width = w.shape[1]
    rows = min(BIG, length)
    blocks = length // rows

    def at(s, b, me):
        return (s, b, 0)

    def fixed(s, b, me):
        return (0, 0)

    return pl.pallas_call(
        enter_kernel,
        grid_spec=pltpu.PrefetchScalarGridSpec(
            num_scalar_prefetch=1,
            grid=(seqs, blocks),
            in_specs=[
                pl.BlockSpec((1, model), fixed),
                pl.BlockSpec((model, width), fixed),
                pl.BlockSpec((8, width), fixed),
                pl.BlockSpec((width, SMALL), fixed),
            ]
            + piece_specs(dps, piece, model),
            out_specs=[
                pl.BlockSpec((1, rows, model), at),
                pl.BlockSpec((1, rows, width), at),
                pl.BlockSpec((1, rows, width), at),
                pl.BlockSpec((1, rows, width), at),
                pl.BlockSpec((WIDE // 2, rows), lambda s, b, me: (0, s * blocks + b)),
                pl.BlockSpec((WIDE // 2, rows), lambda s, b, me: (0, s * blocks + b)),
            ],
            scratch_shapes=[pltpu.VMEM((rows + 8, width), f32), pltpu.VMEM((length, model), bf16)],
        ),
        out_shape=[
            jax.ShapeDtypeStruct((seqs, length, model), bf16),
            jax.ShapeDtypeStruct((seqs, length, width), bf16),
            jax.ShapeDtypeStruct((seqs, length, width), f32),
            jax.ShapeDtypeStruct((seqs, length, width), bf16),
            jax.ShapeDtypeStruct((WIDE // 2, seqs * length), f32),
            jax.ShapeDtypeStruct((WIDE // 2, seqs * length), f32),
        ],
        compiler_params=params(60),
        cost_estimate=cost(7),
        name="enter",
    )(me, gain, w, chan, wx, *tok)


def own_columns_of(rows):
    row = lax.broadcasted_iota(jnp.int32, (rows, T * N), 0)
    column = lax.broadcasted_iota(jnp.int32, (rows, T * N), 1)
    return column // N == row % T


def spread(block):
    row = lax.broadcasted_iota(jnp.int32, (N, T * N), 0)
    column = lax.broadcasted_iota(jnp.int32, (N, T * N), 1)
    tile = (column % N == row).astype(f32).astype(bf16)
    tiled = jnp.dot(block.astype(bf16), tile, preferred_element_type=f32)
    return jnp.where(own_columns_of(block.shape[0]), tiled, 0.0).astype(bf16)


def softplus(v):
    return jnp.maximum(v, 0.0) + jnp.log1p(jnp.exp(-jnp.abs(v)))


def forward_kernel(
    xt_ref, act_ref, dtw_ref, chan_ref, a_ref, gate_in_ref, h_ref, dt_ref, state, push
):
    @pl.when(pl.program_id(1) == 0)
    def _():
        state[...] = jnp.zeros_like(state)

    columns = xt_ref[...].astype(f32)
    rows_in = columns.T
    rank = rows_in[:, :R].astype(bf16)
    pre = dot(rank, dtw_ref[:, AT_DT : AT_DT + R], 1, 1) + chan_ref[KW + 1 : KW + 2, :]
    steps = softplus(pre)
    dt_ref[0] = steps
    push[...] = steps * act_ref[0].astype(f32)
    scaled = a_ref[...] * LOG2E
    drive = columns[R : R + N]
    reads = spread(rows_in[:, R + N :])
    h = state[...]
    for k in range(ROWS // T):
        for j in range(T):
            t = k * T + j
            decay = jnp.exp2(dt_ref[0, t : t + 1, :] * scaled)
            h = decay * h + drive[:, t : t + 1] * push[t : t + 1, :]
            h_ref[0, t * N : (t + 1) * N, :] = h.astype(bf16)
        here = slice(k * T, (k + 1) * T)
        scanned = dot(reads[here], h_ref[0, k * T * N : (k + 1) * T * N, :], 1, 0)
        gate_in_ref[0, here, :] = scanned + chan_ref[KW + 2 : KW + 3, :] * act_ref[
            0, here, :
        ].astype(f32)
    state[...] = h


def scan_forward(xt, act, dtw, chan, a_matrix):
    seqs, length, width = act.shape
    blocks = length // ROWS

    def at(s, b):
        return (s, b, 0)

    def fixed(s, b):
        return (0, 0)

    return pl.pallas_call(
        forward_kernel,
        grid=(seqs, blocks),
        in_specs=[
            pl.BlockSpec((WIDE, ROWS), lambda s, b: (0, s * blocks + b)),
            pl.BlockSpec((1, ROWS, width), at),
            pl.BlockSpec((width, SMALL), fixed),
            pl.BlockSpec((8, width), fixed),
            pl.BlockSpec((N, width), fixed),
        ],
        out_specs=[
            pl.BlockSpec((1, ROWS, width), at),
            pl.BlockSpec((1, ROWS * N, width), at),
            pl.BlockSpec((1, ROWS, width), at),
        ],
        out_shape=[
            jax.ShapeDtypeStruct((seqs, length, width), f32),
            jax.ShapeDtypeStruct((seqs, length * N, width), bf16),
            jax.ShapeDtypeStruct((seqs, length, width), f32),
        ],
        scratch_shapes=[pltpu.VMEM((N, width), f32), pltpu.VMEM((ROWS, width), f32)],
        compiler_params=params(60),
        cost_estimate=cost(18),
        name="scan_forward",
    )(xt, act, dtw, chan, a_matrix)


def middle_kernel(
    me_ref,
    gate_in_ref,
    act_ref,
    normed_ref,
    wg_ref,
    wo_ref,
    *refs,
):
    dps = lax.axis_size("dp")
    near = len(refs) - 2 * dps - 8
    cot_refs, part_refs = refs[:dps], refs[dps : 2 * dps]
    gout_refs = refs[2 * dps : 2 * dps + near]
    ggi_ref, ggp_ref, gin_ref, gskip_ref = refs[2 * dps + near : 2 * dps + near + 4]
    out_total, in_total, whole, part = refs[2 * dps + near + 4 :]
    block = pl.program_id(1)
    rows = act_ref.shape[1]
    start = (pl.program_id(0) == 0) & (block == 0)
    end = (pl.program_id(0) == pl.num_programs(0) - 1) & (block == pl.num_programs(1) - 1)

    @pl.when(start)
    def _():
        out_total[...] = jnp.zeros_like(out_total)
        in_total[...] = jnp.zeros_like(in_total)
        gskip_ref[...] = jnp.zeros_like(gskip_ref)

    @pl.when(block == 0)
    def _():
        lay_pieces(whole, cot_refs, me_ref[0])

    cot = whole[pl.ds(pl.multiple_of(block * rows, rows), rows), :]
    grad_gated = dot(cot, wo_ref[...], 1, 1)
    normed = normed_ref[0]
    gate = dot(normed, wg_ref[...], 1, 0).astype(bf16).astype(f32)
    sig = jax.nn.sigmoid(gate)
    gate_act = gate * sig
    gate_in = gate_in_ref[0]
    gated = (gate_in * gate_act).astype(bf16)
    ggi = grad_gated * gate_act
    ggi_ref[0] = ggi
    ggp = (grad_gated * gate_in * (sig * (1.0 + gate * (1.0 - sig)))).astype(bf16)
    ggp_ref[0] = ggp
    gskip_ref[...] += jnp.sum(ggi * act_ref[0].astype(f32), axis=0, keepdims=True)
    part[...] = dot(gated, wo_ref[...], 1, 0)
    deal_pieces(part_refs, part, me_ref[0], block)
    out_total[...] += dot(gated, cot, 0, 0)
    in_total[...] += dot(normed, ggp, 0, 0)

    @pl.when(end)
    def _():
        gin_ref[...] = in_total[...].astype(bf16)
        depth, own, _ = gout_refs[0].shape
        for j in range(near * depth):
            place = me_ref[1] ^ j
            for m, ref in enumerate(gout_refs):

                @pl.when(place % near == m)
                def _(ref=ref, place=place, j=j):
                    ref[place // near] = out_total[j * own : (j + 1) * own, :].astype(bf16)


def middle(me, gate_in, act, normed, wg, wo, cot, near, depth):
    dps = len(cot)
    seqs, piece, model = cot[0].shape
    length = dps * piece
    width = wo.shape[0]
    rows = min(BIG, length)
    blocks = length // rows
    own = width // (near * depth)

    def at(s, b, me):
        return (s, b, 0)

    def fixed(s, b, me):
        return (0, 0)

    return pl.pallas_call(
        middle_kernel,
        grid_spec=pltpu.PrefetchScalarGridSpec(
            num_scalar_prefetch=1,
            grid=(seqs, blocks),
            in_specs=[
                pl.BlockSpec((1, rows, width), at),
                pl.BlockSpec((1, rows, width), at),
                pl.BlockSpec((1, rows, model), at),
                pl.BlockSpec((model, width), fixed),
                pl.BlockSpec((width, model), fixed),
            ]
            + piece_specs(dps, piece, model),
            out_specs=piece_specs(dps, piece, model)
            + [pl.BlockSpec((depth, own, model), lambda s, b, me: (0, 0, 0))] * near
            + [
                pl.BlockSpec((1, rows, width), at),
                pl.BlockSpec((1, rows, width), at),
                pl.BlockSpec((model, width), fixed),
                pl.BlockSpec((1, width), fixed),
            ],
            scratch_shapes=[
                pltpu.VMEM((width, model), f32),
                pltpu.VMEM((model, width), f32),
                pltpu.VMEM((length, model), bf16),
                pltpu.VMEM((rows, model), f32),
            ],
        ),
        out_shape=piece_shapes(dps, seqs, piece, model, 2)
        + [jax.ShapeDtypeStruct((depth, own, model), bf16)] * near
        + [
            jax.ShapeDtypeStruct((seqs, length, width), f32),
            jax.ShapeDtypeStruct((seqs, length, width), bf16),
            jax.ShapeDtypeStruct((model, width), bf16),
            jax.ShapeDtypeStruct((1, width), f32),
        ],
        compiler_params=params(60),
        cost_estimate=cost(9),
        name="middle",
    )(me, gate_in, act, normed, wg, wo, *cot)


def backward_kernel(
    me_ref,
    xt_ref,
    act_ref,
    dt_ref,
    ggi_ref,
    chan_ref,
    a_ref,
    h_ref,
    before_ref,
    dtw_ref,
    *refs,
):
    gsp_ref, gact_ref, mine_ref, other_ref, galog_ref = refs[-10:-5]
    carried, total, g_buf, q_buf, gxt_ref = refs[-5:]
    first = pl.program_id(1) == pl.num_programs(1) - 1

    @pl.when(pl.program_id(1) == 0)
    def _():
        carried[...] = jnp.zeros_like(carried)

    @pl.when((pl.program_id(0) == 0) & (pl.program_id(1) == 0))
    def _():
        total[...] = jnp.zeros_like(total)

    columns = xt_ref[...].astype(f32)
    rows_in = columns.T
    a_now = a_ref[...]
    scaled = a_now * LOG2E
    read = columns[R + N :]
    rank = rows_in[:, :R].astype(bf16)
    pre = dot(rank, dtw_ref[:, AT_DT : AT_DT + R], 1, 1) + chan_ref[KW + 1 : KW + 2, :]
    ones = own_columns_of(T).astype(f32).astype(bf16)
    drives = spread(rows_in[:, R : R + N])
    ggi_low = ggi_ref[0].astype(bf16)
    push_low = (dt_ref[0] * act_ref[0].astype(f32)).astype(bf16)
    lanes = lax.broadcasted_iota(jnp.int32, (N, T), 1)
    p = carried[...]
    acc = total[...]
    for k in reversed(range(ROWS // T)):
        for j in reversed(range(T)):
            t = k * T + j
            step_row = dt_ref[0, t : t + 1, :]
            g = read[:, t : t + 1] * ggi_ref[0, t : t + 1, :] + p
            p = jnp.exp2(step_row * scaled) * g
            if t > 0:
                h_before = h_ref[0, (t - 1) * N : t * N, :].astype(f32)
            else:
                h_before = jnp.where(first, 0.0, before_ref[0].astype(f32))
            q = p * h_before
            acc = acc + q * step_row
            g_buf[t * N : (t + 1) * N, :] = g.astype(bf16)
            q_buf[t * N : (t + 1) * N, :] = (a_now * q).astype(bf16)
        here = slice(k * T, (k + 1) * T)
        states = slice(k * T * N, (k + 1) * T * N)
        pulled = dot(drives[here], g_buf[states, :], 1, 0)
        along = dot(ones, q_buf[states, :], 1, 0)
        act_now = act_ref[0, here, :].astype(f32)
        grad_steps = along + act_now * pulled
        gsp_ref[0, here, :] = (grad_steps * jax.nn.sigmoid(pre[here])).astype(bf16)
        gact_ref[0, here, :] = (
            pulled * dt_ref[0, here, :] + chan_ref[KW + 2 : KW + 3, :] * ggi_ref[0, here, :]
        )
        both_d = dot(g_buf[states, :], push_low[here], 1, 1)
        both_r = dot(h_ref[0, states, :], ggi_low[here], 1, 1)
        gdrive = jnp.zeros((N, T), f32)
        gread = jnp.zeros((N, T), f32)
        for j in range(T):
            gdrive = jnp.where(lanes == j, both_d[j * N : (j + 1) * N], gdrive)
            gread = jnp.where(lanes == j, both_r[j * N : (j + 1) * N], gread)
        gxt_ref[R : R + N, here] = gdrive
        gxt_ref[R + N :, here] = gread
    carried[...] = p
    total[...] = acc
    gxt_ref[0:R, :] = dot(dtw_ref[:, AT_DT : AT_DT + R], gsp_ref[0], 0, 1)
    halve(mine_ref, other_ref, gxt_ref[...], me_ref[0])
    galog_ref[...] = acc * a_now


def scan_backward(me, xt, act, dt, ggi, chan, a_matrix, states, dtw):
    seqs, length, width = act.shape
    blocks = length // ROWS

    def back(s, b):
        return (s, blocks - 1 - b, 0)

    def before(s, b):
        return (s, jnp.maximum((blocks - 1 - b) * ROWS - 1, 0), 0)

    def flat(s, b):
        return (0, s * blocks + blocks - 1 - b)

    def fixed(s, b):
        return (0, 0)

    return pl.pallas_call(
        backward_kernel,
        grid=(seqs, blocks),
        in_specs=[
            pl.BlockSpec(memory_space=pltpu.SMEM),
            pl.BlockSpec((WIDE, ROWS), flat),
            pl.BlockSpec((1, ROWS, width), back),
            pl.BlockSpec((1, ROWS, width), back),
            pl.BlockSpec((1, ROWS, width), back),
            pl.BlockSpec((8, width), fixed),
            pl.BlockSpec((N, width), fixed),
            pl.BlockSpec((1, ROWS * N, width), back),
            pl.BlockSpec((1, N, width), before),
            pl.BlockSpec((width, SMALL), fixed),
        ],
        out_specs=[
            pl.BlockSpec((1, ROWS, width), back),
            pl.BlockSpec((1, ROWS, width), back),
            pl.BlockSpec((WIDE // 2, ROWS), flat),
            pl.BlockSpec((WIDE // 2, ROWS), flat),
            pl.BlockSpec((N, width), fixed),
        ],
        out_shape=[
            jax.ShapeDtypeStruct((seqs, length, width), bf16),
            jax.ShapeDtypeStruct((seqs, length, width), f32),
            jax.ShapeDtypeStruct((WIDE // 2, seqs * length), f32),
            jax.ShapeDtypeStruct((WIDE // 2, seqs * length), f32),
            jax.ShapeDtypeStruct((N, width), f32),
        ],
        scratch_shapes=[
            pltpu.VMEM((N, width), f32),
            pltpu.VMEM((N, width), f32),
            pltpu.VMEM((ROWS * N, width), bf16),
            pltpu.VMEM((ROWS * N, width), bf16),
            pltpu.VMEM((WIDE, ROWS), f32),
        ],
        compiler_params=params(60),
        cost_estimate=cost(28),
        name="scan_backward",
    )(me, xt, act, dt, ggi, chan, a_matrix, states, states, dtw)


def leave_kernel(
    gact_ref,
    gxt_ref,
    xt_ref,
    gsp_ref,
    wx_ref,
    pre_ref,
    conv_ref,
    act_ref,
    normed_ref,
    chan_ref,
    gskip_ref,
    *refs,
):
    galog_refs = refs[:-6]
    gci_ref, gin_ref, small_ref, padded, in_total, sums = refs[-6:]
    block = pl.program_id(1)
    rows = gact_ref.shape[1]
    start = (pl.program_id(0) == 0) & (block == 0)
    end = (pl.program_id(0) == pl.num_programs(0) - 1) & (block == pl.num_programs(1) - 1)

    @pl.when(start)
    def _():
        in_total[...] = jnp.zeros_like(in_total)
        small_ref[...] = jnp.zeros_like(small_ref)
        sums[...] = jnp.zeros_like(sums)

    @pl.when(block == 0)
    def _():
        padded[rows : rows + 8, :] = jnp.zeros((8, padded.shape[1]), f32)

    @pl.when(block > 0)
    def _():
        padded[rows : rows + 8, :] = padded[0:8, :]

    gxt = gxt_ref[...]
    act = act_ref[0]
    grad_act = gact_ref[0] + dot(gxt, wx_ref[:, 0:WIDE], 0, 1)
    pre = pre_ref[0]
    sig = jax.nn.sigmoid(pre)
    grad_conv = grad_act * (sig * (1.0 + pre * (1.0 - sig)))
    padded[0:rows, :] = grad_conv
    conv = conv_ref[0].astype(f32)
    gci = jnp.zeros_like(grad_conv)
    for k in range(KW):
        moved = padded[KW - 1 - k : KW - 1 - k + rows, :]
        gci = gci + chan_ref[k : k + 1, :] * moved
        sums[N + k : N + k + 1, :] += jnp.sum(conv * moved, axis=0, keepdims=True)
    sums[N + KW : N + KW + 1, :] += jnp.sum(grad_conv, axis=0, keepdims=True)
    gsp = gsp_ref[0]
    sums[N + KW + 1 : N + KW + 2, :] += jnp.sum(gsp.astype(f32), axis=0, keepdims=True)
    low = gci.astype(bf16)
    gci_ref[0] = low
    in_total[...] += dot(normed_ref[0], low, 0, 0)
    small_ref[:, 0:WIDE] += dot(act, gxt, 0, 1)
    small_ref[:, WIDE : WIDE + R] += dot(gsp, xt_ref[0:R, :], 0, 1)

    @pl.when(end)
    def _():
        gin_ref[...] = in_total[...].astype(bf16)
        sums[0:N, :] = sum(ref[...] for ref in galog_refs)
        sums[N + KW + 2 : N + KW + 3, :] = gskip_ref[...]
        small_ref[:, WIDE + R :] = sums[...].T


def leave(gact, gxt, xt, gsp, wx, pre, conv, act, normed, chan, gskip, galog):
    seqs, length, width = act.shape
    model = normed.shape[2]
    rows = min(BIG, length)
    blocks = length // rows

    def back(s, b):
        return (s, blocks - 1 - b, 0)

    def flat(s, b):
        return (0, s * blocks + blocks - 1 - b)

    def fixed(s, b):
        return (0, 0)

    return pl.pallas_call(
        leave_kernel,
        grid=(seqs, blocks),
        in_specs=[
            pl.BlockSpec((1, rows, width), back),
            pl.BlockSpec((WIDE, rows), flat),
            pl.BlockSpec((WIDE, rows), flat),
            pl.BlockSpec((1, rows, width), back),
            pl.BlockSpec((width, SMALL), fixed),
            pl.BlockSpec((1, rows, width), back),
            pl.BlockSpec((1, rows, width), back),
            pl.BlockSpec((1, rows, width), back),
            pl.BlockSpec((1, rows, model), back),
            pl.BlockSpec((8, width), fixed),
            pl.BlockSpec((1, width), fixed),
        ]
        + [pl.BlockSpec((N, width), fixed)] * len(galog),
        out_specs=[
            pl.BlockSpec((1, rows, width), back),
            pl.BlockSpec((model, width), fixed),
            pl.BlockSpec((width, GRADS), fixed),
        ],
        out_shape=[
            jax.ShapeDtypeStruct((seqs, length, width), bf16),
            jax.ShapeDtypeStruct((model, width), bf16),
            jax.ShapeDtypeStruct((width, GRADS), f32),
        ],
        scratch_shapes=[
            pltpu.VMEM((rows + 8, width), f32),
            pltpu.VMEM((model, width), f32),
            pltpu.VMEM((REST, width), f32),
        ],
        compiler_params=params(60),
        cost_estimate=cost(8),
        name="leave",
    )(gact, gxt, xt, gsp, wx, pre, conv, act, normed, chan, gskip, *galog)


def rows_back_kernel(me_ref, gci_ref, ggp_ref, w0_ref, w1_ref, *refs):
    part = refs[-1]
    part[...] = dot(gci_ref[0], w0_ref[...], 1, 1) + dot(ggp_ref[0], w1_ref[...], 1, 1)
    deal_pieces(refs[:-1], part, me_ref[0], pl.program_id(1))


def rows_back(me, gci, ggp, w0, w1, dps):
    seqs, length, width = gci.shape
    model = w0.shape[0]
    piece = length // dps
    rows = min(BIG, length)
    blocks = length // rows

    def at(s, b, me):
        return (s, b, 0)

    def fixed(s, b, me):
        return (0, 0)

    return pl.pallas_call(
        rows_back_kernel,
        grid_spec=pltpu.PrefetchScalarGridSpec(
            num_scalar_prefetch=1,
            grid=(seqs, blocks),
            in_specs=[
                pl.BlockSpec((1, rows, width), at),
                pl.BlockSpec((1, rows, width), at),
                pl.BlockSpec((model, width), fixed),
                pl.BlockSpec((model, width), fixed),
            ],
            out_specs=piece_specs(dps, piece, model),
            scratch_shapes=[pltpu.VMEM((rows, model), f32)],
        ),
        out_shape=piece_shapes(dps, seqs, piece, model, 2),
        compiler_params=params(60),
        cost_estimate=cost(5),
        name="rows_back",
    )(me, gci, ggp, w0, w1)


def finish_kernel(tok_ref, cot_ref, gain_ref, *refs):
    out_ref = refs[-1]
    grad = refs[0][0]
    for ref in refs[1:-1]:
        grad = grad + ref[0].astype(f32)
    x = tok_ref[0].astype(f32)
    inv = lax.rsqrt(jnp.mean(x * x, axis=-1, keepdims=True) + 1e-05)
    grad = grad * gain_ref[...]
    back = x * inv * inv * inv * jnp.mean(grad * x, axis=-1, keepdims=True)
    out_ref[0] = inv * grad - back + cot_ref[0].astype(f32)


def finish(tok, cot, gain, parts):
    seqs, piece, model = tok.shape
    rows = pl.BlockSpec((1, piece, model), lambda s: (s, 0, 0))
    return pl.pallas_call(
        finish_kernel,
        grid=(seqs,),
        in_specs=[rows, rows, pl.BlockSpec((1, model), lambda s: (0, 0))] + [rows] * len(parts),
        out_specs=rows,
        out_shape=jax.ShapeDtypeStruct(tok.shape, f32),
        compiler_params=params(60),
        cost_estimate=cost(3),
        name="finish",
    )(tok, cot, gain, *parts)


def collect_kernel(
    conv_ref, gate_ref, out_ref, small_ref, w_ref, gain_ref, gin_ref, gx_ref, gdt_ref, gchan_ref, galog_ref, ggain_ref, squares_ref, square
):
    own_in, columns = w_ref.shape
    width = conv_ref.shape[2]
    dps = columns // (2 * width)
    peers = conv_ref.shape[0] // dps
    own = small_ref.shape[0]
    total = jnp.zeros((1, 128), f32)

    def squares(x):
        x = jnp.sum(x * x, axis=0, keepdims=True)
        return jnp.sum(x, axis=1, keepdims=True)

    ggain = jnp.zeros((own_in, 1), f32)
    for half in range(2):
        for k in range(dps):
            parts = gate_ref if half else conv_ref
            grad = parts[k * peers].astype(f32)
            for j in range(1, peers):
                grad = grad + parts[k * peers + j].astype(f32)
            here = slice((half * dps + k) * width, (half * dps + k + 1) * width)
            gin_ref[:, here] = grad
            total = total + squares(grad)
            low = w_ref[:, here].astype(bf16).astype(f32)
            ggain = ggain + jnp.sum(grad * low, axis=1, keepdims=True)
    total = total + squares(out_ref[...])
    small = small_ref[...]
    total = total + squares(small)
    gx_ref[...] = small[:, :WIDE]
    square[...] = jnp.zeros_like(square)
    square[0:own, 0:GRADS] = small
    square[0:own_in, GRADS : GRADS + 1] = ggain
    turned = square[...].T
    gdt_ref[...] = turned[WIDE : WIDE + R, :own]
    galog_ref[...] = turned[WIDE + R : WIDE + R + N, :own]
    gchan_ref[...] = turned[WIDE + R + N : WIDE + R + N + KW + 3, :own]
    grad = turned[GRADS : GRADS + 1, :own_in] / gain_ref[...].astype(bf16).astype(f32)
    ggain_ref[...] = grad
    squares_ref[...] = jnp.broadcast_to((total + squares(grad))[None], squares_ref.shape)


def collect(conv, gate, out, small, w, gain):
    own_in, columns = w.shape
    own = small.shape[0]
    shapes = [
        (own_in, columns),
        (own, WIDE),
        (R, own),
        (KW + 3, own),
        (N, own),
        (1, own_in),
        (conv.shape[0], 1, 128),
    ]
    whole = pl.BlockSpec(memory_space=pltpu.VMEM)
    return pl.pallas_call(
        collect_kernel,
        in_specs=[whole] * 6,
        out_specs=[whole] * len(shapes),
        out_shape=[jax.ShapeDtypeStruct(shape, f32) for shape in shapes],
        scratch_shapes=[pltpu.VMEM((128, 256), f32)],
        compiler_params=params(16),
        cost_estimate=cost(3),
        name="collect",
    )(conv, gate, out, small, w, gain)


def adam_kernel(squares_ref, *refs):
    count = len(learn_rates)
    weights, moments, grads = refs[:count], refs[count : 2 * count], refs[2 * count : 3 * count]
    outs = refs[3 * count :]
    norm = jnp.sqrt(jnp.sum(squares_ref[...], axis=0)[:, 0:1])
    outs[2 * count][...] = norm
    factor = jnp.minimum(1.0, clip_limit / (norm + 1e-06))
    for place in range(count):
        rate = learn_rates[place]
        gradient = grads[place][...] * factor
        weight = weights[place][...]
        rows_first = len(moments[place].shape) == 3 and moments[place].shape[1] == 2
        at = (lambda k: (slice(None), k)) if rows_first else (lambda k: k)
        first = 0.9 * moments[place][at(0)] + 0.1 * gradient
        old = moments[place][at(1)]
        root = jnp.sqrt(0.95 * old * old + 0.05 * gradient * gradient)
        update = first / (1.0 - 0.9**STEP) / (root / (1.0 - 0.95**STEP) ** 0.5 + 1e-08)
        outs[2 * place][at(0)] = first
        outs[2 * place][at(1)] = root
        outs[2 * place + 1][...] = weight - rate * (update + 0.01 * weight)


def adam(squares, weights, moments, grads):
    shapes = []
    for weight, moment in zip(weights, moments):
        shapes.append(jax.ShapeDtypeStruct(moment.shape, f32))
        shapes.append(jax.ShapeDtypeStruct(weight.shape, f32))
    shapes.append(jax.ShapeDtypeStruct((1, 1), f32))
    whole = pl.BlockSpec(memory_space=pltpu.VMEM)
    return pl.pallas_call(
        adam_kernel,
        in_specs=[whole] * (1 + 3 * len(weights)),
        out_specs=[whole] * len(shapes),
        out_shape=shapes,
        compiler_params=params(16),
        cost_estimate=cost(4),
        name="adam",
    )(squares, *weights, *moments, *grads)


def shards(
    tokens,
    cotangent,
    in_weight,
    out_weight,
    xproj_weight,
    dtproj_weight,
    chan_params,
    a_log,
    norm_gain,
    in_moments,
    out_moments,
    xproj_moments,
    dtproj_moments,
    chan_moments,
    alog_moments,
    gain_moments,
):
    both = ("dp", "fsdp")
    dps = lax.axis_size("dp")
    fsdps = lax.axis_size("fsdp")
    depth = min(4, fsdps)
    near = fsdps // depth
    me = jnp.stack([lax.axis_index("dp"), lax.axis_index("fsdp")])
    batches, groups, piece, model = tokens.shape
    seqs = batches * groups
    length = piece * dps
    own_in = in_weight.shape[0]
    own = out_weight.shape[0]
    width = own * fsdps

    in_low = in_weight.astype(bf16).reshape(own_in, 2, dps, width).transpose(2, 1, 0, 3)
    gain_row = jnp.pad(norm_gain.astype(bf16)[None], ((0, 7), (0, width - own_in)))
    in_parts = jnp.concatenate(
        [in_low[:, 0], in_low[:, 1], jnp.broadcast_to(gain_row, (dps, 8, width))], axis=1
    )
    in_parts = lax.all_to_all(in_parts, "dp", 0, 0, tiled=True)
    small = jnp.concatenate(
        [
            xproj_weight.astype(bf16),
            jnp.zeros((own, AT_DT - WIDE), bf16),
            dtproj_weight.astype(bf16).T,
            a_log.astype(bf16).T,
            chan_params.astype(bf16).T,
            jnp.zeros((own, SMALL - AT_REST - N - KW - 3), bf16),
        ],
        axis=1,
    )
    fold = max(width // SMALL, 1)
    aligned = own_in % 16 == 0 and own % (16 * fold) == 0 and width % SMALL == 0
    if aligned:
        packed = jnp.concatenate(jnp.split(small, fold), axis=1)
    else:
        packed = small.reshape(-1, width)
    here = dps * own_in
    gain_rows = jnp.pad(in_parts[:, 2 * own_in], ((0, -dps % 16), (0, 0)))
    first = jnp.concatenate([in_parts[:, :own_in].reshape(here, width), gain_rows, packed])
    out_low = out_weight.astype(bf16).reshape(own, model // width, width).transpose(1, 0, 2)
    second = [
        in_parts[:, own_in : 2 * own_in].reshape(here, width),
        out_low.reshape(-1, width),
    ]
    second = jnp.concatenate(second)
    tok = parts_dp_far(tokens.reshape(seqs, piece, model))
    first_own = swap_near(first)
    first, tok, first_own = lax.optimization_barrier((gather_far(first), tok, first_own))
    cot = parts_dp_far(after(cotangent.reshape(seqs, piece, model), first))
    tok = parts_dp_near(tok)
    first_rest = swap_near(jnp.stack(first[1:]))
    first, first_rest, cot = lax.optimization_barrier((first, first_rest, cot))

    def own_columns(parts):
        parts = parts.reshape(fsdps, dps, own_in, width)
        return parts.transpose(1, 0, 2, 3).reshape(model, width)

    if aligned:
        w_conv, small, gain, a_matrix, chan = assemble(
            assemble_first_kernel,
            "assemble_first",
            me,
            first,
            first_own,
            first_rest,
            [
                ((model, width), bf16),
                ((width, SMALL), bf16),
                ((1, model), f32),
                ((N, width), f32),
                ((8, width), f32),
            ],
            [pltpu.VMEM((model // own_in, 128), f32)],
            60,
        )
    else:
        merged = merge_near(first, first_own, first_rest)
        w_conv = own_columns(merged[:, :here])
        gain = merged[:, here : here + dps, :own_in].transpose(1, 0, 2)
        gain = gain.reshape(1, model).astype(f32)
        small = merged[:, here + dps + -dps % 16 :].reshape(width, SMALL)
        rest = small[:, AT_REST : AT_REST + REST].astype(f32).T
        a_matrix = -jnp.exp(rest[:N])
        chan = rest[N : N + 8]

    far = gather_far(second)
    normed, conv, pre, act, *xt = enter(me, gain, w_conv, chan, small, tok)
    cot = parts_dp_near(cot)
    xt, far = lax.optimization_barrier((xt, far))
    xt = sum_dp_near(*xt)
    second_own = swap_near(after(far[0], xt))
    second_rest = swap_near(jnp.stack(after(far[1:], xt)))
    xt = sum_dp_far(xt, f32)
    if aligned:
        w_gate, w_out = assemble(
            assemble_second_kernel,
            "assemble_second",
            me,
            far,
            second_own,
            second_rest,
            [((model, width), bf16), ((width, model), bf16)],
            [],
            24,
        )
    else:
        merged = merge_near(far, second_own, second_rest)
        w_gate = own_columns(merged[:, :here])
        w_out = merged[:, here:].reshape(fsdps, model // width, own, width)
        w_out = w_out.transpose(0, 2, 1, 3).reshape(width, model)
    gate_in, states, dt = scan_forward(xt, act, small, chan, a_matrix)
    outs = middle(me, gate_in, act, normed, w_gate, w_out, cot, near, depth)
    part, gout = outs[:dps], outs[dps : dps + near]
    ggi, ggp, gin_gate, gskip = outs[dps + near :]
    gate_parts = lax.all_to_all(gin_gate.reshape(-1, own_in, width), both, 0, 0, tiled=True)
    gout_near = reduce_near(gout)
    out_mine, out_parts = send_dp_near(part)

    gsp, gact, *gxt, galog = scan_backward(
        me, xt, act, dt, ggi, chan, a_matrix, states, small
    )
    gxt, out_mine, gout_near = lax.optimization_barrier((gxt, out_mine, gout_near))
    gxt = sum_dp_near(*gxt)
    gout_far = send_far(list(after(gout_near, gxt)))
    out_rows = send_dp_far(list(out_mine), list(after(out_parts, gxt)))
    gxt = sum_dp_far(gxt, bf16)
    gxt, gate_parts = lax.optimization_barrier((gxt, gate_parts))
    gci, gin_conv, small_grad = leave(
        gact, gxt, xt, gsp, small, pre, conv, act, normed, chan, gskip, [galog]
    )
    gin_conv, gout_far = lax.optimization_barrier((gin_conv, gout_far))
    conv_parts = lax.all_to_all(gin_conv.reshape(-1, own_in, width), both, 0, 0, tiled=True)
    grad_out = sum(part.astype(f32) for part in gout_far)
    small_near = reduce_near(split_near(small_grad.reshape(fsdps, own, GRADS)))
    part_back = rows_back(me, gci, ggp, w_conv, w_gate, dps)
    back_mine, back_parts = send_dp_near(part_back)
    small_near, back_parts = lax.optimization_barrier((small_near, back_parts))
    own_small = sum(part.astype(f32) for part in send_far(list(small_near)))
    part_back = send_dp_far(back_mine, list(back_parts))
    out_rows = sum(part.astype(f32) for part in out_rows).reshape(tokens.shape)
    block_output = (tokens.astype(f32) + out_rows).astype(bf16)

    def flat2(x):
        return x.reshape(x.shape[:-1] + (1, x.shape[-1]))

    grad_in, grad_x, grad_dt, grad_chan, grad_alog, grad_gain, squares = collect(
        conv_parts, gate_parts, grad_out, own_small, in_weight, flat2(norm_gain)
    )
    grad_normed = sum(part.astype(f32) for part in after(part_back, squares)).reshape(tokens.shape)

    input_grad = finish(
        tokens.reshape(seqs, piece, model),
        cotangent.reshape(seqs, piece, model),
        gain,
        after(part_back, squares),
    ).reshape(tokens.shape)
    squares = lax.all_to_all(squares, both, 0, 0, tiled=True)
    weights = (in_weight, out_weight, xproj_weight, dtproj_weight, chan_params, a_log, flat2(norm_gain))
    moments = (
        in_moments,
        out_moments,
        xproj_moments,
        dtproj_moments,
        chan_moments.transpose(1, 0, 2),
        alog_moments,
        flat2(gain_moments),
    )
    grads = (grad_in, grad_out, grad_x, grad_dt, grad_chan, grad_alog, grad_gain)
    updated = list(adam(squares, weights, moments, grads))
    grad_norm = updated.pop().reshape(())
    updated[8] = updated[8].transpose(1, 0, 2)
    updated[-2] = updated[-2].reshape(gain_moments.shape)
    updated[-1] = updated[-1].reshape(norm_gain.shape)
    return (block_output, input_grad, grad_norm) + tuple(updated)


def solution(mesh):
    both = ("dp", "fsdp")
    row_specs = (P(None, "fsdp", "dp", None),) * 2
    weight_specs = (
        P(both, None),
        P(both, None),
        P(both, None),
        P(None, both),
        P(None, both),
        P(None, both),
        P(both),
    )
    moment_specs = (
        P(None, both, None),
        P(None, both, None),
        P(None, both, None),
        P(None, None, both),
        P(None, None, both),
        P(None, None, both),
        P(None, both),
    )
    updated = tuple(spec for pair in zip(moment_specs, weight_specs) for spec in pair)
    return jax.shard_map(
        shards,
        mesh=mesh,
        in_specs=row_specs + weight_specs + moment_specs,
        out_specs=row_specs + (P(),) + updated,
        check_vma=False,
    )
```
